128 devices in a mesh: rep: 4 (over x_hi, core), grid: 32 (over x_lo, z, y).
Axes of the slice: x: 4 (x_hi: 2, x_lo: 2; x = x_hi * 2 + x_lo), y: 4, z: 4, core: 2. Of those that a mesh axis runs over, the one named last changes fastest.
Arguments:
- panel_left: float32 [2048, 16384], P('grid', 'rep'), may hold values from -6 to 6
- panel_right: float32 [16384, 8192], P('rep', 'grid'), may hold values from -0.046875 to 0.046875
Outputs:
- product: float32 [2048, 8192], P('rep', 'grid')
The draws below stay inside these ranges and needn't reach their ends.
All inputs are finite; a program needn't handle non-finite values.
Results may differ from the reference program's by a relative error of at most 0.0001.
Values sent between devices are 32-bit elements; how exact they have to be, the bound alone decides.
No kernel may reach another device: no remote copies, remote signals or barrier semaphores. Data moves between devices by JAX's collectives and lax.ppermute only.
A program may use at most 128 MiB of HBM per device.

```python
import jax
import jax.numpy as jnp
from jax import lax

K = 16384
N = 8192
M = 2048
N_REP = 4


def level_of(stream_key, dims, pieces, low, high):
    loudness, own = 1.0, jax.random.fold_in(stream_key, 6)
    for axis_at, parts in pieces:
        steps = jnp.exp(jax.random.uniform(jax.random.fold_in(own, axis_at), (parts,), jnp.float32, low / len(pieces), high / len(pieces)))
        loudness = loudness * jnp.repeat(steps, dims[axis_at] // parts).reshape([-1 if axis == axis_at else 1 for axis in range(len(dims))])
    return loudness


def bell_draw(key, shape, deviation, bound, split=(), kind=jnp.bfloat16):
    entries = jax.random.normal(key, shape, jnp.float32) * deviation
    if len(split) > 0:
        entries = level_of(key, shape, split, -0.22, 0.18) * entries
    return jnp.clip(entries, min=-bound, max=bound).astype(kind)


def setup_inputs(seed: int = 0) -> dict:
    streams_of = jax.random.split(jax.random.key(seed), 3)
    return {
        "panel_left": bell_draw(streams_of[0], (M, K), 1.0, 6.0, ((0, 32), (1, 4)), jnp.float32),
        "panel_right": bell_draw(streams_of[1], (K, N), K ** -0.5, 0.046875, ((0, 4), (1, 32)), jnp.float32),
    }


def reference(panel_left, panel_right):
    width = K // N_REP
    total = jnp.zeros((panel_left.shape[0], panel_right.shape[1]), jnp.float32)
    for block in range(N_REP):
        left_part = panel_left[:, block * width:(block + 1) * width]
        right_part = panel_right[block * width:(block + 1) * width, :]
        total = total + jnp.dot(left_part, right_part, precision=lax.Precision.HIGHEST, preferred_element_type=jnp.float32)
    return total
```

```python
import jax
import jax.numpy as jnp
from jax import lax
from jax.sharding import PartitionSpec as P

AXES = ("rep", "grid")


def moved(dx=0, dz=0, dy=0, dhi=0, core=0, chosen=lambda rep, grid: True):
    pairs = []
    for rep in range(4):
        for grid in range(32):
            if chosen(rep, grid):
                pairs.append((rep * 32 + grid, (rep ^ (2 * dhi) ^ core) * 32 + (grid ^ (16 * dx) ^ (4 * dz) ^ dy)))
    return pairs


def owns(side):
    return lambda rep, grid: ((rep & 1) ^ ((grid >> 3) & 1)) == side


def send(value, **where):
    return lax.ppermute(value, AXES, moved(**where))


NEAR = (dict(), dict(dy=1), dict(dy=3), dict(dx=1))


def flip_if(bit, value, axis):
    return jnp.where(bit == 1, jnp.flip(value, axis), value)


def reordered(value, dx=0, dy=0):
    split = value.reshape(2, 2, 2, -1, value.shape[1])
    axes = [axis for axis, bit in enumerate((dx, dy >> 1, dy & 1)) if bit]
    return jnp.flip(split, axes).reshape(value.shape) if axes else value


def per_device(left, right):
    rows, depth = left.shape
    columns = right.shape[1]
    part = depth // 4
    rep, grid = lax.axis_index("rep"), lax.axis_index("grid")
    core, x_hi = rep & 1, rep >> 1
    x_lo, z, y = grid >> 4, (grid >> 2) & 3, grid & 3
    quarter = 2 * (x_lo ^ (y >> 1)) + (x_lo ^ (y >> 1) ^ (y & 1))

    left_of = [lax.dynamic_slice_in_dim(left, (quarter ^ d) * part, part, 1) for d in range(4)]
    right_of = [lax.dynamic_slice_in_dim(right, (quarter ^ d) * part, part, 0) for d in range(4)]

    blocks = {(0, 0): left_of[0]}
    for dx, dy in ((0, 1), (0, 3), (1, 0), (1, 1), (1, 3), (0, 2), (1, 2)):
        flips = (dy & 1) ^ (dy >> 1), dy >> 1
        d = (3 * dx) ^ (2 * flips[1] + flips[0])
        blocks[dx, dy] = send(left_of[d], dx=dx, dy=dy)
    groups = [
        [(0, 0)],
        [(0, 1), (0, 3), (1, 0)],
        [(1, 1), (1, 3), (0, 2), (1, 2)],
    ]
    panel = jnp.concatenate([right_of[0]] + [send(right_of[d], **NEAR[d]) for d in range(1, 4)], axis=1)

    by_dz = {dz: {} for dz in range(4)}
    for group in groups:
        own = jnp.concatenate([blocks[name] for name in group], axis=0) if len(group) > 1 else blocks[group[0]]
        half = own.shape[0] // 2
        one, three = send(own, dz=1), send(own, dz=3)
        two = jnp.concatenate([send(one[:half], dz=3), send(three[half:], dz=1)], axis=0)
        for dz, value in enumerate((own, one, two, three)):
            for at, name in enumerate(group):
                by_dz[dz][name] = value[at * rows:(at + 1) * rows]

    finals = {}
    order = [(dx, dy) for dx in range(2) for dy in range(4)]
    for dz in (0, 1, 3, 2):
        side = dz >> 1
        stack = jnp.concatenate([by_dz[dz][name] for name in order], axis=0)
        partial = jnp.dot(stack, panel, precision=lax.Precision.HIGH, preferred_element_type=jnp.float32)
        partial = partial.reshape(stack.shape[0], 4, columns).transpose(1, 0, 2)
        other = send(partial, core=1, chosen=owns(1 - side))
        both = [reordered(partial[d] + other[d], **NEAR[d]) for d in range(4)]
        total = both[0]
        for d in range(1, 4):
            total = total + send(both[d], chosen=owns(side), **NEAR[d])
        total = total.reshape(2, stack.shape[0] // 2, columns)
        keep = x_hi ^ x_lo
        mine = lax.dynamic_index_in_dim(total, keep, 0, False)
        theirs = lax.dynamic_index_in_dim(total, 1 - keep, 0, False)
        finals[dz] = mine + send(theirs, dhi=1, chosen=owns(side))

    early = core == (z >> 1)
    first = jnp.where(early, finals[0], finals[2])
    second = jnp.where(early, finals[1], finals[3])
    out = jnp.stack([first, second]).reshape(2, 2, 2, rows, columns)
    out = flip_if(z & 1, out, 0)
    out = flip_if(y >> 1, out, 1)
    out = flip_if(y & 1, out, 2)
    return out.reshape(8 * rows, columns)


def solution(mesh):
    return jax.shard_map(
        per_device,
        mesh=mesh,
        in_specs=(P("grid", "rep"), P("rep", "grid")),
        out_specs=P("rep", "grid"),
        check_vma=False,
    )
```

```python
import functools

import jax
import jax.numpy as jnp
from jax import lax
from jax.experimental import pallas as pl
from jax.experimental.pallas import tpu as pltpu
from jax.sharding import PartitionSpec as P

AXES = ("rep", "grid")
VMEM_LIMIT = 48 * 1024 * 1024


def number(x_hi, core, x_lo, z, y):
    return (2 * x_hi + core) * 32 + 16 * x_lo + 4 * z + y


def every(pick):
    return [
        pick(x_hi, core, x_lo, z, y)
        for x_hi in range(2) for core in range(2) for x_lo in range(2) for z in range(4) for y in range(4)
    ]


def moved(dx=0, dz=0, dy=0, core=0):
    return every(lambda h, c, x, z, y: (number(h, c, x, z, y), number(h, c ^ core, x ^ dx, z ^ dz, y ^ dy)))


def send(value, **where):
    return lax.ppermute(value, AXES, moved(**where))


PLANES = [
    [number(h, c, x, z, y) for z in range(4) for y in range(4)]
    for h in range(2) for c in range(2) for x in range(2)
]
LINES = [
    [number(h, c, x, z, y) for h in range(2) for c in range(2) for x in range(2)]
    for z in range(4) for y in range(4)
]


def halves(value):
    high = value.astype(jnp.bfloat16)
    return high, (value - high.astype(jnp.float32)).astype(jnp.bfloat16)


def split_kernel(own_0, own_1, far_0, far_1, high, low):
    for piece, refs in enumerate(((own_0, far_0), (own_1, far_1))):
        for group, ref in enumerate(refs):
            columns = ref.shape[1]
            at = slice(group * columns, (group + 1) * columns)
            high[piece, :, at], low[piece, :, at] = halves(ref[...])


def split_right(own_0, own_1, far_0, far_1, steps=8):
    depth, columns = own_0.shape
    shape = jax.ShapeDtypeStruct((2, depth, 2 * columns), jnp.bfloat16)
    out = pl.BlockSpec((2, depth // steps, 2 * columns), lambda i: (0, i, 0))
    return pl.pallas_call(
        split_kernel,
        grid=(steps,),
        in_specs=[pl.BlockSpec((depth // steps, columns), lambda i: (i, 0))] * 4,
        out_specs=[out, out],
        out_shape=[shape, shape],
        compiler_params=pltpu.CompilerParams(vmem_limit_bytes=VMEM_LIMIT),
        cost_estimate=pl.CostEstimate(flops=0, bytes_accessed=depth * columns * 32, transcendentals=0),
    )(own_0, own_1, far_0, far_1)


def multiply_kernel(place, left, high, low, *rest):
    out = rest[-1]
    own = place[1]
    total = None
    for piece in range(2):
        block = left[:, piece]
        left_high, left_low = halves(block.reshape(block.shape[0] * block.shape[1], block.shape[2]))
        for one, two in ((left_high, high), (left_high, low), (left_low, high)):
            term = jnp.dot(one, two[piece], preferred_element_type=jnp.float32)
            total = term if total is None else total + term
    columns = total.shape[1] // 2
    out[0, 0, own] = total[:, :columns]
    out[0, 0, 1 - own] = total[:, columns:]


def multiply(place, left, high, low, earlier=None):
    positions, _, rows, depth = left.shape
    columns = high.shape[2] // 2
    group = positions // 2
    whole = pl.BlockSpec(high.shape, lambda i, place: (0, 0, 0), pipeline_mode=pl.Buffered(1))
    chained = () if earlier is None else (earlier,)
    return pl.pallas_call(
        multiply_kernel,
        grid_spec=pltpu.PrefetchScalarGridSpec(
            num_scalar_prefetch=1,
            grid=(2,),
            in_specs=[
                pl.BlockSpec((group, 2, rows, depth), lambda i, place: (i, 0, 0, 0)),
                whole,
                whole,
            ] + [pl.BlockSpec(memory_space=pl.ANY)] * len(chained),
            out_specs=pl.BlockSpec(
                (1, 1, 2, group * rows, columns), lambda i, place: (place[0], i, 0, 0, 0)
            ),
        ),
        out_shape=jax.ShapeDtypeStruct((2, 2, 2, group * rows, columns), jnp.float32),
        input_output_aliases={4: 0} if chained else {},
        compiler_params=pltpu.CompilerParams(vmem_limit_bytes=VMEM_LIMIT),
        cost_estimate=pl.CostEstimate(
            flops=12 * positions * rows * depth * 2 * columns, bytes_accessed=32 << 20, transcendentals=0
        ),
    )(place, left, high, low, *chained)


def per_device(left, right):
    rows, depth = left.shape[0] // 2, left.shape[1] // 2
    columns = right.shape[1]
    rep, grid = lax.axis_index("rep"), lax.axis_index("grid")
    core, x_lo = rep & 1, grid >> 4

    def left_part(value, at, half):
        return lax.dynamic_slice(value, (at * rows, half * depth), (rows, depth))

    swapped = send(lax.dynamic_slice(left, ((1 - core) * rows, 0), (rows, 2 * depth)), core=1)
    mine = jnp.stack([left_part(left, core, x_lo), left_part(swapped, 0, x_lo)])
    theirs = jnp.stack([left_part(left, core, 1 - x_lo), left_part(swapped, 0, 1 - x_lo)])

    near = lax.all_gather(mine, AXES, axis=0, axis_index_groups=PLANES)
    far = lax.all_gather(send(theirs, dx=1), AXES, axis=0, axis_index_groups=PLANES)

    own = lax.dynamic_slice(right, (x_lo * depth, 0), (depth, columns))
    other = send(lax.dynamic_slice(right, ((1 - x_lo) * depth, 0), (depth, columns)), dx=1)
    high, low = split_right(own, send(own, core=1), other, send(other, core=1))

    parts = multiply(jnp.stack([x_lo, x_lo]), near, high, low)
    parts = multiply(jnp.stack([1 - x_lo, x_lo]), far, high, low, parts)

    parts = lax.all_to_all(
        parts.reshape(-1, columns), AXES, 0, 0, tiled=True, axis_index_groups=LINES
    )
    parts = parts.reshape(2, 2, 2, 8, rows, columns)
    total = (parts[0, :, 0] + parts[0, :, 1]) + (parts[1, :, 0] + parts[1, :, 1])
    return total.transpose(1, 0, 2, 3).reshape(16 * rows, columns)


def solution(mesh):
    return jax.shard_map(
        per_device,
        mesh=mesh,
        in_specs=(P("grid", "rep"), P("rep", "grid")),
        out_specs=P("rep", "grid"),
        check_vma=False,
    )
```

```python
import jax
import jax.numpy as jnp
from jax import lax
from jax.experimental import pallas as pl
from jax.experimental.pallas import tpu as pltpu
from jax.sharding import PartitionSpec as P

AXES = ("rep", "grid")
VMEM_LIMIT = 40 * 1024 * 1024
PARAMS = pltpu.CompilerParams(vmem_limit_bytes=VMEM_LIMIT)


def number(x_hi, core, x_lo, z, y):
    return (2 * x_hi + core) * 32 + 16 * x_lo + 4 * z + y


def pairs(target):
    found = []
    for x_hi in range(2):
        for core in range(2):
            for x_lo in range(2):
                for z in range(4):
                    for y in range(4):
                        there = target(x_hi, core, x_lo, z, y)
                        if there is not None:
                            found.append((number(x_hi, core, x_lo, z, y), number(*there)))
    return found


def send(value, dx=0, dz=0, dy=0, core=0):
    return lax.ppermute(
        value, AXES, pairs(lambda h, c, x, z, y: (h, c ^ core, x ^ dx, z ^ dz, y ^ dy))
    )


def send_if(value, same, other):
    def target(h, c, x, z, y):
        flips = same if h == x else other
        return None if flips is None else (h ^ flips[0], c, x ^ flips[1], z, y)

    return lax.ppermute(value, AXES, pairs(target))


PLANES = [
    [number(h, c, x, z, y) for z in range(4) for y in range(4)]
    for h in range(2) for c in range(2) for x in range(2)
]
POSITIONS = [(dz, dy) for dz in range(4) for dy in range(4)]
EARLY = [(dz, dy) for dz, dy in POSITIONS if dz != 2 and dy != 2]
LATE = [(dz, dy) for dz, dy in POSITIONS if dz == 2 or dy == 2]


def halves(value):
    high = value.astype(jnp.bfloat16)
    return high, (value - high.astype(jnp.float32)).astype(jnp.bfloat16)


def split_kernel(first, second, high, low):
    for piece, ref in enumerate((first, second)):
        high[piece], low[piece] = halves(ref[...])


def split_right(first, second, steps=4):
    depth, columns = first.shape
    shape = jax.ShapeDtypeStruct((2, depth, columns), jnp.bfloat16)
    out = pl.BlockSpec((2, depth // steps, columns), lambda i: (0, i, 0))
    return pl.pallas_call(
        split_kernel,
        grid=(steps,),
        in_specs=[pl.BlockSpec((depth // steps, columns), lambda i: (i, 0))] * 2,
        out_specs=[out, out],
        out_shape=[shape, shape],
        compiler_params=PARAMS,
        cost_estimate=pl.CostEstimate(flops=0, bytes_accessed=depth * columns * 16, transcendentals=0),
    )(first, second)


def products(lefts, rights):
    found = []
    for high, low in rights:
        total = None
        for piece, (left_high, left_low) in enumerate(lefts):
            for one, two in ((left_high, high), (left_high, low), (left_low, high)):
                term = jnp.dot(one, two[piece], preferred_element_type=jnp.float32)
                total = term if total is None else total + term
        found.append(total)
    return found


def near_kernel(same, left, own_high, own_low, far_high, far_low, first, second):
    lefts = []
    for piece in range(2):
        block = left[:, piece]
        lefts.append(halves(block.reshape(block.shape[0] * block.shape[1], block.shape[2])))
    own, far = products(lefts, ((own_high, own_low), (far_high, far_low)))
    swap = same[0] == 1
    first[...] = jnp.where(swap, far, own).reshape(first.shape)
    second[...] = jnp.where(swap, own, far).reshape(second.shape)


def whole(value):
    return pl.BlockSpec(value.shape, lambda *_: (0,) * value.ndim, pipeline_mode=pl.Buffered(1))


def near_products(same, left, rights):
    positions, _, rows, depth = left.shape
    columns = rights[0].shape[2]
    group = positions // 2
    shape = jax.ShapeDtypeStruct((positions, rows, columns), jnp.float32)
    out = pl.BlockSpec((group, rows, columns), lambda i, same: (i, 0, 0))
    return pl.pallas_call(
        near_kernel,
        grid_spec=pltpu.PrefetchScalarGridSpec(
            num_scalar_prefetch=1,
            grid=(2,),
            in_specs=[pl.BlockSpec((group, 2, rows, depth), lambda i, same: (i, 0, 0, 0))]
            + [whole(right) for right in rights],
            out_specs=[out, out],
        ),
        out_shape=[shape, shape],
        compiler_params=PARAMS,
        cost_estimate=pl.CostEstimate(
            flops=24 * positions * rows * depth * columns, bytes_accessed=20 << 20, transcendentals=0
        ),
    )(same, left, *rights)


def far_products(same, sources, rights):
    positions = len(sources[0])
    columns = rights[0].shape[2]
    rows, depth = sources[0][0][0].shape[1:]
    arrays, uses = [], {}
    for piece in sources:
        for array, at in piece:
            if id(array) not in uses:
                uses[id(array)] = (len(arrays), set())
                arrays.append(array)
            uses[id(array)][1].add(at)
    specs, places = [], {}
    for array in arrays:
        slot, used = uses[id(array)]
        if len(used) == 1:
            (only,) = used
            specs.append(pl.BlockSpec((1, rows, depth), lambda i, same, only=only: (only, 0, 0)))
            places[slot, only] = 0
        else:
            specs.append(whole(array))
            places.update({(slot, at): at for at in used})
    plan = [[(uses[id(array)][0], places[uses[id(array)][0], at]) for array, at in piece] for piece in sources]

    def kernel(same, *refs):
        blocks, rest = refs[: len(arrays)], refs[len(arrays):]
        own_high, own_low, far_high, far_low, first, second, high, low = rest
        for piece in range(2):
            for place, (slot, at) in enumerate(plan[piece]):
                span = slice(place * rows, (place + 1) * rows)
                high[piece, span], low[piece, span] = halves(blocks[slot][at])
        lefts = [(high[piece], low[piece]) for piece in range(2)]
        own, far = products(lefts, ((own_high, own_low), (far_high, far_low)))
        swap = same[0] == 1
        first[...] = jnp.where(swap, own, far).reshape(first.shape)
        second[...] = jnp.where(swap, far, own).reshape(second.shape)

    shape = jax.ShapeDtypeStruct((positions, rows, columns), jnp.float32)
    scratch = pltpu.VMEM((2, positions * rows, depth), jnp.bfloat16)
    return pl.pallas_call(
        kernel,
        grid_spec=pltpu.PrefetchScalarGridSpec(
            num_scalar_prefetch=1,
            grid=(1,),
            in_specs=specs + [whole(right) for right in rights],
            out_specs=[pl.BlockSpec(shape.shape, lambda i, same: (0, 0, 0))] * 2,
            scratch_shapes=[scratch, scratch],
        ),
        out_shape=[shape, shape],
        compiler_params=PARAMS,
        cost_estimate=pl.CostEstimate(
            flops=24 * positions * rows * depth * columns, bytes_accessed=12 << 20, transcendentals=0
        ),
    )(same, *arrays, *rights)


def total_kernel(place, near_a, near_b, near_own, early_a, early_b, early_own, late_a, late_b, late_own, keep, give):
    same, core, z, y = place[0] == 1, place[1], place[2], place[3]
    groups = ((EARLY, early_a, early_b, early_own), (LATE, late_a, late_b, late_own))
    for positions, one, two, own in groups:
        for place_in, (dz, dy) in enumerate(positions):
            plane, line = z ^ dz, y ^ dy
            at = plane * 4 + line
            mine = jnp.where(same, near_own[at], own[place_in])
            value = near_a[at] + near_b[at] + one[place_in] + two[place_in] + mine
            into = (plane & 1) * 4 + line

            @pl.when((plane >> 1) == core)
            def _():
                keep[into] = value

            @pl.when((plane >> 1) != core)
            def _():
                give[into] = value


def total_of(place, near, early, late):
    _, rows, columns = near[0].shape
    shape = jax.ShapeDtypeStruct((8, rows, columns), jnp.float32)
    values = [*near, *early, *late]
    return pl.pallas_call(
        total_kernel,
        grid_spec=pltpu.PrefetchScalarGridSpec(
            num_scalar_prefetch=1,
            grid=(1,),
            in_specs=[whole(value) for value in values],
            out_specs=[pl.BlockSpec(shape.shape, lambda i, place: (0, 0, 0))] * 2,
        ),
        out_shape=[shape, shape],
        compiler_params=PARAMS,
        cost_estimate=pl.CostEstimate(flops=1 << 20, bytes_accessed=4 << 20, transcendentals=0),
    )(place, *values)


def join_kernel(core, kept, given, out):
    rows = kept.shape[1]
    mine = core[0]
    out[:, pl.ds(pl.multiple_of(mine * rows, rows), rows)] = kept[...]
    out[:, pl.ds(pl.multiple_of((1 - mine) * rows, rows), rows)] = given[...]


def join(core, kept, given):
    blocks, rows, columns = kept.shape
    shape = jax.ShapeDtypeStruct((blocks, 2 * rows, columns), jnp.float32)
    return pl.pallas_call(
        join_kernel,
        grid_spec=pltpu.PrefetchScalarGridSpec(
            num_scalar_prefetch=1,
            grid=(1,),
            in_specs=[whole(kept), whole(given)],
            out_specs=pl.BlockSpec(shape.shape, lambda i, core: (0, 0, 0)),
        ),
        out_shape=shape,
        compiler_params=PARAMS,
        cost_estimate=pl.CostEstimate(flops=0, bytes_accessed=1 << 20, transcendentals=0),
    )(core, kept, given)


def gathered(block, small, big):
    ring = [block] + [send(block, **{small: step}) for step in (1, 2, 3)]
    line = jnp.stack(ring)
    one, three = send(line, **{big: 1}), send(line, **{big: 3})
    two = send(one[:2], **{big: 3}), send(three[2:], **{big: 1})

    def source(far, near):
        if far == 2:
            return two[near >> 1], near & 1
        return {0: line, 1: one, 3: three}[far], near

    return source


def per_device(left, right):
    rows, depth = left.shape[0] // 2, left.shape[1] // 2
    columns = right.shape[1]
    rep, grid = lax.axis_index("rep"), lax.axis_index("grid")
    core, x_hi = rep & 1, rep >> 1
    x_lo, z, y = grid >> 4, (grid >> 2) & 3, grid & 3
    same = (x_hi == x_lo).astype(jnp.int32)

    def left_part(value, at, half):
        return lax.dynamic_slice(value, (at * rows, half * depth), (rows, depth))

    swapped = send(lax.dynamic_slice(left, ((1 - core) * rows, 0), (rows, 2 * depth)), core=1)
    mine = jnp.stack([left_part(left, core, x_lo), left_part(swapped, 0, x_lo)])
    near = lax.all_gather(mine, AXES, axis=0, axis_index_groups=PLANES)

    by_y = gathered(send(left_part(left, core, 1 - x_lo), dx=1), "dy", "dz")
    by_z = gathered(send(left_part(swapped, 0, 1 - x_lo), dx=1), "dz", "dy")

    own = lax.dynamic_slice(right, (x_lo * depth, 0), (depth, columns))
    other = send(lax.dynamic_slice(right, ((1 - x_lo) * depth, 0), (depth, columns)), dx=1)
    rights = (*split_right(own, send(own, core=1)), *split_right(other, send(other, core=1)))

    flag = same.reshape(1)
    first, second = near_products(flag, near, rights)
    near_sums = send_if(first, (0, 1), (1, 0)), send_if(second, None, (1, 1)), second

    far_sums = []
    for positions in (EARLY, LATE):
        sources = (
            [by_y(dz, dy) for dz, dy in positions],
            [by_z(dy, dz) for dz, dy in positions],
        )
        first, second = far_products(flag, sources, rights)
        far_sums.append((send_if(first, (1, 0), (0, 1)), send_if(second, (1, 1), None), second))

    keep, give = total_of(jnp.stack([same, core, z, y]), near_sums, *far_sums)
    return join(core.reshape(1), keep, send(give, core=1)).reshape(16 * rows, columns)


def solution(mesh):
    return jax.shard_map(
        per_device,
        mesh=mesh,
        in_specs=(P("grid", "rep"), P("rep", "grid")),
        out_specs=P("rep", "grid"),
        check_vma=False,
    )
```

```python
import jax
import jax.numpy as jnp
from jax import lax
from jax.experimental import pallas as pl
from jax.experimental.pallas import tpu as pltpu
from jax.sharding import PartitionSpec as P

AXES = ("rep", "grid")
VMEM_LIMIT = 40 * 1024 * 1024
PARAMS = pltpu.CompilerParams(vmem_limit_bytes=VMEM_LIMIT)


def number(x_hi, core, x_lo, z, y):
    return (2 * x_hi + core) * 32 + 16 * x_lo + 4 * z + y


def pairs(target):
    found = []
    for x_hi in range(2):
        for core in range(2):
            for x_lo in range(2):
                for z in range(4):
                    for y in range(4):
                        there = target(x_hi, core, x_lo, z, y)
                        if there is not None:
                            found.append((number(x_hi, core, x_lo, z, y), number(*there)))
    return found


def send(value, dx=0, dz=0, dy=0, core=0):
    return lax.ppermute(
        value, AXES, pairs(lambda h, c, x, z, y: (h, c ^ core, x ^ dx, z ^ dz, y ^ dy))
    )


def send_if(value, same, other):
    def target(h, c, x, z, y):
        flips = same if h == x else other
        return None if flips is None else (h ^ flips[0], c, x ^ flips[1], z, y)

    return lax.ppermute(value, AXES, pairs(target))


PLANES = [
    [number(h, c, x, z, y) for z in range(4) for y in range(4)]
    for h in range(2) for c in range(2) for x in range(2)
]
POSITIONS = [(dz, dy) for dz in range(4) for dy in range(4)]
EARLY = [(dz, dy) for dz, dy in POSITIONS if dz != 2 and dy != 2]
LATE = [(dz, dy) for dz, dy in POSITIONS if dz == 2 or dy == 2]


def halves(value):
    high = value.astype(jnp.bfloat16)
    return high, (value - high.astype(jnp.float32)).astype(jnp.bfloat16)


def split_kernel(first, second, high, low):
    for piece, ref in enumerate((first, second)):
        high[piece], low[piece] = halves(ref[...])


def split_right(first, second, steps=4):
    depth, columns = first.shape
    shape = jax.ShapeDtypeStruct((2, depth, columns), jnp.bfloat16)
    out = pl.BlockSpec((2, depth // steps, columns), lambda i: (0, i, 0))
    return pl.pallas_call(
        split_kernel,
        grid=(steps,),
        in_specs=[pl.BlockSpec((depth // steps, columns), lambda i: (i, 0))] * 2,
        out_specs=[out, out],
        out_shape=[shape, shape],
        compiler_params=PARAMS,
        cost_estimate=pl.CostEstimate(flops=0, bytes_accessed=depth * columns * 16, transcendentals=0),
    )(first, second)


def products(lefts, rights):
    found = []
    for high, low in rights:
        total = None
        for piece, (left_high, left_low) in enumerate(lefts):
            for one, two in ((left_high, high), (left_high, low), (left_low, high)):
                term = jnp.dot(one, two[piece], preferred_element_type=jnp.float32)
                total = term if total is None else total + term
        found.append(total)
    return found


def near_kernel(same, left, own_high, own_low, far_high, far_low, first, second):
    lefts = []
    for piece in range(2):
        block = left[:, piece]
        lefts.append(halves(block.reshape(block.shape[0] * block.shape[1], block.shape[2])))
    own, far = products(lefts, ((own_high, own_low), (far_high, far_low)))
    swap = same[0] == 1
    first[...] = jnp.where(swap, far, own).reshape(first.shape)
    second[...] = jnp.where(swap, own, far).reshape(second.shape)


def whole(value):
    return pl.BlockSpec(value.shape, lambda *_: (0,) * value.ndim, pipeline_mode=pl.Buffered(1))


def near_products(same, left, rights):
    positions, _, rows, depth = left.shape
    columns = rights[0].shape[2]
    group = positions // 2
    shape = jax.ShapeDtypeStruct((positions, rows, columns), jnp.float32)
    out = pl.BlockSpec((group, rows, columns), lambda i, same: (i, 0, 0))
    return pl.pallas_call(
        near_kernel,
        grid_spec=pltpu.PrefetchScalarGridSpec(
            num_scalar_prefetch=1,
            grid=(2,),
            in_specs=[pl.BlockSpec((group, 2, rows, depth), lambda i, same: (i, 0, 0, 0))]
            + [whole(right) for right in rights],
            out_specs=[out, out],
        ),
        out_shape=[shape, shape],
        compiler_params=PARAMS,
        cost_estimate=pl.CostEstimate(
            flops=24 * positions * rows * depth * columns, bytes_accessed=20 << 20, transcendentals=0
        ),
    )(same, left, *rights)


def far_products(same, sources, rights):
    positions = len(sources[0])
    columns = rights[0].shape[2]
    rows, depth = sources[0][0][0].shape[1:]
    arrays, uses = [], {}
    for piece in sources:
        for array, at in piece:
            if id(array) not in uses:
                uses[id(array)] = (len(arrays), set())
                arrays.append(array)
            uses[id(array)][1].add(at)
    specs, places = [], {}
    for array in arrays:
        slot, used = uses[id(array)]
        if len(used) == 1:
            (only,) = used
            specs.append(pl.BlockSpec((1, rows, depth), lambda i, same, only=only: (only, 0, 0)))
            places[slot, only] = 0
        else:
            specs.append(whole(array))
            places.update({(slot, at): at for at in used})
    plan = [[(uses[id(array)][0], places[uses[id(array)][0], at]) for array, at in piece] for piece in sources]

    def kernel(same, *refs):
        blocks, rest = refs[: len(arrays)], refs[len(arrays):]
        own_high, own_low, far_high, far_low, first, second, high, low = rest
        for piece in range(2):
            for place, (slot, at) in enumerate(plan[piece]):
                span = slice(place * rows, (place + 1) * rows)
                high[piece, span], low[piece, span] = halves(blocks[slot][at])
        lefts = [(high[piece], low[piece]) for piece in range(2)]
        own, far = products(lefts, ((own_high, own_low), (far_high, far_low)))
        swap = same[0] == 1
        first[...] = jnp.where(swap, own, far).reshape(first.shape)
        second[...] = jnp.where(swap, far, own).reshape(second.shape)

    shape = jax.ShapeDtypeStruct((positions, rows, columns), jnp.float32)
    scratch = pltpu.VMEM((2, positions * rows, depth), jnp.bfloat16)
    return pl.pallas_call(
        kernel,
        grid_spec=pltpu.PrefetchScalarGridSpec(
            num_scalar_prefetch=1,
            grid=(1,),
            in_specs=specs + [whole(right) for right in rights],
            out_specs=[pl.BlockSpec(shape.shape, lambda i, same: (0, 0, 0))] * 2,
            scratch_shapes=[scratch, scratch],
        ),
        out_shape=[shape, shape],
        compiler_params=PARAMS,
        cost_estimate=pl.CostEstimate(
            flops=24 * positions * rows * depth * columns, bytes_accessed=12 << 20, transcendentals=0
        ),
    )(same, *arrays, *rights)


def total_kernel(place, near_a, near_b, near_own, early_a, early_b, early_own, late_a, late_b, late_own, keep, give):
    same, core, z, y = place[0] == 1, place[1], place[2], place[3]
    groups = ((EARLY, early_a, early_b, early_own), (LATE, late_a, late_b, late_own))
    for positions, one, two, own in groups:
        for place_in, (dz, dy) in enumerate(positions):
            plane, line = z ^ dz, y ^ dy
            at = plane * 4 + line
            mine = jnp.where(same, near_own[at], own[place_in])
            value = near_a[at] + near_b[at] + one[place_in] + two[place_in] + mine
            into = (plane & 1) * 4 + line

            @pl.when((plane >> 1) == core)
            def _():
                keep[into] = value

            @pl.when((plane >> 1) != core)
            def _():
                give[into] = value


def total_of(place, near, early, late):
    _, rows, columns = near[0].shape
    shape = jax.ShapeDtypeStruct((8, rows, columns), jnp.float32)
    values = [*near, *early, *late]
    return pl.pallas_call(
        total_kernel,
        grid_spec=pltpu.PrefetchScalarGridSpec(
            num_scalar_prefetch=1,
            grid=(1,),
            in_specs=[whole(value) for value in values],
            out_specs=[pl.BlockSpec(shape.shape, lambda i, place: (0, 0, 0))] * 2,
        ),
        out_shape=[shape, shape],
        compiler_params=PARAMS,
        cost_estimate=pl.CostEstimate(flops=1 << 20, bytes_accessed=4 << 20, transcendentals=0),
    )(place, *values)


def join_kernel(core, kept, given, out):
    rows = kept.shape[1]
    mine = core[0]
    out[:, pl.ds(pl.multiple_of(mine * rows, rows), rows)] = kept[...]
    out[:, pl.ds(pl.multiple_of((1 - mine) * rows, rows), rows)] = given[...]


def join(core, kept, given):
    blocks, rows, columns = kept.shape
    shape = jax.ShapeDtypeStruct((blocks, 2 * rows, columns), jnp.float32)
    return pl.pallas_call(
        join_kernel,
        grid_spec=pltpu.PrefetchScalarGridSpec(
            num_scalar_prefetch=1,
            grid=(1,),
            in_specs=[whole(kept), whole(given)],
            out_specs=pl.BlockSpec(shape.shape, lambda i, core: (0, 0, 0)),
        ),
        out_shape=shape,
        compiler_params=PARAMS,
        cost_estimate=pl.CostEstimate(flops=0, bytes_accessed=1 << 20, transcendentals=0),
    )(core, kept, given)


def cut_kernel(place, value, _, out, sem):
    depth = out.shape[0]
    at = pl.ds(pl.multiple_of(place[0] * depth, depth), depth)
    copy = pltpu.make_async_copy(value.at[at], out, sem)
    copy.start()
    copy.wait()


def cut_after(place, value, earlier, depth):
    anywhere = pl.BlockSpec(memory_space=pl.ANY)
    return pl.pallas_call(
        cut_kernel,
        grid_spec=pltpu.PrefetchScalarGridSpec(
            num_scalar_prefetch=1,
            grid=(1,),
            in_specs=[anywhere, anywhere],
            out_specs=anywhere,
            scratch_shapes=[pltpu.SemaphoreType.DMA(())],
        ),
        out_shape=jax.ShapeDtypeStruct((depth, value.shape[1]), value.dtype),
        compiler_params=PARAMS,
        cost_estimate=pl.CostEstimate(flops=0, bytes_accessed=4 << 20, transcendentals=0),
    )(place, value, earlier)


def gathered(block, small, big):
    ring = [block] + [send(block, **{small: step}) for step in (1, 2, 3)]
    line = jnp.stack(ring)
    one, three = send(line, **{big: 1}), send(line, **{big: 3})
    two = send(one[:2], **{big: 3}), send(three[2:], **{big: 1})

    def source(far, near):
        if far == 2:
            return two[near >> 1], near & 1
        return {0: line, 1: one, 3: three}[far], near

    return source


def per_device(left, right):
    rows, depth = left.shape[0] // 2, left.shape[1] // 2
    columns = right.shape[1]
    rep, grid = lax.axis_index("rep"), lax.axis_index("grid")
    core, x_hi = rep & 1, rep >> 1
    x_lo, z, y = grid >> 4, (grid >> 2) & 3, grid & 3
    same = (x_hi == x_lo).astype(jnp.int32)

    def left_part(value, at, half):
        return lax.dynamic_slice(value, (at * rows, half * depth), (rows, depth))

    swapped = send(lax.dynamic_slice(left, ((1 - core) * rows, 0), (rows, 2 * depth)), core=1)
    mine = jnp.stack([left_part(left, core, x_lo), left_part(swapped, 0, x_lo)])
    near = lax.all_gather(mine, AXES, axis=0, axis_index_groups=PLANES)

    theirs = jnp.stack([left_part(left, core, 1 - x_lo), left_part(swapped, 0, 1 - x_lo)])
    arrived = send(theirs, dx=1)
    by_y = gathered(arrived[0], "dy", "dz")
    by_z = gathered(arrived[1], "dz", "dy")

    own = lax.dynamic_slice(right, (x_lo * depth, 0), (depth, columns))
    other = send(cut_after((1 - x_lo).reshape(1), right, arrived, depth), dx=1)
    rights = (*split_right(own, send(own, core=1)), *split_right(other, send(other, core=1)))

    flag = same.reshape(1)
    first, second = near_products(flag, near, rights)
    near_sums = send_if(first, (0, 1), (1, 0)), send_if(second, None, (1, 1)), second

    far_sums = []
    for positions in (EARLY, LATE):
        sources = (
            [by_y(dz, dy) for dz, dy in positions],
            [by_z(dy, dz) for dz, dy in positions],
        )
        first, second = far_products(flag, sources, rights)
        far_sums.append((send_if(first, (1, 0), (0, 1)), send_if(second, (1, 1), None), second))

    keep, give = total_of(jnp.stack([same, core, z, y]), near_sums, *far_sums)
    return join(core.reshape(1), keep, send(give, core=1)).reshape(16 * rows, columns)


def solution(mesh):
    return jax.shard_map(
        per_device,
        mesh=mesh,
        in_specs=(P("grid", "rep"), P("rep", "grid")),
        out_specs=P("rep", "grid"),
        check_vma=False,
    )
```

```python
import jax
import jax.numpy as jnp
from jax import lax
from jax.experimental import pallas as pl
from jax.experimental.pallas import tpu as pltpu
from jax.sharding import PartitionSpec as P

AXES = ("rep", "grid")
VMEM_LIMIT = 40 * 1024 * 1024
PARAMS = pltpu.CompilerParams(vmem_limit_bytes=VMEM_LIMIT)
SHORT = pl.CostEstimate(flops=1, bytes_accessed=1, transcendentals=0)


def number(x_hi, core, x_lo, z, y):
    return (2 * x_hi + core) * 32 + 16 * x_lo + 4 * z + y


def pairs(target):
    found = []
    for x_hi in range(2):
        for core in range(2):
            for x_lo in range(2):
                for z in range(4):
                    for y in range(4):
                        there = target(x_hi, core, x_lo, z, y)
                        if there is not None:
                            found.append((number(x_hi, core, x_lo, z, y), number(*there)))
    return found


def send(value, dx=0, dz=0, dy=0, core=0):
    return lax.ppermute(
        value, AXES, pairs(lambda h, c, x, z, y: (h, c ^ core, x ^ dx, z ^ dz, y ^ dy))
    )


def send_if(value, same, other):
    def target(h, c, x, z, y):
        flips = same if h == x else other
        return None if flips is None else (h ^ flips[0], c, x ^ flips[1], z, y)

    return lax.ppermute(value, AXES, pairs(target))


PLANES = [
    [number(h, c, x, z, y) for z in range(4) for y in range(4)]
    for h in range(2) for c in range(2) for x in range(2)
]
EARLY = (
    [(0, 0, dy) for dy in range(4)] + [(1, dz, dy) for dy in (0, 1, 3) for dz in (0, 1)],
    [(0, 3, dy) for dy in range(4)] + [(1, dz, dy) for dy in (0, 1, 3) for dz in (2, 3)],
)
LATE = (
    [(0, 1, dy) for dy in range(4)] + [(1, dz, 2) for dz in (0, 1)],
    [(0, 2, dy) for dy in range(4)] + [(1, dz, 2) for dz in (2, 3)],
)


def halves(value):
    high = value.astype(jnp.bfloat16)
    return high, (value - high.astype(jnp.float32)).astype(jnp.bfloat16)


def products(left_high, left_low, high, low):
    total = None
    for one, two in ((left_high, high), (left_high, low), (left_low, high)):
        term = jnp.dot(one, two, preferred_element_type=jnp.float32)
        total = term if total is None else total + term
    columns = total.shape[1] // 2
    return total[:, :columns], total[:, columns:]


def near_kernel(flags, left, own, far, *rest):
    keep_first, keep_second, give, high, low = rest[-5:]
    same, core = flags[0] == 1, flags[1]
    columns = own.shape[1]

    @pl.when(pl.program_id(0) == 0)
    def _():
        high[:, :columns], low[:, :columns] = halves(own[...])
        high[:, columns:], low[:, columns:] = halves(far[...])

    block = left[...].reshape(left.shape[0] * left.shape[1], left.shape[2])
    mine, other = products(*halves(block), high[...], low[...])
    first = jnp.where(same, other, mine).reshape(keep_first.shape)
    second = jnp.where(same, mine, other).reshape(keep_first.shape)

    @pl.when(pl.program_id(0) == core)
    def _():
        keep_first[...] = first
        keep_second[...] = second

    @pl.when(pl.program_id(0) != core)
    def _():
        give[0] = first
        give[1] = second


def whole(value):
    return pl.BlockSpec(value.shape, lambda *_: (0,) * value.ndim, pipeline_mode=pl.Buffered(1))


def near_products(flags, left, own, far, earlier):
    positions, rows, depth = left.shape
    columns = own.shape[1]
    group = positions // 2
    kept = jax.ShapeDtypeStruct((group, rows, columns), jnp.float32)
    given = jax.ShapeDtypeStruct((2, group, rows, columns), jnp.float32)
    part = pltpu.VMEM((depth, 2 * columns), jnp.bfloat16)
    vmem = pl.BlockSpec(memory_space=pltpu.VMEM)
    *found, high, low = pl.pallas_call(
        near_kernel,
        grid_spec=pltpu.PrefetchScalarGridSpec(
            num_scalar_prefetch=1,
            grid=(2,),
            in_specs=[pl.BlockSpec((group, rows, depth), lambda i, flags: (i, 0, 0)), whole(own), whole(far)]
            + [pl.BlockSpec(memory_space=pl.ANY)] * len(earlier),
            out_specs=[whole(kept), whole(kept), whole(given), vmem, vmem],
        ),
        out_shape=[kept, kept, given, part, part],
        compiler_params=PARAMS,
        cost_estimate=SHORT,
    )(flags, left, own, far, *earlier)
    return found, [pltpu.with_memory_space_constraint(value, pltpu.VMEM) for value in (high, low)]


def far_products(flags, sources, rights, earlier):
    pieces = sources[0] + sources[1]
    entries = len(sources[0])
    columns = rights[0].shape[1] // 2
    rows, depth = pieces[0][0].shape[1:]
    arrays, uses = [], {}
    for array, at in pieces:
        if id(array) not in uses:
            uses[id(array)] = (len(arrays), set())
            arrays.append(array)
        uses[id(array)][1].add(at)
    specs, places = [], {}
    for array in arrays:
        slot, used = uses[id(array)]
        if len(used) == 1:
            (only,) = used
            specs.append(pl.BlockSpec((1, rows, depth), lambda i, flags, only=only: (only, 0, 0)))
            places[slot, only] = 0
        else:
            specs.append(whole(array))
            places.update({(slot, at): at for at in used})
    plan = [(uses[id(array)][0], places[uses[id(array)][0], at]) for array, at in pieces]

    def kernel(flags, *refs):
        blocks, rest = refs[: len(arrays)], refs[len(arrays) + len(earlier):]
        high, low, keep_first, keep_second, give, left_high, left_low = rest
        for place, (slot, at) in enumerate(plan):
            span = slice(place * rows, (place + 1) * rows)
            left_high[span], left_low[span] = halves(blocks[slot][at])
        mine, other = products(left_high[...], left_low[...], high[...], low[...])
        same, swap = flags[0] == 1, flags[2] == 1
        for at, value in enumerate((jnp.where(same, mine, other), jnp.where(same, other, mine))):
            zero, one = value[: entries * rows], value[entries * rows:]
            keep = keep_second if at else keep_first
            keep[...] = jnp.where(swap, one, zero).reshape(keep.shape)
            give[at] = jnp.where(swap, zero, one).reshape(keep.shape)

    kept = jax.ShapeDtypeStruct((entries, rows, columns), jnp.float32)
    given = jax.ShapeDtypeStruct((2, entries, rows, columns), jnp.float32)
    scratch = pltpu.VMEM((2 * entries * rows, depth), jnp.bfloat16)
    return pl.pallas_call(
        kernel,
        grid_spec=pltpu.PrefetchScalarGridSpec(
            num_scalar_prefetch=1,
            grid=(1,),
            in_specs=specs
            + [pl.BlockSpec(memory_space=pl.ANY)] * len(earlier)
            + [pl.BlockSpec(memory_space=pltpu.VMEM)] * 2,
            out_specs=[whole(kept), whole(kept), whole(given)],
            scratch_shapes=[scratch, scratch],
        ),
        out_shape=[kept, kept, given],
        compiler_params=PARAMS,
        cost_estimate=SHORT,
    )(flags, *arrays, *earlier, *rights)


def added(keep_first, keep_second, give):
    got = send(give, core=1)
    return keep_first + got[0], keep_second + got[1]


def total_kernel(place, near_a, near_b, near_own, early_a, early_b, early_own, late_a, late_b, late_own, out):
    same, swap, z, y = place[0] == 1, place[1] == 1, place[2], place[3]
    out[...] = near_a[...] + near_b[...] + jnp.where(same, near_own[...], 0.0)
    rows = early_a.shape[1]
    groups = ((EARLY, early_a, early_b, early_own), (LATE, late_a, late_b, late_own))
    for (zero, one), first, second, own in groups:
        for entry, ((half, dz, dy), (_, other_dz, _)) in enumerate(zip(zero, one)):
            plane = z ^ jnp.where(swap, other_dz, dz)
            at, span = (plane & 1) * 4 + (y ^ dy), slice(half * rows, (half + 1) * rows)
            out[at, span] += first[entry] + second[entry] + jnp.where(same, 0.0, own[entry])


def total_of(place, near, early, late):
    shape = jax.ShapeDtypeStruct(near[0].shape, jnp.float32)
    values = [*near, *early, *late]
    return pl.pallas_call(
        total_kernel,
        grid_spec=pltpu.PrefetchScalarGridSpec(
            num_scalar_prefetch=1,
            grid=(1,),
            in_specs=[whole(value) for value in values],
            out_specs=whole(shape),
        ),
        out_shape=shape,
        compiler_params=PARAMS,
        cost_estimate=SHORT,
    )(place, *values)


def cut_kernel(place, value, _, out, sem):
    depth = out.shape[0]
    at = pl.ds(pl.multiple_of(place[0] * depth, depth), depth)
    copy = pltpu.make_async_copy(value.at[at], out, sem)
    copy.start()
    copy.wait()


def cut_after(place, value, earlier, depth):
    anywhere = pl.BlockSpec(memory_space=pl.ANY)
    return pl.pallas_call(
        cut_kernel,
        grid_spec=pltpu.PrefetchScalarGridSpec(
            num_scalar_prefetch=1,
            grid=(1,),
            in_specs=[anywhere, anywhere],
            out_specs=anywhere,
            scratch_shapes=[pltpu.SemaphoreType.DMA(())],
        ),
        out_shape=jax.ShapeDtypeStruct((depth, value.shape[1]), value.dtype),
        compiler_params=PARAMS,
        cost_estimate=SHORT,
    )(place, value, earlier)


def rings(by_y, by_z):
    lines = [
        [block] + [send(block, **{axis: step}) for step in (1, 2, 3)]
        for block, axis in ((by_y, "dy"), (by_z, "dz"))
    ]
    first, second = lax.optimization_barrier(lines)
    return jnp.stack(first), jnp.stack(second)


def gathered(line, axis):
    one, three = send(line, **{axis: 1}), send(line, **{axis: 3})
    onward = one[:2], three[2:]
    two = send(onward[0], **{axis: 3}), send(onward[1], **{axis: 1})

    def source(far, near):
        if far == 2:
            return two[near >> 1], near & 1
        return {0: line, 1: one, 3: three}[far], near

    return source, onward


def per_device(left, right):
    rows, depth = left.shape[0], left.shape[1] // 2
    columns = right.shape[1]
    rep, grid = lax.axis_index("rep"), lax.axis_index("grid")
    core, x_hi = rep & 1, rep >> 1
    x_lo, z, y = grid >> 4, (grid >> 2) & 3, grid & 3
    same = (x_hi == x_lo).astype(jnp.int32)
    swap = core ^ (z >> 1)

    near = lax.all_gather(
        lax.dynamic_slice(left, (0, x_lo * depth), (rows, depth)), AXES, axis=0, axis_index_groups=PLANES
    )
    arrived = send(lax.dynamic_slice(left, (0, (1 - x_lo) * depth), (rows, depth)), dx=1)
    line_y, line_z = rings(arrived[: rows // 2], arrived[rows // 2:])
    (by_y, onward_y), (by_z, onward_z) = gathered(line_y, "dz"), gathered(line_z, "dy")

    own = lax.dynamic_slice(right, (x_lo * depth, 0), (depth, columns))
    other = send(cut_after((1 - x_lo).reshape(1), right, arrived, depth), dx=1)

    flags = jnp.stack([same, core, swap])
    products_of_near, rights = near_products(flags, near, own, other, [])
    first, second = added(*products_of_near)
    near_sums = send_if(first, (0, 1), (1, 0)), send_if(second, None, (1, 1)), second

    far_sums, earlier = [], []
    for groups in (EARLY, LATE):
        sources = [
            [by_z(dy, dz) if half else by_y(dz, dy) for half, dz, dy in group] for group in groups
        ]
        found = far_products(flags, sources, rights, earlier)
        first, second = added(*found)
        earlier = [near_sums[0], second]
        far_sums.append((send_if(first, (1, 0), (0, 1)), send_if(second, (1, 1), None), second))

    total = total_of(jnp.stack([same, swap, z, y]), near_sums, *far_sums)
    return total.reshape(8 * rows, columns)


def solution(mesh):
    return jax.shard_map(
        per_device,
        mesh=mesh,
        in_specs=(P("grid", "rep"), P("rep", "grid")),
        out_specs=P("rep", "grid"),
        check_vma=False,
    )
```

```python
import jax
import jax.numpy as jnp
from jax import lax
from jax.experimental import pallas as pl
from jax.experimental.pallas import tpu as pltpu
from jax.sharding import PartitionSpec as P

AXES = ("rep", "grid")
PARAMS = pltpu.CompilerParams(vmem_limit_bytes=40 * 1024 * 1024)
SHORT = pl.CostEstimate(flops=1, bytes_accessed=1, transcendentals=0)
NEAR = (dict(), dict(dy=1), dict(dy=3), dict(dx=1))


def number(x_hi, core, x_lo, z, y):
    return (2 * x_hi + core) * 32 + 16 * x_lo + 4 * z + y


def send(value, dhi=0, core=0, dx=0, dz=0, dy=0):
    pairs = [
        (number(h, c, x, z, y), number(h ^ dhi, c ^ core, x ^ dx, z ^ dz, y ^ dy))
        for h in range(2) for c in range(2) for x in range(2) for z in range(4) for y in range(4)
    ]
    return lax.ppermute(value, AXES, pairs)


RINGS = [
    [number(h, c, x, z, y) for y in range(4)]
    for h in range(2) for c in range(2) for x in range(2) for z in range(4)
]


def halves(value):
    high = value.astype(jnp.bfloat16)
    return high, (value - high.astype(jnp.float32)).astype(jnp.bfloat16)


def whole(value):
    return pl.BlockSpec(value.shape, lambda *_: (0,) * value.ndim, pipeline_mode=pl.Buffered(1))


ANYWHERE = pl.BlockSpec(memory_space=pl.ANY)
VMEM = pl.BlockSpec(memory_space=pltpu.VMEM)


def call(kernel, scalars, values, in_specs, out_shape, out_specs, scratch=()):
    return pl.pallas_call(
        kernel,
        grid_spec=pltpu.PrefetchScalarGridSpec(
            num_scalar_prefetch=1, grid=(1,), in_specs=in_specs, out_specs=out_specs, scratch_shapes=scratch
        ),
        out_shape=out_shape,
        compiler_params=PARAMS,
        cost_estimate=SHORT,
    )(scalars, *values)


def cut_kernel(quarter, value, _, *rest):
    outs, sems = rest[:-1], rest[-1]
    depth = outs[0].shape[0]
    copies = []
    for d, out in enumerate(outs):
        at = pl.ds(pl.multiple_of((quarter[0] ^ (d + 1)) * depth, depth), depth)
        copies.append(pltpu.make_async_copy(value.at[at], out, sems.at[d]))
    for copy in copies:
        copy.start()
    for copy in copies:
        copy.wait()


def cut_after(quarter, value, earlier):
    shape = jax.ShapeDtypeStruct((value.shape[0] // 4, value.shape[1]), value.dtype)
    return call(
        cut_kernel, quarter, (value, earlier), [ANYWHERE] * 2, [shape] * 3, [ANYWHERE] * 3,
        [pltpu.SemaphoreType.DMA((3,))],
    )


def split_kernel(_, *refs):
    pieces, (high, low) = refs[:4], refs[4:]
    columns = pieces[0].shape[1]
    for d, piece in enumerate(pieces):
        at = slice(d * columns, (d + 1) * columns)
        high[:, at], low[:, at] = halves(piece[...])


def split(scalars, pieces):
    depth, columns = pieces[0].shape
    shape = pltpu.VMEM((depth, 4 * columns), jnp.bfloat16)
    found = call(split_kernel, scalars, pieces, [whole(piece) for piece in pieces], [shape] * 2, [VMEM] * 2)
    return [pltpu.with_memory_space_constraint(value, pltpu.VMEM) for value in found]


def products(swap, groups, rights, earlier):
    arrays = [array for group in groups for array in group]
    depth = arrays[0].shape[2]
    rows = sum(array.shape[0] * array.shape[1] for array in groups[0])
    columns = rights[0].shape[1] // 4

    def kernel(swap, *refs):
        blocks, rest = refs[: len(arrays)], refs[len(arrays) + len(earlier):]
        high, low, keep, give, left_high, left_low = rest
        at = 0
        for block in blocks:
            value = block[...].reshape(block.shape[0] * block.shape[1], depth)
            span = slice(at, at + value.shape[0])
            left_high[span], left_low[span] = halves(value)
            at += value.shape[0]
        swapped = swap[0] == 1
        for d in range(4):
            span = slice(d * columns, (d + 1) * columns)
            total = jnp.dot(left_high[...], high[:, span], preferred_element_type=jnp.float32)
            total += jnp.dot(left_high[...], low[:, span], preferred_element_type=jnp.float32)
            total += jnp.dot(left_low[...], high[:, span], preferred_element_type=jnp.float32)
            total = total.reshape(2, 2, rows // 2, columns)
            for part in range(2):
                zero, one = total[0, part], total[1, part]
                into = part ^ (d == 3)
                keep[d, into] = jnp.where(swapped, one, zero)
                give[d, into] = jnp.where(swapped, zero, one)

    shape = jax.ShapeDtypeStruct((4, 2, rows // 2, columns), jnp.float32)
    scratch = pltpu.VMEM((2 * rows, depth), jnp.bfloat16)
    return call(
        kernel, swap, (*arrays, *earlier, *rights),
        [whole(array) for array in arrays] + [ANYWHERE] * len(earlier) + [VMEM] * 2,
        [shape] * 2, [whole(shape)] * 2, [scratch] * 2,
    )


def sum_kernel(side, *refs):
    terms, (mine, theirs) = refs[:-2], refs[-2:]
    for out, part in ((mine, side[0]), (theirs, 1 - side[0])):
        total = terms[0][part]
        for term in terms[1:]:
            total = total + term[part]
        out[...] = total


def summed(side, terms):
    shape = jax.ShapeDtypeStruct(terms[0].shape[1:], jnp.float32)
    return call(
        sum_kernel, side, terms, [whole(term) for term in terms], [shape] * 2, [whole(shape)] * 2
    )


def join_kernel(place, one, other_one, two, other_two, out):
    out[place[0]] = one[...] + other_one[...]
    out[1 - place[0]] = two[...] + other_two[...]


def join(place, values):
    shape = jax.ShapeDtypeStruct((2, *values[0].shape), jnp.float32)
    return call(join_kernel, place, values, [whole(value) for value in values], shape, whole(shape))


def per_device(left, right):
    rows, depth = left.shape[0], left.shape[1] // 4
    columns = right.shape[1]
    rep, grid = lax.axis_index("rep"), lax.axis_index("grid")
    core, x_hi = rep & 1, rep >> 1
    x_lo, z, y = grid >> 4, (grid >> 2) & 3, grid & 3
    quarter = 2 * (x_lo ^ (y >> 1)) + (x_lo ^ (y >> 1) ^ (y & 1))
    swap = (core ^ (z >> 1)).reshape(1)
    side = (x_hi ^ x_lo).reshape(1)

    blocks = [lax.dynamic_slice(left, (0, (number ^ (3 * x_lo)) * depth), (rows, depth)) for number in (0, 1, 3, 2)]
    mine = lax.all_to_all(jnp.stack(blocks), AXES, 0, 0, tiled=True, axis_index_groups=RINGS)
    other = send(mine, dx=1, dy=2)

    planes = []
    for part in (mine, other):
        one, three = send(part, dz=1), send(part, dz=3)
        two = send(one[:2], dz=3), send(three[2:], dz=1)
        planes.append(((part,), (one,), two, (three,)))

    pieces = [lax.dynamic_slice(right, (quarter * depth, 0), (depth, columns))]
    (ready, *_) = lax.optimization_barrier((other, planes[0][1][0], planes[0][3][0]))
    for d, piece in enumerate(cut_after(quarter.reshape(1), right, ready)):
        pieces.append(send(piece, **NEAR[d + 1]))
    rights = split(swap, pieces)

    late = [*planes[0][2], *planes[1][2]]
    ends, earlier = [], [planes[1][1][0]]
    for kept, given in ((0, 3), (1, 2)):
        groups = [[array for part in planes for array in part[dz]] for dz in (kept, given)]
        keep, give = products(swap, groups, rights, earlier)
        give, *_ = lax.optimization_barrier((give, *late))
        got = send(give, core=1)
        sums = [keep[d] + got[d] for d in range(4)]
        terms = [sums[0]] + [send(sums[d], **NEAR[d]) for d in range(1, 4)]
        earlier = [keep]
        here, there = summed(side, terms)
        ends += [here, send(there, dhi=1)]

    total = join(((z & 1) ^ swap[0]).reshape(1), ends)
    return total.reshape(8 * rows, columns)


def solution(mesh):
    return jax.shard_map(
        per_device,
        mesh=mesh,
        in_specs=(P("grid", "rep"), P("rep", "grid")),
        out_specs=P("rep", "grid"),
        check_vma=False,
    )
```

```python
import jax
import jax.numpy as jnp
from jax import lax
from jax.experimental import pallas as pl
from jax.experimental.pallas import tpu as pltpu
from jax.sharding import PartitionSpec as P

AXES = ("rep", "grid")
PARAMS = pltpu.CompilerParams(vmem_limit_bytes=40 * 1024 * 1024)
SHORT = pl.CostEstimate(flops=1, bytes_accessed=1, transcendentals=0)
NEAR = (dict(), dict(dy=1), dict(dy=3), dict(dx=1))


def number(x_hi, core, x_lo, z, y):
    return (2 * x_hi + core) * 32 + 16 * x_lo + 4 * z + y


def send(value, dhi=0, core=0, dx=0, dz=0, dy=0):
    pairs = [
        (number(h, c, x, z, y), number(h ^ dhi, c ^ core, x ^ dx, z ^ dz, y ^ dy))
        for h in range(2) for c in range(2) for x in range(2) for z in range(4) for y in range(4)
    ]
    return lax.ppermute(value, AXES, pairs)


def halves(value):
    high = value.astype(jnp.bfloat16)
    return high, (value - high.astype(jnp.float32)).astype(jnp.bfloat16)


def whole(value):
    return pl.BlockSpec(value.shape, lambda *_: (0,) * value.ndim, pipeline_mode=pl.Buffered(1))


ANYWHERE = pl.BlockSpec(memory_space=pl.ANY)
VMEM = pl.BlockSpec(memory_space=pltpu.VMEM)


def call(kernel, scalars, values, in_specs, out_shape, out_specs, scratch=()):
    return pl.pallas_call(
        kernel,
        grid_spec=pltpu.PrefetchScalarGridSpec(
            num_scalar_prefetch=1, grid=(1,), in_specs=in_specs, out_specs=out_specs, scratch_shapes=scratch
        ),
        out_shape=out_shape,
        compiler_params=PARAMS,
        cost_estimate=SHORT,
    )(scalars, *values)


def cut_kernel(quarter, value, _, *rest):
    outs, sems = rest[:-1], rest[-1]
    depth = outs[0].shape[0]
    copies = []
    for d, out in enumerate(outs):
        at = pl.ds(pl.multiple_of((quarter[0] ^ (d + 1)) * depth, depth), depth)
        copies.append(pltpu.make_async_copy(value.at[at], out, sems.at[d]))
    for copy in copies:
        copy.start()
    for copy in copies:
        copy.wait()


def cut_after(quarter, value, earlier):
    shape = jax.ShapeDtypeStruct((value.shape[0] // 4, value.shape[1]), value.dtype)
    return call(
        cut_kernel, quarter, (value, earlier), [ANYWHERE] * 2, [shape] * 3, [ANYWHERE] * 3,
        [pltpu.SemaphoreType.DMA((3,))],
    )


def split_kernel(_, *refs):
    pieces, (high, low) = refs[:4], refs[4:]
    columns = pieces[0].shape[1]
    for d, piece in enumerate(pieces):
        at = slice(d * columns, (d + 1) * columns)
        high[:, at], low[:, at] = halves(piece[...])


def split(scalars, pieces):
    depth, columns = pieces[0].shape
    shape = pltpu.VMEM((depth, 4 * columns), jnp.bfloat16)
    found = call(split_kernel, scalars, pieces, [whole(piece) for piece in pieces], [shape] * 2, [VMEM] * 2)
    return [pltpu.with_memory_space_constraint(value, pltpu.VMEM) for value in found]


def multiplied(blocks, left_high, left_low, high, low, store):
    depth = left_high.shape[1]
    at = 0
    for block in blocks:
        value = block[...].reshape(block.shape[0] * block.shape[1], depth)
        span = slice(at, at + value.shape[0])
        left_high[span], left_low[span] = halves(value)
        at += value.shape[0]
    columns = high.shape[1] // 4
    for d in range(4):
        span = slice(d * columns, (d + 1) * columns)
        total = jnp.dot(left_high[...], high[:, span], preferred_element_type=jnp.float32)
        total += jnp.dot(left_high[...], low[:, span], preferred_element_type=jnp.float32)
        total += jnp.dot(left_low[...], high[:, span], preferred_element_type=jnp.float32)
        store(d, total.reshape(-1, 2, 4, blocks[0].shape[1], columns))


def places(d):
    return [(part, block, part ^ (d == 3), block ^ (0, 1, 3, 2)[d]) for part in range(2) for block in range(4)]


def flat(planes):
    return [array for plane in planes for part in plane for array in part]


def early_products(swap, pair, ahead, rights, earlier):
    arrays = flat([*pair, ahead])
    rows, depth = arrays[0].shape[1:]
    columns = rights[0].shape[1] // 4

    def kernel(swap, *refs):
        blocks, rest = refs[: len(arrays)], refs[len(arrays) + len(earlier):]
        high, low, keep, give, third, left_high, left_low = rest
        swapped = swap[0] == 1

        def store(d, total):
            for part, block, to_part, to_block in places(d):
                zero, one = total[0, part, block], total[1, part, block]
                keep[d, to_part, to_block] = jnp.where(swapped, one, zero)
                give[d, to_part, to_block] = jnp.where(swapped, zero, one)
                third[d, to_part, to_block] = total[2, part, block]

        multiplied(blocks, left_high, left_low, high, low, store)

    shape = jax.ShapeDtypeStruct((4, 2, 4, rows, columns), jnp.float32)
    scratch = pltpu.VMEM((24 * rows, depth), jnp.bfloat16)
    return call(
        kernel, swap, (*arrays, *earlier, *rights),
        [whole(array) for array in arrays] + [ANYWHERE] * len(earlier) + [VMEM] * 2,
        [shape] * 3, [whole(shape)] * 3, [scratch] * 2,
    )


def late_products(swap, plane, third, rights, earlier):
    arrays = flat([plane])
    rows, depth = arrays[0].shape[1:]
    columns = rights[0].shape[1] // 4

    def kernel(swap, *refs):
        blocks, rest = refs[: len(arrays)], refs[len(arrays) + len(earlier):]
        high, low, ahead, keep, give, left_high, left_low = rest
        swapped = swap[0] == 1

        def store(d, total):
            for part, block, to_part, to_block in places(d):
                zero, one = ahead[d, to_part, to_block], total[0, part, block]
                keep[d, to_part, to_block] = jnp.where(swapped, one, zero)
                give[d, to_part, to_block] = jnp.where(swapped, zero, one)

        multiplied(blocks, left_high, left_low, high, low, store)

    shape = jax.ShapeDtypeStruct((4, 2, 4, rows, columns), jnp.float32)
    scratch = pltpu.VMEM((8 * rows, depth), jnp.bfloat16)
    return call(
        kernel, swap, (*arrays, *earlier, *rights, third),
        [whole(array) for array in arrays] + [ANYWHERE] * len(earlier) + [VMEM] * 2 + [whole(third)],
        [shape] * 2, [whole(shape)] * 2, [scratch] * 2,
    )


def sum_kernel(side, *refs):
    terms, (mine, theirs) = refs[:-2], refs[-2:]
    for out, part in ((mine, side[0]), (theirs, 1 - side[0])):
        total = terms[0][part]
        for term in terms[1:]:
            total = total + term[part]
        out[...] = total


def summed(side, terms):
    shape = jax.ShapeDtypeStruct(terms[0].shape[1:], jnp.float32)
    return call(
        sum_kernel, side, terms, [whole(term) for term in terms], [shape] * 2, [whole(shape)] * 2
    )


def join_kernel(place, one, other_one, two, other_two, out):
    for block in range(4):
        line = place[1] ^ block
        out[place[0], line] = one[block] + other_one[block]
        out[1 - place[0], line] = two[block] + other_two[block]


def join(place, values):
    shape = jax.ShapeDtypeStruct((2, *values[0].shape), jnp.float32)
    return call(join_kernel, place, values, [whole(value) for value in values], shape, whole(shape))


def per_device(left, right):
    rows, depth = left.shape[0], left.shape[1] // 4
    columns = right.shape[1]
    rep, grid = lax.axis_index("rep"), lax.axis_index("grid")
    core, x_hi = rep & 1, rep >> 1
    x_lo, z, y = grid >> 4, (grid >> 2) & 3, grid & 3
    quarter = 2 * (x_lo ^ (y >> 1)) + (x_lo ^ (y >> 1) ^ (y & 1))
    swap = (core ^ (z >> 1)).reshape(1)
    side = (x_hi ^ x_lo).reshape(1)

    def block(d):
        return lax.dynamic_slice(left, (0, (quarter ^ d) * depth), (rows, depth))

    mine = jnp.stack([block(0), send(block(1), dy=1), send(block(3), dy=2), send(block(2), dy=3)])
    other = send(mine, dx=1, dy=2)

    planes = []
    for part in (mine, other):
        one, three = send(part, dz=1), send(part, dz=3)
        two = send(one[:2], dz=3), send(three[2:], dz=1)
        planes.append(((part,), (one,), two, (three,)))

    pieces = [lax.dynamic_slice(right, (quarter * depth, 0), (depth, columns))]
    (ready, *_) = lax.optimization_barrier((other, planes[0][1][0], planes[0][3][0]))
    for d, piece in enumerate(cut_after(quarter.reshape(1), right, ready)):
        pieces.append(send(piece, **NEAR[d + 1]))
    rights = split(swap, pieces)

    late = [*planes[0][2], *planes[1][2]]
    zero, one, two, three = ([part[dz] for part in planes] for dz in range(4))
    keep, give, third = early_products(swap, (zero, three), one, rights, [planes[1][1][0]])
    ends = []
    for last in (False, True):
        if last:
            keep, give = late_products(swap, two, third, rights, [])
        else:
            give, *_ = lax.optimization_barrier((give, *late))
        got = send(give, core=1)
        sums = [keep[d] + got[d] for d in range(4)]
        terms = [sums[0]] + [send(sums[d], **NEAR[d]) for d in range(1, 4)]
        here, there = summed(side, terms)
        ends += [here, send(there, dhi=1)]

    total = join(jnp.stack([(z & 1) ^ swap[0], y ^ (2 * side[0])]), ends)
    return total.reshape(8 * rows, columns)


def solution(mesh):
    return jax.shard_map(
        per_device,
        mesh=mesh,
        in_specs=(P("grid", "rep"), P("rep", "grid")),
        out_specs=P("rep", "grid"),
        check_vma=False,
    )
```

```python
import jax
import jax.numpy as jnp
from jax import lax
from jax.experimental import pallas as pl
from jax.experimental.pallas import tpu as pltpu
from jax.sharding import PartitionSpec as P

AXES = ("rep", "grid")
PARAMS = pltpu.CompilerParams(vmem_limit_bytes=26 * 1024 * 1024)
SHORT = pl.CostEstimate(flops=1, bytes_accessed=1, transcendentals=0)
NEAR = (dict(), dict(dy=1), dict(dy=3), dict(dx=1))


def number(x_hi, core, x_lo, z, y):
    return (2 * x_hi + core) * 32 + 16 * x_lo + 4 * z + y


def send(value, dhi=0, core=0, dx=0, dz=0, dy=0):
    pairs = [
        (number(h, c, x, z, y), number(h ^ dhi, c ^ core, x ^ dx, z ^ dz, y ^ dy))
        for h in range(2) for c in range(2) for x in range(2) for z in range(4) for y in range(4)
    ]
    return lax.ppermute(value, AXES, pairs)


def halves(value):
    high = value.astype(jnp.bfloat16)
    return high, (value - high.astype(jnp.float32)).astype(jnp.bfloat16)


def whole(value):
    return pl.BlockSpec(value.shape, lambda *_: (0,) * value.ndim, pipeline_mode=pl.Buffered(1))


ANYWHERE = pl.BlockSpec(memory_space=pl.ANY)
VMEM = pl.BlockSpec(memory_space=pltpu.VMEM)


def call(kernel, scalars, values, in_specs, out_shape, out_specs, scratch=(), aliases=None):
    return pl.pallas_call(
        kernel,
        grid_spec=pltpu.PrefetchScalarGridSpec(
            num_scalar_prefetch=1, grid=(1,), in_specs=in_specs, out_specs=out_specs, scratch_shapes=scratch
        ),
        out_shape=out_shape,
        input_output_aliases=aliases or {},
        compiler_params=PARAMS,
        cost_estimate=SHORT,
    )(scalars, *values)


def cut_kernel(quarter, value, _, *rest):
    outs, sems = rest[:-1], rest[-1]
    depth = outs[0].shape[0]
    copies = []
    for d, out in enumerate(outs):
        at = pl.ds(pl.multiple_of((quarter[0] ^ (d + 1)) * depth, depth), depth)
        copies.append(pltpu.make_async_copy(value.at[at], out, sems.at[d]))
    for copy in copies:
        copy.start()
    for copy in copies:
        copy.wait()


def cut_after(quarter, value, earlier):
    shape = jax.ShapeDtypeStruct((value.shape[0] // 4, value.shape[1]), value.dtype)
    return call(
        cut_kernel, quarter, (value, earlier), [ANYWHERE] * 2, [shape] * 3, [ANYWHERE] * 3,
        [pltpu.SemaphoreType.DMA((3,))],
    )


def split_kernel(_, *refs):
    pieces, (high, low) = refs[:4], refs[4:]
    columns = pieces[0].shape[1]
    for d, piece in enumerate(pieces):
        at = slice(d * columns, (d + 1) * columns)
        high[:, at], low[:, at] = halves(piece[...])


def split(scalars, pieces):
    depth, columns = pieces[0].shape
    shape = pltpu.VMEM((depth, 4 * columns), jnp.bfloat16)
    found = call(split_kernel, scalars, pieces, [whole(piece) for piece in pieces], [shape] * 2, [VMEM] * 2)
    return [pltpu.with_memory_space_constraint(value, pltpu.VMEM) for value in found]


def multiplied(blocks, left_high, left_low, high, low, store):
    depth = left_high.shape[1]
    at = 0
    for block in blocks:
        value = block[...].reshape(block.shape[0] * block.shape[1], depth)
        span = slice(at, at + value.shape[0])
        left_high[span], left_low[span] = halves(value)
        at += value.shape[0]
    columns = high.shape[1] // 4
    for d in range(4):
        span = slice(d * columns, (d + 1) * columns)
        total = jnp.dot(left_high[...], high[:, span], preferred_element_type=jnp.float32)
        total += jnp.dot(left_high[...], low[:, span], preferred_element_type=jnp.float32)
        total += jnp.dot(left_low[...], high[:, span], preferred_element_type=jnp.float32)
        store(d, total.reshape(-1, 4, blocks[0].shape[1], columns))


def places(d):
    return [(block, block ^ (0, 1, 3, 2)[d]) for block in range(4)]


def early_products(swap, part, planes, rights, earlier, before=()):
    arrays = [array for plane in planes for array in plane]
    rows, depth = arrays[0].shape[1:]
    columns = rights[0].shape[1] // 4
    unread = [*earlier, *before]

    def kernel(swap, *refs):
        blocks, rest = refs[: len(arrays)], refs[len(arrays) + len(unread):]
        high, low, keep, give, third, left_high, left_low = rest
        swapped = swap[0] == 1

        def store(d, total):
            for block, into in places(d):
                zero, one = total[0, block], total[1, block]
                keep[d, 0, into] = jnp.where(swapped, one, zero)
                give[d, 0, into] = jnp.where(swapped, zero, one)
                third[d, 0, into] = total[2, block]

        multiplied(blocks, left_high, left_low, high, low, store)

    shape = jax.ShapeDtypeStruct((4, 2, 4, rows, columns), jnp.float32)
    out = pl.BlockSpec((4, 1, 4, rows, columns), lambda *_: (0, part, 0, 0, 0), pipeline_mode=pl.Buffered(1))
    scratch = pltpu.VMEM((12 * rows, depth), jnp.bfloat16)
    first = 1 + len(arrays) + len(earlier)
    return call(
        kernel, swap, (*arrays, *unread, *rights),
        [whole(array) for array in arrays] + [ANYWHERE] * len(unread) + [VMEM] * 2,
        [shape] * 3, [out] * 3, [scratch] * 2, {first + at: at for at in range(len(before))},
    )


def late_products(swap, parts, third, rights):
    arrays = [array for part in parts for array in part]
    rows, depth = arrays[0].shape[1:]
    columns = rights[0].shape[1] // 4

    def kernel(swap, *refs):
        blocks, rest = refs[: len(arrays)], refs[len(arrays):]
        high, low, ahead, keep, give, left_high, left_low = rest
        swapped = swap[0] == 1

        def store(d, total):
            for part in range(2):
                for block, into in places(d):
                    zero, one = ahead[d, part, into], total[part, block]
                    keep[d, part, into] = jnp.where(swapped, one, zero)
                    give[d, part, into] = jnp.where(swapped, zero, one)

        multiplied(blocks, left_high, left_low, high, low, store)

    shape = jax.ShapeDtypeStruct((4, 2, 4, rows, columns), jnp.float32)
    scratch = pltpu.VMEM((8 * rows, depth), jnp.bfloat16)
    return call(
        kernel, swap, (*arrays, *rights, third),
        [whole(array) for array in arrays] + [VMEM] * 2 + [whole(third)],
        [shape] * 2, [whole(shape)] * 2, [scratch] * 2,
    )


def sum_kernel(side, *refs):
    terms, (mine, theirs) = refs[:-2], refs[-2:]
    for out, part in ((mine, side[0]), (theirs, 1 - side[0])):
        across = terms[3][1 - part]
        out[...] = (terms[0][part] + terms[1][part]) + (terms[2][part] + across)


def summed(side, terms):
    shape = jax.ShapeDtypeStruct(terms[0].shape[1:], jnp.float32)
    return call(
        sum_kernel, side, terms, [whole(term) for term in terms], [shape] * 2, [whole(shape)] * 2
    )


def join_kernel(place, one, other_one, two, other_two, out):
    for block in range(4):
        line = place[1] ^ block
        out[place[0], line] = one[block] + other_one[block]
        out[1 - place[0], line] = two[block] + other_two[block]


def join(place, values):
    shape = jax.ShapeDtypeStruct((2, *values[0].shape), jnp.float32)
    return call(join_kernel, place, values, [whole(value) for value in values], shape, whole(shape))


def per_device(left, right):
    rows, depth = left.shape[0], left.shape[1] // 4
    columns = right.shape[1]
    rep, grid = lax.axis_index("rep"), lax.axis_index("grid")
    core, x_hi = rep & 1, rep >> 1
    x_lo, z, y = grid >> 4, (grid >> 2) & 3, grid & 3
    quarter = 2 * (x_lo ^ (y >> 1)) + (x_lo ^ (y >> 1) ^ (y & 1))
    swap = (core ^ (z >> 1)).reshape(1)
    side = (x_hi ^ x_lo).reshape(1)

    def block(d):
        return lax.dynamic_slice(left, (0, (quarter ^ d) * depth), (rows, depth))

    mine = jnp.stack([block(0), send(block(1), dy=1), send(block(3), dy=2), send(block(2), dy=3)])
    other = send(mine, dx=1, dy=2)

    own_one, own_three = send(mine, dz=1), send(mine, dz=3)
    far, *_ = lax.optimization_barrier((other, own_one, own_three))
    far_one, far_three = lax.optimization_barrier((send(far, dz=1), send(far, dz=3)))

    own_two, far_two = send(own_three, dz=1), send(far_one, dz=3)

    pieces = [lax.dynamic_slice(right, (quarter * depth, 0), (depth, columns))]
    for d, piece in enumerate(cut_after(quarter.reshape(1), right, other)):
        pieces.append(send(piece, **NEAR[d + 1]))
    rights = split(swap, pieces)

    before = early_products(swap, 0, ((mine,), (own_three,), (own_one,)), rights, [])
    keep, give, third = early_products(swap, 1, ((far,), (far_three,), (far_one,)), rights, [], before)
    ends = []
    for last in (False, True):
        if last:
            keep, give = late_products(swap, ((own_two,), (far_two,)), third, rights)
        else:
            give, *_ = lax.optimization_barrier((give, own_two, far_two))
        got = send(give, core=1)
        sums = [keep[d] + got[d] for d in range(4)]
        terms = [sums[0]] + [send(sums[d], **NEAR[d]) for d in range(1, 4)]
        here, there = summed(side, terms)
        ends += [here, send(there, dhi=1)]

    total = join(jnp.stack([(z & 1) ^ swap[0], y ^ (2 * side[0])]), ends)
    return total.reshape(8 * rows, columns)


def solution(mesh):
    return jax.shard_map(
        per_device,
        mesh=mesh,
        in_specs=(P("grid", "rep"), P("rep", "grid")),
        out_specs=P("rep", "grid"),
        check_vma=False,
    )
```

```python
import jax
import jax.numpy as jnp
from jax import lax
from jax.experimental import pallas as pl
from jax.experimental.pallas import tpu as pltpu
from jax.sharding import PartitionSpec as P

AXES = ("rep", "grid")
PARAMS = pltpu.CompilerParams(vmem_limit_bytes=26 * 1024 * 1024)
SHORT = pl.CostEstimate(flops=1, bytes_accessed=1, transcendentals=0)
NEAR = (dict(), dict(dy=1), dict(dy=3), dict(dx=1))


def number(x_hi, core, x_lo, z, y):
    return (2 * x_hi + core) * 32 + 16 * x_lo + 4 * z + y


def send(value, dhi=0, core=0, dx=0, dz=0, dy=0):
    pairs = [
        (number(h, c, x, z, y), number(h ^ dhi, c ^ core, x ^ dx, z ^ dz, y ^ dy))
        for h in range(2) for c in range(2) for x in range(2) for z in range(4) for y in range(4)
    ]
    return lax.ppermute(value, AXES, pairs)


def halves(value):
    high = value.astype(jnp.bfloat16)
    return high, (value - high.astype(jnp.float32)).astype(jnp.bfloat16)


def whole(value):
    return pl.BlockSpec(value.shape, lambda *_: (0,) * value.ndim, pipeline_mode=pl.Buffered(1))


ANYWHERE = pl.BlockSpec(memory_space=pl.ANY)
VMEM = pl.BlockSpec(memory_space=pltpu.VMEM)


def call(kernel, scalars, values, in_specs, out_shape, out_specs, scratch=(), aliases=None):
    return pl.pallas_call(
        kernel,
        grid_spec=pltpu.PrefetchScalarGridSpec(
            num_scalar_prefetch=1, grid=(1,), in_specs=in_specs, out_specs=out_specs, scratch_shapes=scratch
        ),
        out_shape=out_shape,
        input_output_aliases=aliases or {},
        compiler_params=PARAMS,
        cost_estimate=SHORT,
    )(scalars, *values)


def cut_kernel(quarter, value, _, *rest):
    outs, sems = rest[:-1], rest[-1]
    depth = outs[0].shape[0]
    copies = []
    for d, out in enumerate(outs):
        at = pl.ds(pl.multiple_of((quarter[0] ^ d) * depth, depth), depth)
        copies.append(pltpu.make_async_copy(value.at[at], out, sems.at[d]))
    for copy in copies:
        copy.start()
    for copy in copies:
        copy.wait()


def cut_after(quarter, value, earlier):
    shape = jax.ShapeDtypeStruct((value.shape[0] // 4, value.shape[1]), value.dtype)
    return call(
        cut_kernel, quarter, (value, earlier), [ANYWHERE] * 2, [shape] * 4, [ANYWHERE] * 4,
        [pltpu.SemaphoreType.DMA((4,))],
    )


def split_kernel(_, *refs):
    pieces, (high, low) = refs[:4], refs[4:]
    columns = pieces[0].shape[1]
    for d, piece in enumerate(pieces):
        at = slice(d * columns, (d + 1) * columns)
        high[:, at], low[:, at] = halves(piece[...])


def split(scalars, pieces):
    depth, columns = pieces[0].shape
    shape = pltpu.VMEM((depth, 4 * columns), jnp.bfloat16)
    found = call(split_kernel, scalars, pieces, [whole(piece) for piece in pieces], [shape] * 2, [VMEM] * 2)
    return [pltpu.with_memory_space_constraint(value, pltpu.VMEM) for value in found]


def multiplied(blocks, left_high, left_low, high, low, store):
    depth = left_high.shape[1]
    at = 0
    for block in blocks:
        value = block[...].reshape(block.shape[0] * block.shape[1], depth)
        span = slice(at, at + value.shape[0])
        left_high[span], left_low[span] = halves(value)
        at += value.shape[0]
    columns = high.shape[1] // 4
    for d in range(4):
        span = slice(d * columns, (d + 1) * columns)
        total = jnp.dot(left_high[...], high[:, span], preferred_element_type=jnp.float32)
        total += jnp.dot(left_high[...], low[:, span], preferred_element_type=jnp.float32)
        total += jnp.dot(left_low[...], high[:, span], preferred_element_type=jnp.float32)
        store(d, total.reshape(-1, 4, blocks[0].shape[1], columns))


def places(d):
    return [(block, block ^ (0, 1, 3, 0)[d]) for block in range(4)]


def early_products(swap, planes, rights):
    arrays = [array for plane in planes for array in plane]
    rows, depth = arrays[0].shape[1:]
    columns = rights[0].shape[1] // 4

    def kernel(swap, *refs):
        blocks, (high, low, keep, third, give, give_too, left_high, left_low) = refs[: len(arrays)], refs[len(arrays):]
        swapped = swap[0] == 1

        def store(d, total):
            for block, into in places(d):
                zero, one = total[0, block], total[1, block]
                keep[d, into] = jnp.where(swapped, one, zero)
                (give_too if d > 1 else give)[d % 2, into] = jnp.where(swapped, zero, one)
                third[d, into] = total[2, block]

        multiplied(blocks, left_high, left_low, high, low, store)

    kept, given = (jax.ShapeDtypeStruct((count, 4, rows, columns), jnp.float32) for count in (4, 2))
    scratch = pltpu.VMEM((12 * rows, depth), jnp.bfloat16)
    shapes = [kept, kept, given, given]
    return call(
        kernel, swap, (*arrays, *rights), [whole(array) for array in arrays] + [VMEM] * 2,
        shapes, [whole(shape) for shape in shapes], [scratch] * 2,
    )


def added_kernel(_, *refs):
    keeps, gots, outs = refs[:2], refs[2:6], refs[-4:]
    for part, keep in enumerate(keeps):
        for d, out in enumerate(outs):
            out[part] = keep[d] + gots[2 * part + d // 2][d % 2]


def added(scalars, keeps, gots, after):
    shape = jax.ShapeDtypeStruct((2, *keeps[0].shape[1:]), jnp.float32)
    return call(
        added_kernel, scalars, (*keeps, *gots, *after),
        [whole(value) for value in (*keeps, *gots)] + [ANYWHERE] * len(after), [shape] * 4, [whole(shape)] * 4,
    )


def late_products(swap, parts, thirds, rights, after):
    arrays = [array for part in parts for array in part]
    rows, depth = arrays[0].shape[1:]
    columns = rights[0].shape[1] // 4

    def kernel(swap, *refs):
        blocks, rest = refs[: len(arrays)], refs[len(arrays) + len(after):]
        high, low, ahead, ahead_too, keep, give, left_high, left_low = rest
        swapped = swap[0] == 1

        def store(d, total):
            for part in range(2):
                for block, into in places(d):
                    zero, one = (ahead, ahead_too)[part][d, into], total[part, block]
                    keep[d, part, into] = jnp.where(swapped, one, zero)
                    give[d, part, into] = jnp.where(swapped, zero, one)

        multiplied(blocks, left_high, left_low, high, low, store)

    shape = jax.ShapeDtypeStruct((4, 2, 4, rows, columns), jnp.float32)
    scratch = pltpu.VMEM((8 * rows, depth), jnp.bfloat16)
    return call(
        kernel, swap, (*arrays, *after, *rights, *thirds),
        [whole(array) for array in arrays] + [ANYWHERE] * len(after) + [VMEM] * 2 + [whole(third) for third in thirds],
        [shape] * 2, [whole(shape)] * 2, [scratch] * 2,
    )


def sum_kernel(side, *refs):
    terms, (mine, theirs) = refs[:-2], refs[-2:]
    for out, part in ((mine, side[0]), (theirs, 1 - side[0])):
        across = terms[3][1 - part]
        out[...] = (terms[0][part] + terms[1][part]) + (terms[2][part] + across)


def summed(side, terms):
    shape = jax.ShapeDtypeStruct(terms[0].shape[1:], jnp.float32)
    return call(
        sum_kernel, side, terms, [whole(term) for term in terms], [shape] * 2, [whole(shape)] * 2
    )


def join_kernel(place, one, other_one, two, other_two, out):
    for block in range(4):
        line = place[1] ^ block
        out[place[0], line] = one[block] + other_one[block]
        out[1 - place[0], line] = two[block] + other_two[block]


def join(place, values):
    shape = jax.ShapeDtypeStruct((2, *values[0].shape), jnp.float32)
    return call(join_kernel, place, values, [whole(value) for value in values], shape, whole(shape))


def per_device(left, right):
    rows, depth = left.shape[0], left.shape[1] // 4
    columns = right.shape[1]
    rep, grid = lax.axis_index("rep"), lax.axis_index("grid")
    core, x_hi = rep & 1, rep >> 1
    x_lo, z, y = grid >> 4, (grid >> 2) & 3, grid & 3
    quarter = 2 * (x_lo ^ (y >> 1)) + (x_lo ^ (y >> 1) ^ (y & 1))
    swap = (core ^ (z >> 1)).reshape(1)
    side = (x_hi ^ x_lo).reshape(1)

    def block(d):
        return lax.dynamic_slice(left, (0, (quarter ^ d) * depth), (rows, depth))

    mine = jnp.stack([block(0), send(block(1), dy=1), send(block(3), dy=2), send(block(2), dy=3)])
    other = jnp.stack([send(block(3), dx=1), send(block(2), dx=1, dy=1), send(block(0), dx=1, dy=2), send(block(1), dx=1, dy=3)])

    own_one, own_three = send(mine, dz=1), send(mine, dz=3)
    far, *_ = lax.optimization_barrier((other, own_one, own_three))
    far_one, far_three = lax.optimization_barrier((send(far, dz=1), send(far, dz=3)))

    own_two, far_two = send(own_three, dz=1), send(far_one, dz=3)

    pieces = cut_after(quarter.reshape(1), right, other)
    pieces = [pieces[0]] + [send(pieces[d], **NEAR[d]) for d in range(1, 4)]
    rights = split(swap, pieces)

    keeps, thirds, gots = [], [], []
    for part in ((mine, own_one, own_three), (far, far_one, far_three)):
        keep, third, *gives = early_products(swap, [(part[0],), (part[2],), (part[1],)], rights)
        keeps.append(keep)
        thirds.append(third)
        gots += [send(give, core=1) for give in gives]

    ends = []
    for last in (False, True):
        if last:
            keep, give = late_products(swap, ((own_two,), (far_two,)), thirds, rights, sums[1:])
            got = send(give, core=1)
            sums = [keep[d] + got[d] for d in range(4)]
        else:
            sums = added(swap, keeps, gots, [])
        terms = [sums[0]] + [send(sums[d], **NEAR[d]) for d in range(1, 4)]
        here, there = summed(side, terms)
        ends += [here, send(there, dhi=1)]

    total = join(jnp.stack([(z & 1) ^ swap[0], y]), ends)
    return total.reshape(8 * rows, columns)


def solution(mesh):
    return jax.shard_map(
        per_device,
        mesh=mesh,
        in_specs=(P("grid", "rep"), P("rep", "grid")),
        out_specs=P("rep", "grid"),
        check_vma=False,
    )
```

```python
import jax
import jax.numpy as jnp
from jax import lax
from jax.experimental import pallas as pl
from jax.experimental.pallas import tpu as pltpu
from jax.sharding import PartitionSpec as P

AXES = ("rep", "grid")
PARAMS = pltpu.CompilerParams(vmem_limit_bytes=26 * 1024 * 1024)
SHORT = pl.CostEstimate(flops=1, bytes_accessed=1, transcendentals=0)
NEAR = (dict(), dict(dy=1), dict(dy=3), dict(dx=1))


def number(x_hi, core, x_lo, z, y):
    return (2 * x_hi + core) * 32 + 16 * x_lo + 4 * z + y


def send(value, dhi=0, core=0, dx=0, dz=0, dy=0):
    pairs = [
        (number(h, c, x, z, y), number(h ^ dhi, c ^ core, x ^ dx, z ^ dz, y ^ dy))
        for h in range(2) for c in range(2) for x in range(2) for z in range(4) for y in range(4)
    ]
    return lax.ppermute(value, AXES, pairs)


def halves(value):
    high = value.astype(jnp.bfloat16)
    return high, (value - high.astype(jnp.float32)).astype(jnp.bfloat16)


def whole(value):
    return pl.BlockSpec(value.shape, lambda *_: (0,) * value.ndim, pipeline_mode=pl.Buffered(1))


ANYWHERE = pl.BlockSpec(memory_space=pl.ANY)
VMEM = pl.BlockSpec(memory_space=pltpu.VMEM)


def call(kernel, scalars, values, in_specs, out_shape, out_specs, scratch=(), aliases=None):
    return pl.pallas_call(
        kernel,
        grid_spec=pltpu.PrefetchScalarGridSpec(
            num_scalar_prefetch=1, grid=(1,), in_specs=in_specs, out_specs=out_specs, scratch_shapes=scratch
        ),
        out_shape=out_shape,
        input_output_aliases=aliases or {},
        compiler_params=PARAMS,
        cost_estimate=SHORT,
    )(scalars, *values)


def cut_kernel(quarter, value, _, *rest):
    outs, sems = rest[:-1], rest[-1]
    depth = outs[0].shape[0]
    copies = []
    for d, out in enumerate(outs):
        at = pl.ds(pl.multiple_of((quarter[0] ^ d) * depth, depth), depth)
        copies.append(pltpu.make_async_copy(value.at[at], out, sems.at[d]))
    for copy in copies:
        copy.start()
    for copy in copies:
        copy.wait()


def cut_after(quarter, value, earlier):
    shape = jax.ShapeDtypeStruct((value.shape[0] // 4, value.shape[1]), value.dtype)
    return call(
        cut_kernel, quarter, (value, earlier), [ANYWHERE] * 2, [shape] * 4, [ANYWHERE] * 4,
        [pltpu.SemaphoreType.DMA((4,))],
    )


def split_kernel(_, *refs):
    pieces, (high, low) = refs[:4], refs[4:]
    columns = pieces[0].shape[1]
    for d, piece in enumerate(pieces):
        at = slice(d * columns, (d + 1) * columns)
        high[:, at], low[:, at] = halves(piece[...])


def split(scalars, pieces):
    depth, columns = pieces[0].shape
    shape = pltpu.VMEM((depth, 4 * columns), jnp.bfloat16)
    found = call(split_kernel, scalars, pieces, [whole(piece) for piece in pieces], [shape] * 2, [VMEM] * 2)
    return [pltpu.with_memory_space_constraint(value, pltpu.VMEM) for value in found]


def multiplied(blocks, left_high, left_low, high, low, store):
    depth = left_high.shape[1]
    at = 0
    for block in blocks:
        value = block[...].reshape(block.shape[0] * block.shape[1], depth)
        span = slice(at, at + value.shape[0])
        left_high[span], left_low[span] = halves(value)
        at += value.shape[0]
    columns = high.shape[1] // 4
    for d in range(4):
        span = slice(d * columns, (d + 1) * columns)
        total = jnp.dot(left_high[...], high[:, span], preferred_element_type=jnp.float32)
        total += jnp.dot(left_high[...], low[:, span], preferred_element_type=jnp.float32)
        total += jnp.dot(left_low[...], high[:, span], preferred_element_type=jnp.float32)
        store(d, total.reshape(-1, 4, blocks[0].shape[1], columns))


def places(d):
    return [(block, block ^ (0, 1, 3, 0)[d]) for block in range(4)]


def early_products(swap, part, planes, rights, before=()):
    arrays = [array for plane in planes for array in plane]
    rows, depth = arrays[0].shape[1:]
    columns = rights[0].shape[1] // 4

    def kernel(swap, *refs):
        blocks, rest = refs[: len(arrays)], refs[len(arrays) + len(before):]
        high, low, keep, third, *gives, left_high, left_low = rest
        swapped = swap[0] == 1

        def store(d, total):
            for block, into in places(d):
                zero, one = total[0, block], total[1, block]
                keep[d, 0, into] = jnp.where(swapped, one, zero)
                gives[d][0, into] = jnp.where(swapped, zero, one)
                third[d, 0, into] = total[2, block]

        multiplied(blocks, left_high, left_low, high, low, store)

    kept = jax.ShapeDtypeStruct((4, 2, 4, rows, columns), jnp.float32)
    given = jax.ShapeDtypeStruct((2, 4, rows, columns), jnp.float32)
    once = pl.Buffered(1)
    kept_out = pl.BlockSpec((4, 1, 4, rows, columns), lambda *_: (0, part, 0, 0, 0), pipeline_mode=once)
    given_out = pl.BlockSpec((1, 4, rows, columns), lambda *_: (part, 0, 0, 0), pipeline_mode=once)
    scratch = pltpu.VMEM((12 * rows, depth), jnp.bfloat16)
    first = 1 + len(arrays)
    return call(
        kernel, swap, (*arrays, *before, *rights),
        [whole(array) for array in arrays] + [ANYWHERE] * len(before) + [VMEM] * 2,
        [kept] * 2 + [given] * 4, [kept_out] * 2 + [given_out] * 4, [scratch] * 2,
        {first + at: at for at in range(len(before))},
    )


def added_kernel(_, keep, *refs):
    gots, outs = refs[:len(refs) // 2], refs[len(refs) // 2:]
    for at, (got, out) in enumerate(zip(gots, outs)):
        out[...] = keep[at + 1] + got[...]


def added(scalars, keep, gots):
    shape = jax.ShapeDtypeStruct(gots[0].shape, jnp.float32)
    return call(
        added_kernel, scalars, (keep, *gots), [whole(value) for value in (keep, *gots)], [shape] * 3, [whole(shape)] * 3
    )


def late_products(swap, parts, third, rights, after):
    arrays = [array for part in parts for array in part]
    rows, depth = arrays[0].shape[1:]
    columns = rights[0].shape[1] // 4

    def kernel(swap, *refs):
        blocks, rest = refs[: len(arrays)], refs[len(arrays) + len(after):]
        high, low, ahead, keep, *gives, left_high, left_low = rest
        swapped = swap[0] == 1

        def store(d, total):
            for part in range(2):
                for block, into in places(d):
                    zero, one = ahead[d, part, into], total[part, block]
                    keep[d, part, into] = jnp.where(swapped, one, zero)
                    gives[d][part, into] = jnp.where(swapped, zero, one)

        multiplied(blocks, left_high, left_low, high, low, store)

    kept = jax.ShapeDtypeStruct((4, 2, 4, rows, columns), jnp.float32)
    given = jax.ShapeDtypeStruct((2, 4, rows, columns), jnp.float32)
    shapes = [kept] + [given] * 4
    scratch = pltpu.VMEM((8 * rows, depth), jnp.bfloat16)
    return call(
        kernel, swap, (*arrays, *after, *rights, third),
        [whole(array) for array in arrays] + [ANYWHERE] * len(after) + [VMEM] * 2 + [whole(third)],
        shapes, [whole(shape) for shape in shapes], [scratch] * 2,
    )


def sum_kernel(side, keep, got, *refs):
    terms, (mine, theirs) = refs[:-2], refs[-2:]
    for out, part in ((mine, side[0]), (theirs, 1 - side[0])):
        across = terms[2][1 - part]
        out[...] = (keep[0, part] + got[part]) + (terms[0][part] + (terms[1][part] + across))


def summed(side, keep, got, terms):
    shape = jax.ShapeDtypeStruct(got.shape[1:], jnp.float32)
    own = pl.BlockSpec((1, *keep.shape[1:]), lambda *_: (0,) * keep.ndim, pipeline_mode=pl.Buffered(1))
    return call(
        sum_kernel, side, (keep, got, *terms), [own] + [whole(value) for value in (got, *terms)],
        [shape] * 2, [whole(shape)] * 2,
    )


def join_kernel(place, one, other_one, two, other_two, out):
    for block in range(4):
        line = place[1] ^ block
        out[place[0], line] = one[block] + other_one[block]
        out[1 - place[0], line] = two[block] + other_two[block]


def join(place, values):
    shape = jax.ShapeDtypeStruct((2, *values[0].shape), jnp.float32)
    return call(join_kernel, place, values, [whole(value) for value in values], shape, whole(shape))


def per_device(left, right):
    rows, depth = left.shape[0], left.shape[1] // 4
    columns = right.shape[1]
    rep, grid = lax.axis_index("rep"), lax.axis_index("grid")
    core, x_hi = rep & 1, rep >> 1
    x_lo, z, y = grid >> 4, (grid >> 2) & 3, grid & 3
    quarter = 2 * (x_lo ^ (y >> 1)) + (x_lo ^ (y >> 1) ^ (y & 1))
    swap = (core ^ (z >> 1)).reshape(1)
    side = (x_hi ^ x_lo).reshape(1)

    def block(d):
        return lax.dynamic_slice(left, (0, (quarter ^ d) * depth), (rows, depth))

    mine = jnp.stack([block(0), send(block(1), dy=1), send(block(3), dy=2), send(block(2), dy=3)])
    others = [send(block(3), dx=1), send(block(2), dx=1, dy=1)]
    mine, *others = lax.optimization_barrier((mine, *others))
    others += [send(block(0), dx=1, dy=2), send(block(1), dx=1, dy=3)]
    other = jnp.stack(others)
    own_one, own_three = send(mine, dz=1), send(mine, dz=3)
    far, *_ = lax.optimization_barrier((other, own_one, own_three))
    far_one, far_three = lax.optimization_barrier((send(far, dz=1), send(far, dz=3)))

    own_two, far_two = send(own_three, dz=1), send(far_one, dz=3)

    pieces = cut_after(quarter.reshape(1), right, other)
    pieces = [pieces[0]] + [send(pieces[d], **NEAR[d]) for d in range(1, 4)]
    rights = split(swap, pieces)

    before = early_products(swap, 0, ((mine,), (own_three,), (own_one,)), rights)
    early = early_products(swap, 1, ((far,), (far_three,), (far_one,)), rights, before)

    ends, third, after = [], early[1], None
    for last in (False, True):
        if last:
            keep, *gives = late_products(swap, ((own_two,), (far_two,)), third, rights, after)
        else:
            keep, _, *gives = early
        got = [send(give, core=1) for give in gives]
        after = added(swap, keep, got[1:])
        here, there = summed(side, keep, got[0], [send(after[d - 1], **NEAR[d]) for d in range(1, 4)])
        ends += [here, send(there, dhi=1)]

    total = join(jnp.stack([(z & 1) ^ swap[0], y]), ends)
    return total.reshape(8 * rows, columns)


def solution(mesh):
    return jax.shard_map(
        per_device,
        mesh=mesh,
        in_specs=(P("grid", "rep"), P("rep", "grid")),
        out_specs=P("rep", "grid"),
        check_vma=False,
    )
```

```python
import jax
import jax.numpy as jnp
from jax import lax
from jax.experimental import pallas as pl
from jax.experimental.pallas import tpu as pltpu
from jax.sharding import PartitionSpec as P

AXES = ("rep", "grid")
PARAMS = pltpu.CompilerParams(vmem_limit_bytes=20 * 1024 * 1024)
SHORT = pl.CostEstimate(flops=1, bytes_accessed=1, transcendentals=0)
NEAR = (dict(), dict(dy=1), dict(dy=3), dict(dx=1))


def number(x_hi, core, x_lo, z, y):
    return (2 * x_hi + core) * 32 + 16 * x_lo + 4 * z + y


def send(value, dhi=0, core=0, dx=0, dz=0, dy=0):
    pairs = [
        (number(h, c, x, z, y), number(h ^ dhi, c ^ core, x ^ dx, z ^ dz, y ^ dy))
        for h in range(2) for c in range(2) for x in range(2) for z in range(4) for y in range(4)
    ]
    return lax.ppermute(value, AXES, pairs)


CORES = [
    [number(h, c, x, z, y) for c in range(2)]
    for h in range(2) for x in range(2) for z in range(4) for y in range(4)
]


def halves(value):
    high = value.astype(jnp.bfloat16)
    return high, (value - high.astype(jnp.float32)).astype(jnp.bfloat16)


def whole(value):
    return pl.BlockSpec(value.shape, lambda *_: (0,) * value.ndim, pipeline_mode=pl.Buffered(1))


ANYWHERE = pl.BlockSpec(memory_space=pl.ANY)
VMEM = pl.BlockSpec(memory_space=pltpu.VMEM)


def call(kernel, scalars, values, in_specs, out_shape, out_specs, scratch=(), aliases=None):
    return pl.pallas_call(
        kernel,
        grid_spec=pltpu.PrefetchScalarGridSpec(
            num_scalar_prefetch=1, grid=(1,), in_specs=in_specs, out_specs=out_specs, scratch_shapes=scratch
        ),
        out_shape=out_shape,
        input_output_aliases=aliases or {},
        compiler_params=PARAMS,
        cost_estimate=SHORT,
    )(scalars, *values)


def cut_kernel(quarter, value, _, *rest):
    outs, sems = rest[:-1], rest[-1]
    depth = outs[0].shape[0]
    copies = []
    for d, out in enumerate(outs):
        at = pl.ds(pl.multiple_of((quarter[0] ^ d) * depth, depth), depth)
        copies.append(pltpu.make_async_copy(value.at[at], out, sems.at[d]))
    for copy in copies:
        copy.start()
    for copy in copies:
        copy.wait()


def cut_after(quarter, value, earlier):
    shape = jax.ShapeDtypeStruct((value.shape[0] // 4, value.shape[1]), value.dtype)
    return call(
        cut_kernel, quarter, (value, earlier), [ANYWHERE] * 2, [shape] * 4, [ANYWHERE] * 4,
        [pltpu.SemaphoreType.DMA((4,))],
    )


def split_kernel(_, *refs):
    pieces, (high, low) = refs[:4], refs[4:]
    columns = pieces[0].shape[1]
    for d, piece in enumerate(pieces):
        at = slice(d * columns, (d + 1) * columns)
        high[:, at], low[:, at] = halves(piece[...])


def split(scalars, pieces):
    depth, columns = pieces[0].shape
    shape = pltpu.VMEM((depth, 4 * columns), jnp.bfloat16)
    found = call(split_kernel, scalars, pieces, [whole(piece) for piece in pieces], [shape] * 2, [VMEM] * 2)
    return [pltpu.with_memory_space_constraint(value, pltpu.VMEM) for value in found]


def multiplied(blocks, left_high, left_low, high, low, store):
    depth = left_high.shape[1]
    at = 0
    for block in blocks:
        value = block[...].reshape(block.shape[0] * block.shape[1], depth)
        span = slice(at, at + value.shape[0])
        left_high[span], left_low[span] = halves(value)
        at += value.shape[0]
    columns = high.shape[1] // 4
    for d in range(4):
        span = slice(d * columns, (d + 1) * columns)
        total = jnp.dot(left_high[...], high[:, span], preferred_element_type=jnp.float32)
        total += jnp.dot(left_high[...], low[:, span], preferred_element_type=jnp.float32)
        total += jnp.dot(left_low[...], high[:, span], preferred_element_type=jnp.float32)
        store(d, total.reshape(-1, 4, blocks[0].shape[1], columns))


def places(d):
    return [(block, block ^ (0, 1, 3, 2)[d]) for block in range(4)]


def early_products(swap, part, planes, rights, before=()):
    arrays = [array for plane in planes for array in plane]
    rows, depth = arrays[0].shape[1:]
    columns = rights[0].shape[1] // 4

    def kernel(swap, *refs):
        blocks, rest = refs[: len(arrays)], refs[len(arrays) + len(before):]
        high, low, keep, third, *gives, left_high, left_low = rest
        swapped = swap[0] == 1

        def store(d, total):
            for block, into in places(d):
                zero, one = total[0, block], total[1, block]
                keep[d, 0, into] = jnp.where(swapped, one, zero)
                gives[d][0, into] = jnp.where(swapped, zero, one)
                third[d, 0, into] = total[2, block]

        multiplied(blocks, left_high, left_low, high, low, store)

    kept = jax.ShapeDtypeStruct((4, 2, 4, rows, columns), jnp.float32)
    given = jax.ShapeDtypeStruct((2, 4, rows, columns), jnp.float32)
    once = pl.Buffered(1)
    kept_out = pl.BlockSpec((4, 1, 4, rows, columns), lambda *_: (0, part, 0, 0, 0), pipeline_mode=once)
    given_out = pl.BlockSpec((1, 4, rows, columns), lambda *_: (part, 0, 0, 0), pipeline_mode=once)
    scratch = pltpu.VMEM((12 * rows, depth), jnp.bfloat16)
    first = 1 + len(arrays)
    return call(
        kernel, swap, (*arrays, *before, *rights),
        [whole(array) for array in arrays] + [ANYWHERE] * len(before) + [VMEM] * 2,
        [kept] * 2 + [given] * 4, [kept_out] * 2 + [given_out] * 4, [scratch] * 2,
        {first + at: at for at in range(len(before))},
    )


def added_kernel(_, keep, *refs):
    gots, outs = refs[:len(refs) // 2], refs[len(refs) // 2:]
    for at, (got, out) in enumerate(zip(gots, outs)):
        out[...] = keep[at + 1] + got[...]


def added(scalars, keep, gots):
    shape = jax.ShapeDtypeStruct(gots[0].shape, jnp.float32)
    return call(
        added_kernel, scalars, (keep, *gots), [whole(value) for value in (keep, *gots)], [shape] * 3, [whole(shape)] * 3
    )


def late_products(flags, parts, third, rights, after):
    arrays = [array for part in parts for array in part]
    rows, depth = arrays[0].shape[1:]
    columns = rights[0].shape[1] // 4

    def kernel(flags, *refs):
        blocks, rest = refs[: len(arrays)], refs[len(arrays) + len(after):]
        high, low, ahead, keep, give, both, left_high, left_low = rest
        swapped, core = flags[0] == 1, flags[1]

        def store(d, total):
            for part in range(2):
                for block, into in places(d):
                    zero, one = ahead[d, part, into], total[part, block]
                    kept, given = jnp.where(swapped, one, zero), jnp.where(swapped, zero, one)
                    if d == 0:
                        keep[0, part, into], give[part, into] = kept, given
                    else:
                        both[core, d - 1, part, into], both[1 - core, d - 1, part, into] = kept, given

        multiplied(blocks, left_high, left_low, high, low, store)

    piece = (2, 4, rows, columns)
    shapes = [jax.ShapeDtypeStruct(shape, jnp.float32) for shape in ((1, *piece), piece, (2, 3, *piece))]
    scratch = pltpu.VMEM((8 * rows, depth), jnp.bfloat16)
    return call(
        kernel, flags, (*arrays, *after, *rights, third),
        [whole(array) for array in arrays] + [ANYWHERE] * len(after) + [VMEM] * 2 + [whole(third)],
        shapes, [whole(shape) for shape in shapes], [scratch] * 2,
    )


def added_by_core_kernel(_, both, *outs):
    for d, out in enumerate(outs):
        out[...] = both[0, d] + both[1, d]


def added_by_core(scalars, both):
    shape = jax.ShapeDtypeStruct(both.shape[2:], jnp.float32)
    return call(added_by_core_kernel, scalars, (both,), [whole(both)], [shape] * 3, [whole(shape)] * 3)


def sum_kernel(side, keep, got, *refs):
    terms, (mine, theirs) = refs[:-2], refs[-2:]
    for out, part in ((mine, side[0]), (theirs, 1 - side[0])):
        across = terms[2][1 - part]
        out[...] = (keep[0, part] + got[part]) + (terms[0][part] + (terms[1][part] + across))


def summed(side, keep, got, terms):
    shape = jax.ShapeDtypeStruct(got.shape[1:], jnp.float32)
    own = pl.BlockSpec((1, *keep.shape[1:]), lambda *_: (0,) * keep.ndim, pipeline_mode=pl.Buffered(1))
    return call(
        sum_kernel, side, (keep, got, *terms), [own] + [whole(value) for value in (got, *terms)],
        [shape] * 2, [whole(shape)] * 2,
    )


def join_kernel(place, one, other_one, two, other_two, out):
    for block in range(4):
        line = place[1] ^ block
        out[place[0], line] = one[block] + other_one[block]
        out[1 - place[0], line] = two[block] + other_two[block]


def join(place, values):
    shape = jax.ShapeDtypeStruct((2, *values[0].shape), jnp.float32)
    return call(join_kernel, place, values, [whole(value) for value in values], shape, whole(shape))


def per_device(left, right):
    rows, depth = left.shape[0], left.shape[1] // 4
    columns = right.shape[1]
    rep, grid = lax.axis_index("rep"), lax.axis_index("grid")
    core, x_hi = rep & 1, rep >> 1
    x_lo, z, y = grid >> 4, (grid >> 2) & 3, grid & 3
    quarter = 2 * (x_lo ^ (y >> 1)) + (x_lo ^ (y >> 1) ^ (y & 1))
    swap = (core ^ (z >> 1)).reshape(1)
    side = (x_hi ^ x_lo).reshape(1)

    def block(d):
        return lax.dynamic_slice(left, (0, (quarter ^ d) * depth), (rows, depth))

    mine = jnp.stack([block(0), send(block(1), dy=1), send(block(3), dy=2), send(block(2), dy=3)])
    other = send(mine, dx=1, dy=2)
    own_one, own_three = send(mine, dz=1), send(mine, dz=3)
    far, *_ = lax.optimization_barrier((other, own_one, own_three))
    far_one, far_three = lax.optimization_barrier((send(far, dz=1), send(far, dz=3)))

    own_two, far_two = send(own_three, dz=1), send(far_one, dz=3)

    pieces = cut_after(quarter.reshape(1), right, other)
    pieces = [pieces[0]] + [send(pieces[d], **NEAR[d]) for d in range(1, 4)]
    rights = split(swap, pieces)

    before = early_products(swap, 0, ((mine,), (own_three,), (own_one,)), rights)
    early = early_products(swap, 1, ((far,), (far_three,), (far_one,)), rights, before)

    keep, third, *gives = early
    got = [send(give, core=1) for give in gives]
    sums = added(swap, keep, got[1:])
    late_keep, late_give, both = late_products(
        jnp.stack([swap[0], core]), ((own_two,), (far_two,)), third, rights, sums
    )
    both = lax.all_to_all(both, AXES, 0, 0, tiled=True, axis_index_groups=CORES)

    ends = []
    for kept, given, terms in ((keep, got[0], sums), (late_keep, send(late_give, core=1), added_by_core(swap, both))):
        across = send(terms[2], **NEAR[3])
        here, there = summed(side, kept, given, [send(terms[0], **NEAR[1]), send(terms[1], **NEAR[2]), across])
        ends += [here, send(there, dhi=1)]

    total = join(jnp.stack([(z & 1) ^ swap[0], y ^ (2 * side[0])]), ends)
    return total.reshape(8 * rows, columns)


def solution(mesh):
    return jax.shard_map(
        per_device,
        mesh=mesh,
        in_specs=(P("grid", "rep"), P("rep", "grid")),
        out_specs=P("rep", "grid"),
        check_vma=False,
    )
```

```python
import jax
import jax.numpy as jnp
from jax import lax
from jax.experimental import pallas as pl
from jax.experimental.pallas import tpu as pltpu
from jax.sharding import PartitionSpec as P

AXES = ("rep", "grid")
PARAMS = pltpu.CompilerParams(vmem_limit_bytes=20 * 1024 * 1024)
SHORT = pl.CostEstimate(flops=1, bytes_accessed=1, transcendentals=0)
NEAR = (dict(), dict(dx=1), dict(dy=1), dict(dy=3))
DIFFERS = (0, 3, 1, 2)


def number(x_hi, core, x_lo, z, y):
    return (2 * x_hi + core) * 32 + 16 * x_lo + 4 * z + y


def send(value, dhi=0, core=0, dx=0, dz=0, dy=0):
    pairs = [
        (number(h, c, x, z, y), number(h ^ dhi, c ^ core, x ^ dx, z ^ dz, y ^ dy))
        for h in range(2) for c in range(2) for x in range(2) for z in range(4) for y in range(4)
    ]
    return lax.ppermute(value, AXES, pairs)


CORES = [
    [number(h, c, x, z, y) for c in range(2)]
    for h in range(2) for x in range(2) for z in range(4) for y in range(4)
]


def halves(value):
    high = value.astype(jnp.bfloat16)
    return high, (value - high.astype(jnp.float32)).astype(jnp.bfloat16)


def whole(value):
    return pl.BlockSpec(value.shape, lambda *_: (0,) * value.ndim, pipeline_mode=pl.Buffered(1))


ANYWHERE = pl.BlockSpec(memory_space=pl.ANY)
VMEM = pl.BlockSpec(memory_space=pltpu.VMEM)


def call(kernel, scalars, values, in_specs, out_shape, out_specs, scratch=(), aliases=None):
    return pl.pallas_call(
        kernel,
        grid_spec=pltpu.PrefetchScalarGridSpec(
            num_scalar_prefetch=1, grid=(1,), in_specs=in_specs, out_specs=out_specs, scratch_shapes=scratch
        ),
        out_shape=out_shape,
        input_output_aliases=aliases or {},
        compiler_params=PARAMS,
        cost_estimate=SHORT,
    )(scalars, *values)


def cut_kernel(quarter, value, _, *rest):
    outs, sems = rest[:-1], rest[-1]
    depth = outs[0].shape[0]
    copies = []
    for d, out in enumerate(outs):
        at = pl.ds(pl.multiple_of((quarter[0] ^ DIFFERS[d]) * depth, depth), depth)
        copies.append(pltpu.make_async_copy(value.at[at], out, sems.at[d]))
    for copy in copies:
        copy.start()
    for copy in copies:
        copy.wait()


def cut_after(quarter, value, earlier):
    shape = jax.ShapeDtypeStruct((value.shape[0] // 4, value.shape[1]), value.dtype)
    return call(
        cut_kernel, quarter, (value, earlier), [ANYWHERE] * 2, [shape] * 4, [ANYWHERE] * 4,
        [pltpu.SemaphoreType.DMA((4,))],
    )


def split_kernel(_, *refs):
    pieces, (high, low) = refs[:4], refs[4:]
    columns = pieces[0].shape[1]
    for d, piece in enumerate(pieces):
        at = slice(d * columns, (d + 1) * columns)
        high[:, at], low[:, at] = halves(piece[...])


def split(scalars, pieces):
    depth, columns = pieces[0].shape
    shape = pltpu.VMEM((depth, 4 * columns), jnp.bfloat16)
    found = call(split_kernel, scalars, pieces, [whole(piece) for piece in pieces], [shape] * 2, [VMEM] * 2)
    return [pltpu.with_memory_space_constraint(value, pltpu.VMEM) for value in found]


def multiplied(blocks, left_high, left_low, high, low, store):
    depth = left_high.shape[1]
    at = 0
    for block in blocks:
        value = block[...].reshape(block.shape[0] * block.shape[1], depth)
        span = slice(at, at + value.shape[0])
        left_high[span], left_low[span] = halves(value)
        at += value.shape[0]
    columns = high.shape[1] // 4
    for d in range(4):
        span = slice(d * columns, (d + 1) * columns)
        total = jnp.dot(left_high[...], high[:, span], preferred_element_type=jnp.float32)
        total += jnp.dot(left_high[...], low[:, span], preferred_element_type=jnp.float32)
        total += jnp.dot(left_low[...], high[:, span], preferred_element_type=jnp.float32)
        store(d, total.reshape(-1, 4, blocks[0].shape[1], columns))


def places(d):
    return [(block, block ^ (0, 2, 1, 3)[d]) for block in range(4)]


def early_products(swap, part, planes, rights, before=()):
    arrays = [array for plane in planes for array in plane]
    rows, depth = arrays[0].shape[1:]
    columns = rights[0].shape[1] // 4

    def kernel(swap, *refs):
        blocks, rest = refs[: len(arrays)], refs[len(arrays) + len(before):]
        high, low, keep, third, *gives, left_high, left_low = rest
        swapped = swap[0] == 1

        def store(d, total):
            for block, into in places(d):
                zero, one = total[0, block], total[1, block]
                keep[d, 0, into] = jnp.where(swapped, one, zero)
                gives[d][0, into] = jnp.where(swapped, zero, one)
                third[d, 0, into] = total[2, block]

        multiplied(blocks, left_high, left_low, high, low, store)

    kept = jax.ShapeDtypeStruct((4, 2, 4, rows, columns), jnp.float32)
    given = jax.ShapeDtypeStruct((2, 4, rows, columns), jnp.float32)
    once = pl.Buffered(1)
    kept_out = pl.BlockSpec((4, 1, 4, rows, columns), lambda *_: (0, part, 0, 0, 0), pipeline_mode=once)
    given_out = pl.BlockSpec((1, 4, rows, columns), lambda *_: (part, 0, 0, 0), pipeline_mode=once)
    scratch = pltpu.VMEM((12 * rows, depth), jnp.bfloat16)
    first = 1 + len(arrays)
    return call(
        kernel, swap, (*arrays, *before, *rights),
        [whole(array) for array in arrays] + [ANYWHERE] * len(before) + [VMEM] * 2,
        [kept] * 2 + [given] * 4, [kept_out] * 2 + [given_out] * 4, [scratch] * 2,
        {first + at: at for at in range(len(before))},
    )


def added_kernel(_, keep, *refs):
    gots, outs = refs[:len(refs) // 2], refs[len(refs) // 2:]
    for at, (got, out) in enumerate(zip(gots, outs)):
        out[...] = keep[at + 1] + got[...]


def added(scalars, keep, gots):
    shape = jax.ShapeDtypeStruct(gots[0].shape, jnp.float32)
    return call(
        added_kernel, scalars, (keep, *gots), [whole(value) for value in (keep, *gots)], [shape] * 3, [whole(shape)] * 3
    )


def late_products(flags, parts, third, rights, after):
    arrays = [array for part in parts for array in part]
    rows, depth = arrays[0].shape[1:]
    columns = rights[0].shape[1] // 4

    def kernel(flags, *refs):
        blocks, rest = refs[: len(arrays)], refs[len(arrays) + len(after):]
        high, low, ahead, keep, give, both, left_high, left_low = rest
        swapped, core = flags[0] == 1, flags[1]

        def store(d, total):
            for part in range(2):
                for block, into in places(d):
                    zero, one = ahead[d, part, into], total[part, block]
                    kept, given = jnp.where(swapped, one, zero), jnp.where(swapped, zero, one)
                    if d == 0:
                        keep[0, part, into], give[part, into] = kept, given
                    else:
                        both[core, d - 1, part, into], both[1 - core, d - 1, part, into] = kept, given

        multiplied(blocks, left_high, left_low, high, low, store)

    piece = (2, 4, rows, columns)
    shapes = [jax.ShapeDtypeStruct(shape, jnp.float32) for shape in ((1, *piece), piece, (2, 3, *piece))]
    scratch = pltpu.VMEM((8 * rows, depth), jnp.bfloat16)
    return call(
        kernel, flags, (*arrays, *after, *rights, third),
        [whole(array) for array in arrays] + [ANYWHERE] * len(after) + [VMEM] * 2 + [whole(third)],
        shapes, [whole(shape) for shape in shapes], [scratch] * 2,
    )


def added_by_core_kernel(side, both, *outs):
    for d, (here, there) in enumerate(zip(outs[:3], outs[3:])):
        here[...] = both[0, d, side[0]] + both[1, d, side[0]]
        there[...] = both[0, d, 1 - side[0]] + both[1, d, 1 - side[0]]


def added_by_core(side, both):
    shape = jax.ShapeDtypeStruct(both.shape[3:], jnp.float32)
    found = call(added_by_core_kernel, side, (both,), [whole(both)], [shape] * 6, [whole(shape)] * 6)
    return found[:3], found[3:]


def onward_kernel(side, keep, got, one, two, three, out):
    part = 1 - side[0]
    out[...] = (keep[0, part] + got[part]) + (one[...] + (two[...] + three[...]))


def onward(side, keep, got, terms):
    shape = jax.ShapeDtypeStruct(got.shape[1:], jnp.float32)
    values = (keep, got, *terms)
    return call(onward_kernel, side, values, [whole(value) for value in values], shape, whole(shape))


def sum_kernel(side, keep, got, *refs):
    terms, (mine, theirs) = refs[:-2], refs[-2:]
    for out, part in ((mine, side[0]), (theirs, 1 - side[0])):
        across = terms[0][1 - part]
        out[...] = (keep[0, part] + got[part]) + (across + (terms[1][part] + terms[2][part]))


def summed(side, keep, got, terms):
    shape = jax.ShapeDtypeStruct(got.shape[1:], jnp.float32)
    own = pl.BlockSpec((1, *keep.shape[1:]), lambda *_: (0,) * keep.ndim, pipeline_mode=pl.Buffered(1))
    return call(
        sum_kernel, side, (keep, got, *terms), [own] + [whole(value) for value in (got, *terms)],
        [shape] * 2, [whole(shape)] * 2,
    )


def join_kernel(place, one, other_one, keep, got, across, two, three, other_two, out):
    part = place[2]
    for block in range(4):
        line = place[1] ^ block
        out[place[0], line] = one[block] + other_one[block]
        near = across[block] + (two[block] + three[block])
        out[1 - place[0], line] = (keep[0, part, block] + got[part, block]) + (near + other_two[block])


def join(place, values):
    shape = jax.ShapeDtypeStruct((2, *values[0].shape), jnp.float32)
    return call(join_kernel, place, values, [whole(value) for value in values], shape, whole(shape))


def per_device(left, right):
    rows, depth = left.shape[0], left.shape[1] // 4
    columns = right.shape[1]
    rep, grid = lax.axis_index("rep"), lax.axis_index("grid")
    core, x_hi = rep & 1, rep >> 1
    x_lo, z, y = grid >> 4, (grid >> 2) & 3, grid & 3
    quarter = 2 * (x_lo ^ (y >> 1)) + (x_lo ^ (y >> 1) ^ (y & 1))
    swap = (core ^ (z >> 1)).reshape(1)
    side = (x_hi ^ x_lo).reshape(1)

    def block(d):
        return lax.dynamic_slice(left, (0, (quarter ^ d) * depth), (rows, depth))

    mine = jnp.stack([block(0), send(block(1), dy=1), send(block(3), dy=2), send(block(2), dy=3)])
    other = send(mine, dx=1, dy=2)
    own_one, own_three = send(mine, dz=1), send(mine, dz=3)
    pieces = cut_after(quarter.reshape(1), right, other)
    far, *_ = lax.optimization_barrier((other, own_one, own_three, *pieces))
    far_one, far_three = lax.optimization_barrier((send(far, dz=1), send(far, dz=3)))

    own_two, far_two = send(own_three, dz=1), send(far_one, dz=3)

    pieces = [pieces[0]] + [send(pieces[d], **NEAR[d]) for d in range(1, 4)]
    rights = split(swap, pieces)

    before = early_products(swap, 0, ((mine,), (own_three,), (own_one,)), rights)
    early = early_products(swap, 1, ((far,), (far_three,), (far_one,)), rights, before)

    keep, third, *gives = early
    got = [send(give, core=1) for give in gives]
    sums = added(swap, keep, got[1:])
    late_keep, late_give, both = late_products(
        jnp.stack([swap[0], core]), ((own_two,), (far_two,)), third, rights, sums
    )
    both = lax.all_to_all(both, AXES, 0, 0, tiled=True, axis_index_groups=CORES)

    here, there = summed(side, keep, got[0], [send(sums[d - 1], **NEAR[d]) for d in range(1, 4)])
    early_ends = here, send(there, dhi=1)

    late_got = send(late_give, core=1)
    kept, passed = added_by_core(side, both)
    passed = [send(passed[d - 1], **NEAR[d]) for d in range(1, 4)]
    passed = send(onward(side, late_keep, late_got, passed), dhi=1)
    kept = [send(kept[d - 1], **NEAR[d]) for d in range(1, 4)]

    place = jnp.stack([(z & 1) ^ swap[0], y ^ (2 * side[0]), side[0]])
    total = join(place, (*early_ends, late_keep, late_got, *kept, passed))
    return total.reshape(8 * rows, columns)


def solution(mesh):
    return jax.shard_map(
        per_device,
        mesh=mesh,
        in_specs=(P("grid", "rep"), P("rep", "grid")),
        out_specs=P("rep", "grid"),
        check_vma=False,
    )
```

```python
import jax
import jax.numpy as jnp
from jax import lax
from jax.experimental import pallas as pl
from jax.experimental.pallas import tpu as pltpu
from jax.sharding import PartitionSpec as P

AXES = ("rep", "grid")
PARAMS = pltpu.CompilerParams(vmem_limit_bytes=20 * 1024 * 1024)
SHORT = pl.CostEstimate(flops=1, bytes_accessed=1, transcendentals=0)
NEAR = (dict(), dict(dx=1), dict(dy=1), dict(dy=3))
DIFFERS = (0, 3, 1, 2)


def number(x_hi, core, x_lo, z, y):
    return (2 * x_hi + core) * 32 + 16 * x_lo + 4 * z + y


def send(value, dhi=0, core=0, dx=0, dz=0, dy=0):
    pairs = [
        (number(h, c, x, z, y), number(h ^ dhi, c ^ core, x ^ dx, z ^ dz, y ^ dy))
        for h in range(2) for c in range(2) for x in range(2) for z in range(4) for y in range(4)
    ]
    return lax.ppermute(value, AXES, pairs)


CORES = [
    [number(h, c, x, z, y) for c in range(2)]
    for h in range(2) for x in range(2) for z in range(4) for y in range(4)
]


def halves(value):
    high = value.astype(jnp.bfloat16)
    return high, (value - high.astype(jnp.float32)).astype(jnp.bfloat16)


def whole(value):
    return pl.BlockSpec(value.shape, lambda *_: (0,) * value.ndim, pipeline_mode=pl.Buffered(1))


ANYWHERE = pl.BlockSpec(memory_space=pl.ANY)
VMEM = pl.BlockSpec(memory_space=pltpu.VMEM)


def call(kernel, scalars, values, in_specs, out_shape, out_specs, scratch=(), aliases=None):
    return pl.pallas_call(
        kernel,
        grid_spec=pltpu.PrefetchScalarGridSpec(
            num_scalar_prefetch=1, grid=(1,), in_specs=in_specs, out_specs=out_specs, scratch_shapes=scratch
        ),
        out_shape=out_shape,
        input_output_aliases=aliases or {},
        compiler_params=PARAMS,
        cost_estimate=SHORT,
    )(scalars, *values)


def cut_kernel(quarter, value, _, *rest):
    outs, sems = rest[:-1], rest[-1]
    depth = outs[0].shape[0]
    copies = []
    for d, out in enumerate(outs):
        at = pl.ds(pl.multiple_of((quarter[0] ^ DIFFERS[d]) * depth, depth), depth)
        copies.append(pltpu.make_async_copy(value.at[at], out, sems.at[d]))
    for copy in copies:
        copy.start()
    for copy in copies:
        copy.wait()


def cut_after(quarter, value, earlier):
    shape = jax.ShapeDtypeStruct((value.shape[0] // 4, value.shape[1]), value.dtype)
    return call(
        cut_kernel, quarter, (value, earlier), [ANYWHERE] * 2, [shape] * 4, [ANYWHERE] * 4,
        [pltpu.SemaphoreType.DMA((4,))],
    )


def split_kernel(_, *refs):
    pieces, (high, low) = refs[:4], refs[4:]
    columns = pieces[0].shape[1]
    for d, piece in enumerate(pieces):
        at = slice(d * columns, (d + 1) * columns)
        high[:, at], low[:, at] = halves(piece[...])


def split(scalars, pieces):
    depth, columns = pieces[0].shape
    shape = pltpu.VMEM((depth, 4 * columns), jnp.bfloat16)
    found = call(split_kernel, scalars, pieces, [whole(piece) for piece in pieces], [shape] * 2, [VMEM] * 2)
    return [pltpu.with_memory_space_constraint(value, pltpu.VMEM) for value in found]


def multiplied(blocks, left_high, left_low, high, low, store):
    depth = left_high.shape[1]
    at = 0
    for block in blocks:
        value = block[...].reshape(block.shape[0] * block.shape[1], depth)
        span = slice(at, at + value.shape[0])
        left_high[span], left_low[span] = halves(value)
        at += value.shape[0]
    columns = high.shape[1] // 4
    for d in range(4):
        span = slice(d * columns, (d + 1) * columns)
        total = jnp.dot(left_high[...], high[:, span], preferred_element_type=jnp.float32)
        total += jnp.dot(left_high[...], low[:, span], preferred_element_type=jnp.float32)
        total += jnp.dot(left_low[...], high[:, span], preferred_element_type=jnp.float32)
        store(d, total.reshape(-1, 4, blocks[0].shape[1], columns))


def places(d):
    return [(block, block ^ (0, 2, 1, 3)[d]) for block in range(4)]


def early_products(swap, part, planes, rights, before=()):
    arrays = [array for plane in planes for array in plane]
    rows, depth = arrays[0].shape[1:]
    columns = rights[0].shape[1] // 4

    def kernel(swap, *refs):
        blocks, rest = refs[: len(arrays)], refs[len(arrays) + len(before):]
        high, low, keep, third, *gives, left_high, left_low = rest
        swapped = swap[0] == 1

        def store(d, total):
            for block, into in places(d):
                zero, one = total[0, block], total[1, block]
                keep[d, 0, into] = jnp.where(swapped, one, zero)
                gives[d][0, into] = jnp.where(swapped, zero, one)
                third[d, 0, into] = total[2, block]

        multiplied(blocks, left_high, left_low, high, low, store)

    kept = jax.ShapeDtypeStruct((4, 2, 4, rows, columns), jnp.float32)
    given = jax.ShapeDtypeStruct((2, 4, rows, columns), jnp.float32)
    once = pl.Buffered(1)
    kept_out = pl.BlockSpec((4, 1, 4, rows, columns), lambda *_: (0, part, 0, 0, 0), pipeline_mode=once)
    given_out = pl.BlockSpec((1, 4, rows, columns), lambda *_: (part, 0, 0, 0), pipeline_mode=once)
    scratch = pltpu.VMEM((12 * rows, depth), jnp.bfloat16)
    first = 1 + len(arrays)
    return call(
        kernel, swap, (*arrays, *before, *rights),
        [whole(array) for array in arrays] + [ANYWHERE] * len(before) + [VMEM] * 2,
        [kept] * 2 + [given] * 4, [kept_out] * 2 + [given_out] * 4, [scratch] * 2,
        {first + at: at for at in range(len(before))},
    )


def added_kernel(_, keep, *refs):
    gots, outs = refs[:len(refs) // 2], refs[len(refs) // 2:]
    for at, (got, out) in enumerate(zip(gots, outs)):
        out[...] = keep[at + 1] + got[...]


def added(scalars, keep, gots):
    shape = jax.ShapeDtypeStruct(gots[0].shape, jnp.float32)
    return call(
        added_kernel, scalars, (keep, *gots), [whole(value) for value in (keep, *gots)], [shape] * 3, [whole(shape)] * 3
    )


def late_products(flags, parts, third, rights, after):
    arrays = [array for part in parts for array in part]
    rows, depth = arrays[0].shape[1:]
    columns = rights[0].shape[1] // 4

    def kernel(flags, *refs):
        blocks, rest = refs[: len(arrays)], refs[len(arrays) + len(after):]
        high, low, ahead, keep, give, both, here_keep, here_give, left_high, left_low = rest
        swapped, core, side = flags[0] == 1, flags[1], flags[2] == 1

        def store(d, total):
            for block, into in places(d):
                kept, given = [], []
                for part in range(2):
                    zero, one = ahead[d, part, into], total[part, block]
                    kept.append(jnp.where(swapped, one, zero))
                    given.append(jnp.where(swapped, zero, one))
                if d == 0:
                    for part in range(2):
                        keep[0, part, into], give[part, into] = kept[part], given[part]
                else:
                    here_keep[d - 1, into] = jnp.where(side, kept[1], kept[0])
                    here_give[d - 1, into] = jnp.where(side, given[1], given[0])
                    both[core, d - 1, into] = jnp.where(side, kept[0], kept[1])
                    both[1 - core, d - 1, into] = jnp.where(side, given[0], given[1])

        multiplied(blocks, left_high, left_low, high, low, store)

    piece = (4, rows, columns)
    shapes = [
        jax.ShapeDtypeStruct(shape, jnp.float32)
        for shape in ((1, 2, *piece), (2, *piece), (2, 3, *piece), (3, *piece), (3, *piece))
    ]
    scratch = pltpu.VMEM((8 * rows, depth), jnp.bfloat16)
    return call(
        kernel, flags, (*arrays, *after, *rights, third),
        [whole(array) for array in arrays] + [ANYWHERE] * len(after) + [VMEM] * 2 + [whole(third)],
        shapes, [whole(shape) for shape in shapes], [scratch] * 2,
    )


def three_kernel(_, one, two, *outs):
    for d, out in enumerate(outs):
        out[...] = one[d] + two[d]


def three_sums(scalars, one, two):
    shape = jax.ShapeDtypeStruct(one.shape[1:], jnp.float32)
    return call(three_kernel, scalars, (one, two), [whole(one), whole(two)], [shape] * 3, [whole(shape)] * 3)


def both_kernel(_, both, *outs):
    for d, out in enumerate(outs):
        out[...] = both[0, d] + both[1, d]


def both_sums(scalars, both):
    shape = jax.ShapeDtypeStruct(both.shape[2:], jnp.float32)
    return call(both_kernel, scalars, (both,), [whole(both)], [shape] * 3, [whole(shape)] * 3)


def onward_kernel(side, keep, got, one, two, three, *rest):
    out = rest[-1]
    part = 1 - side[0]
    out[...] = (keep[0, part] + got[part]) + (one[...] + (two[...] + three[...]))


def onward(side, keep, got, terms, after):
    shape = jax.ShapeDtypeStruct(got.shape[1:], jnp.float32)
    values = (keep, got, *terms)
    specs = [whole(value) for value in values] + [ANYWHERE] * len(after)
    return call(onward_kernel, side, (*values, *after), specs, shape, whole(shape))


def sum_kernel(side, keep, got, *refs):
    terms, (mine, theirs) = refs[:-2], refs[-2:]
    for out, part in ((mine, side[0]), (theirs, 1 - side[0])):
        across = terms[0][1 - part]
        out[...] = (keep[0, part] + got[part]) + (across + (terms[1][part] + terms[2][part]))


def summed(side, keep, got, terms):
    shape = jax.ShapeDtypeStruct(got.shape[1:], jnp.float32)
    own = pl.BlockSpec((1, *keep.shape[1:]), lambda *_: (0,) * keep.ndim, pipeline_mode=pl.Buffered(1))
    return call(
        sum_kernel, side, (keep, got, *terms), [own] + [whole(value) for value in (got, *terms)],
        [shape] * 2, [whole(shape)] * 2,
    )


def join_kernel(place, one, other_one, keep, got, across, two, three, other_two, out):
    part = place[2]
    for block in range(4):
        line = place[1] ^ block
        out[place[0], line] = one[block] + other_one[block]
        near = across[block] + (two[block] + three[block])
        out[1 - place[0], line] = (keep[0, part, block] + got[part, block]) + (near + other_two[block])


def join(place, values):
    shape = jax.ShapeDtypeStruct((2, *values[0].shape), jnp.float32)
    return call(join_kernel, place, values, [whole(value) for value in values], shape, whole(shape))


def per_device(left, right):
    rows, depth = left.shape[0], left.shape[1] // 4
    columns = right.shape[1]
    rep, grid = lax.axis_index("rep"), lax.axis_index("grid")
    core, x_hi = rep & 1, rep >> 1
    x_lo, z, y = grid >> 4, (grid >> 2) & 3, grid & 3
    quarter = 2 * (x_lo ^ (y >> 1)) + (x_lo ^ (y >> 1) ^ (y & 1))
    swap = (core ^ (z >> 1)).reshape(1)
    side = (x_hi ^ x_lo).reshape(1)

    def block(d):
        return lax.dynamic_slice(left, (0, (quarter ^ d) * depth), (rows, depth))

    mine = jnp.stack([block(0), send(block(1), dy=1), send(block(3), dy=2), send(block(2), dy=3)])
    other = send(mine, dx=1, dy=2)
    own_one, own_three = send(mine, dz=1), send(mine, dz=3)
    far, *_ = lax.optimization_barrier((other, own_one, own_three))
    far_one, far_three = lax.optimization_barrier((send(far, dz=1), send(far, dz=3)))

    own_two, far_two = send(own_three, dz=1), send(far_one, dz=3)

    pieces = cut_after(quarter.reshape(1), right, other)
    pieces = [pieces[0]] + [send(pieces[d], **NEAR[d]) for d in range(1, 4)]
    rights = split(swap, pieces)

    before = early_products(swap, 0, ((mine,), (own_three,), (own_one,)), rights)
    early = early_products(swap, 1, ((far,), (far_three,), (far_one,)), rights, before)

    keep, third, *gives = early
    got = [send(give, core=1) for give in gives]
    sums = added(swap, keep, got[1:])
    late_keep, late_give, both, here_keep, here_give = late_products(
        jnp.stack([swap[0], core, side[0]]), ((own_two,), (far_two,)), third, rights, sums
    )
    both = lax.all_to_all(both, AXES, 0, 0, tiled=True, axis_index_groups=CORES)

    here, there = summed(side, keep, got[0], [send(sums[d - 1], **NEAR[d]) for d in range(1, 4)])
    early_ends = here, send(there, dhi=1)

    late_got = send(late_give, core=1)
    passed = both_sums(swap, both)
    passed = [send(passed[d - 1], **NEAR[d]) for d in range(1, 4)]
    kept = three_sums(swap, here_keep, send(here_give, core=1))
    passed = send(onward(side, late_keep, late_got, passed, kept), dhi=1)
    kept = [send(kept[d - 1], **NEAR[d]) for d in range(1, 4)]

    place = jnp.stack([(z & 1) ^ swap[0], y ^ (2 * side[0]), side[0]])
    total = join(place, (*early_ends, late_keep, late_got, *kept, passed))
    return total.reshape(8 * rows, columns)


def solution(mesh):
    return jax.shard_map(
        per_device,
        mesh=mesh,
        in_specs=(P("grid", "rep"), P("rep", "grid")),
        out_specs=P("rep", "grid"),
        check_vma=False,
    )
```

```python
import jax
import jax.numpy as jnp
from jax import lax
from jax.experimental import pallas as pl
from jax.experimental.pallas import tpu as pltpu
from jax.sharding import PartitionSpec as P

AXES = ("rep", "grid")
PARAMS = pltpu.CompilerParams(vmem_limit_bytes=20 * 1024 * 1024)
SHORT = pl.CostEstimate(flops=1, bytes_accessed=1, transcendentals=0)
NEAR = (dict(), dict(dx=1), dict(dy=1), dict(dy=3))
DIFFERS = (0, 3, 1, 2)


def number(x_hi, core, x_lo, z, y):
    return (2 * x_hi + core) * 32 + 16 * x_lo + 4 * z + y


def send(value, dhi=0, core=0, dx=0, dz=0, dy=0):
    pairs = [
        (number(h, c, x, z, y), number(h ^ dhi, c ^ core, x ^ dx, z ^ dz, y ^ dy))
        for h in range(2) for c in range(2) for x in range(2) for z in range(4) for y in range(4)
    ]
    return lax.ppermute(value, AXES, pairs)


CORES = [
    [number(h, c, x, z, y) for c in range(2)]
    for h in range(2) for x in range(2) for z in range(4) for y in range(4)
]


def halves(value):
    high = value.astype(jnp.bfloat16)
    return high, (value - high.astype(jnp.float32)).astype(jnp.bfloat16)


def whole(value):
    return pl.BlockSpec(value.shape, lambda *_: (0,) * value.ndim, pipeline_mode=pl.Buffered(1))


ANYWHERE = pl.BlockSpec(memory_space=pl.ANY)
VMEM = pl.BlockSpec(memory_space=pltpu.VMEM)


def call(kernel, scalars, values, in_specs, out_shape, out_specs, scratch=(), aliases=None):
    scalars = scalars if isinstance(scalars, tuple) else (scalars,)
    aliases = {at + len(scalars) - 1: out for at, out in (aliases or {}).items()}
    return pl.pallas_call(
        kernel,
        grid_spec=pltpu.PrefetchScalarGridSpec(
            num_scalar_prefetch=len(scalars), grid=(1,), in_specs=in_specs, out_specs=out_specs, scratch_shapes=scratch
        ),
        out_shape=out_shape,
        input_output_aliases=aliases,
        compiler_params=PARAMS,
        cost_estimate=SHORT,
    )(*scalars, *values)


def cut_kernel(quarter, value, _, *rest):
    outs, sems = rest[:-1], rest[-1]
    depth = outs[0].shape[0]
    copies = []
    for d, out in enumerate(outs):
        at = pl.ds(pl.multiple_of((quarter[0] ^ DIFFERS[d]) * depth, depth), depth)
        copies.append(pltpu.make_async_copy(value.at[at], out, sems.at[d]))
    for copy in copies:
        copy.start()
    for copy in copies:
        copy.wait()


def cut_after(quarter, value, earlier):
    shape = jax.ShapeDtypeStruct((value.shape[0] // 4, value.shape[1]), value.dtype)
    return call(
        cut_kernel, quarter, (value, earlier), [ANYWHERE] * 2, [shape] * 4, [ANYWHERE] * 4,
        [pltpu.SemaphoreType.DMA((4,))],
    )


def split_kernel(_, *refs):
    pieces, (high, low) = refs[:4], refs[4:]
    columns = pieces[0].shape[1]
    for d, piece in enumerate(pieces):
        at = slice(d * columns, (d + 1) * columns)
        high[:, at], low[:, at] = halves(piece[...])


def split(scalars, pieces):
    depth, columns = pieces[0].shape
    shape = pltpu.VMEM((depth, 4 * columns), jnp.bfloat16)
    found = call(split_kernel, scalars, pieces, [whole(piece) for piece in pieces], [shape] * 2, [VMEM] * 2)
    return [pltpu.with_memory_space_constraint(value, pltpu.VMEM) for value in found]


def multiplied(blocks, left_high, left_low, high, low, store):
    depth = left_high.shape[1]
    at = 0
    for block in blocks:
        value = block[...].reshape(block.shape[0] * block.shape[1], depth)
        span = slice(at, at + value.shape[0])
        left_high[span], left_low[span] = halves(value)
        at += value.shape[0]
    columns = high.shape[1] // 4
    for d in range(4):
        span = slice(d * columns, (d + 1) * columns)
        total = jnp.dot(left_high[...], high[:, span], preferred_element_type=jnp.float32)
        total += jnp.dot(left_high[...], low[:, span], preferred_element_type=jnp.float32)
        total += jnp.dot(left_low[...], high[:, span], preferred_element_type=jnp.float32)
        store(d, total.reshape(-1, 4, blocks[0].shape[1], columns))


def places(d):
    return [(block, block ^ (0, 2, 1, 3)[d]) for block in range(4)]


def early_products(swap, part, planes, rights, before=()):
    arrays = [array for plane in planes for array in plane]
    rows, depth = arrays[0].shape[1:]
    columns = rights[0].shape[1] // 4

    def kernel(swap, *refs):
        blocks, rest = refs[: len(arrays)], refs[len(arrays) + len(before):]
        high, low, keep, third, *gives, left_high, left_low = rest
        swapped = swap[0] == 1

        def store(d, total):
            for block, into in places(d):
                zero, one = total[0, block], total[1, block]
                keep[d, 0, into] = jnp.where(swapped, one, zero)
                gives[d][0, into] = jnp.where(swapped, zero, one)
                third[d, 0, into] = total[2, block]

        multiplied(blocks, left_high, left_low, high, low, store)

    kept = jax.ShapeDtypeStruct((4, 2, 4, rows, columns), jnp.float32)
    given = jax.ShapeDtypeStruct((2, 4, rows, columns), jnp.float32)
    once = pl.Buffered(1)
    kept_out = pl.BlockSpec((4, 1, 4, rows, columns), lambda *_: (0, part, 0, 0, 0), pipeline_mode=once)
    given_out = pl.BlockSpec((1, 4, rows, columns), lambda *_: (part, 0, 0, 0), pipeline_mode=once)
    scratch = pltpu.VMEM((12 * rows, depth), jnp.bfloat16)
    first = 1 + len(arrays)
    return call(
        kernel, swap, (*arrays, *before, *rights),
        [whole(array) for array in arrays] + [ANYWHERE] * len(before) + [VMEM] * 2,
        [kept] * 2 + [given] * 4, [kept_out] * 2 + [given_out] * 4, [scratch] * 2,
        {first + at: at for at in range(len(before))},
    )


def added_kernel(_, keep, *refs):
    gots, outs = refs[:len(refs) // 2], refs[len(refs) // 2:]
    for at, (got, out) in enumerate(zip(gots, outs)):
        out[...] = keep[at + 1] + got[...]


def added(scalars, keep, gots):
    shape = jax.ShapeDtypeStruct(gots[0].shape, jnp.float32)
    return call(
        added_kernel, scalars, (keep, *gots), [whole(value) for value in (keep, *gots)], [shape] * 3, [whole(shape)] * 3
    )


def late_products(flags, parts, third, rights, after):
    arrays = [array for part in parts for array in part]
    rows, depth = arrays[0].shape[1:]
    columns = rights[0].shape[1] // 4

    def kernel(swap, at_core, *refs):
        blocks, rest = refs[: len(arrays)], refs[len(arrays) + len(after):]
        high, low, ahead, keep, give, both, left_high, left_low = rest
        swapped, core = swap[0] == 1, at_core[0]

        def store(d, total):
            for part in range(2):
                for block, into in places(d):
                    zero, one = ahead[d, part, into], total[part, block]
                    kept, given = jnp.where(swapped, one, zero), jnp.where(swapped, zero, one)
                    if d == 0:
                        keep[0, part, into], give[part, into] = kept, given
                    else:
                        both[core, d - 1, part, into], both[1 - core, d - 1, part, into] = kept, given

        multiplied(blocks, left_high, left_low, high, low, store)

    piece = (2, 4, rows, columns)
    shapes = [jax.ShapeDtypeStruct(shape, jnp.float32) for shape in ((1, *piece), piece, (2, 3, *piece))]
    scratch = pltpu.VMEM((8 * rows, depth), jnp.bfloat16)
    return call(
        kernel, flags, (*arrays, *after, *rights, third),
        [whole(array) for array in arrays] + [ANYWHERE] * len(after) + [VMEM] * 2 + [whole(third)],
        shapes, [whole(shape) for shape in shapes], [scratch] * 2,
    )


def added_by_core_kernel(side, both, *outs):
    for d, (here, there) in enumerate(zip(outs[:3], outs[3:])):
        here[...] = both[0, d, side[0]] + both[1, d, side[0]]
        there[...] = both[0, d, 1 - side[0]] + both[1, d, 1 - side[0]]


def added_by_core(side, both):
    shape = jax.ShapeDtypeStruct(both.shape[3:], jnp.float32)
    found = call(added_by_core_kernel, side, (both,), [whole(both)], [shape] * 6, [whole(shape)] * 6)
    return found[:3], found[3:]


def onward_kernel(side, keep, got, one, two, three, out):
    part = 1 - side[0]
    out[...] = (keep[0, part] + got[part]) + (one[...] + (two[...] + three[...]))


def onward(side, keep, got, terms):
    shape = jax.ShapeDtypeStruct(got.shape[1:], jnp.float32)
    values = (keep, got, *terms)
    return call(onward_kernel, side, values, [whole(value) for value in values], shape, whole(shape))


def sum_kernel(side, keep, got, *refs):
    terms, (mine, theirs) = refs[:-2], refs[-2:]
    for out, part in ((mine, side[0]), (theirs, 1 - side[0])):
        across = terms[0][1 - part]
        out[...] = (keep[0, part] + got[part]) + (across + (terms[1][part] + terms[2][part]))


def summed(side, keep, got, terms):
    shape = jax.ShapeDtypeStruct(got.shape[1:], jnp.float32)
    own = pl.BlockSpec((1, *keep.shape[1:]), lambda *_: (0,) * keep.ndim, pipeline_mode=pl.Buffered(1))
    return call(
        sum_kernel, side, (keep, got, *terms), [own] + [whole(value) for value in (got, *terms)],
        [shape] * 2, [whole(shape)] * 2,
    )


def join_kernel(plane, first, side, one, other_one, keep, got, across, two, three, other_two, out):
    part = side[0]
    for block in range(4):
        line = first[0] ^ block
        out[plane[0], line] = one[block] + other_one[block]
        near = across[block] + (two[block] + three[block])
        out[1 - plane[0], line] = (keep[0, part, block] + got[part, block]) + (near + other_two[block])


def join(place, values):
    shape = jax.ShapeDtypeStruct((2, *values[0].shape), jnp.float32)
    return call(join_kernel, place, values, [whole(value) for value in values], shape, whole(shape))


def per_device(left, right):
    rows, depth = left.shape[0], left.shape[1] // 4
    columns = right.shape[1]
    rep, grid = lax.axis_index("rep"), lax.axis_index("grid")
    core, x_hi = rep & 1, rep >> 1
    x_lo, z, y = grid >> 4, (grid >> 2) & 3, grid & 3
    quarter = 2 * (x_lo ^ (y >> 1)) + (x_lo ^ (y >> 1) ^ (y & 1))
    swap = (core ^ (z >> 1)).reshape(1)
    side = (x_hi ^ x_lo).reshape(1)

    def block(d):
        return lax.dynamic_slice(left, (0, (quarter ^ d) * depth), (rows, depth))

    mine = jnp.stack([block(0), send(block(1), dy=1), send(block(3), dy=2), send(block(2), dy=3)])
    other = send(mine, dx=1, dy=2)
    own_one, own_three = send(mine, dz=1), send(mine, dz=3)
    far, *_ = lax.optimization_barrier((other, own_one, own_three))
    far_one, far_three = lax.optimization_barrier((send(far, dz=1), send(far, dz=3)))

    own_two, far_two = send(own_three, dz=1), send(far_one, dz=3)

    right = pltpu.with_memory_space_constraint(right, pltpu.HBM)
    pieces = cut_after(quarter.reshape(1), right, other)
    pieces = [pieces[0]] + [send(pieces[d], **NEAR[d]) for d in range(1, 4)]
    rights = split(swap, pieces)

    before = early_products(swap, 0, ((mine,), (own_three,), (own_one,)), rights)
    early = early_products(swap, 1, ((far,), (far_three,), (far_one,)), rights, before)

    keep, third, *gives = early
    got = [send(give, core=1) for give in gives]
    sums = added(swap, keep, got[1:])
    late_keep, late_give, both = late_products(
        (swap, core.reshape(1)), ((own_two,), (far_two,)), third, rights, sums
    )
    both = lax.all_to_all(both, AXES, 0, 0, tiled=True, axis_index_groups=CORES)

    here, there = summed(side, keep, got[0], [send(sums[d - 1], **NEAR[d]) for d in range(1, 4)])
    early_ends = here, send(there, dhi=1)

    late_got = send(late_give, core=1)
    kept, passed = added_by_core(side, both)
    passed = [send(passed[d - 1], **NEAR[d]) for d in range(1, 4)]
    passed = send(onward(side, late_keep, late_got, passed), dhi=1)
    kept = [send(kept[d - 1], **NEAR[d]) for d in range(1, 4)]

    place = ((z & 1) ^ swap[0]).reshape(1), (y ^ (2 * side[0])).reshape(1), side
    total = join(place, (*early_ends, late_keep, late_got, *kept, passed))
    return total.reshape(8 * rows, columns)


def solution(mesh):
    return jax.shard_map(
        per_device,
        mesh=mesh,
        in_specs=(P("grid", "rep"), P("rep", "grid")),
        out_specs=P("rep", "grid"),
        check_vma=False,
    )
```

```python
import jax
import jax.numpy as jnp
from jax import lax
from jax.experimental import pallas as pl
from jax.experimental.pallas import tpu as pltpu
from jax.sharding import PartitionSpec as P

AXES = ("rep", "grid")
PARAMS = pltpu.CompilerParams(vmem_limit_bytes=20 * 1024 * 1024)
SHORT = pl.CostEstimate(flops=1, bytes_accessed=1, transcendentals=0)
NEAR = (dict(), dict(dx=1), dict(dy=1), dict(dy=3))
DIFFERS = (0, 3, 1, 2)


def number(x_hi, core, x_lo, z, y):
    return (2 * x_hi + core) * 32 + 16 * x_lo + 4 * z + y


def send(value, dhi=0, core=0, dx=0, dz=0, dy=0):
    pairs = [
        (number(h, c, x, z, y), number(h ^ dhi, c ^ core, x ^ dx, z ^ dz, y ^ dy))
        for h in range(2) for c in range(2) for x in range(2) for z in range(4) for y in range(4)
    ]
    return lax.ppermute(value, AXES, pairs)


CORES = [
    [number(h, c, x, z, y) for c in range(2)]
    for h in range(2) for x in range(2) for z in range(4) for y in range(4)
]


def halves(value):
    high = value.astype(jnp.bfloat16)
    return high, (value - high.astype(jnp.float32)).astype(jnp.bfloat16)


def whole(value):
    return pl.BlockSpec(value.shape, lambda *_: (0,) * value.ndim, pipeline_mode=pl.Buffered(1))


ANYWHERE = pl.BlockSpec(memory_space=pl.ANY)
VMEM = pl.BlockSpec(memory_space=pltpu.VMEM)


def call(kernel, scalars, values, in_specs, out_shape, out_specs, scratch=(), aliases=None):
    scalars = scalars if isinstance(scalars, tuple) else (scalars,)
    aliases = {at + len(scalars) - 1: out for at, out in (aliases or {}).items()}
    return pl.pallas_call(
        kernel,
        grid_spec=pltpu.PrefetchScalarGridSpec(
            num_scalar_prefetch=len(scalars), grid=(1,), in_specs=in_specs, out_specs=out_specs, scratch_shapes=scratch
        ),
        out_shape=out_shape,
        input_output_aliases=aliases,
        compiler_params=PARAMS,
        cost_estimate=SHORT,
    )(*scalars, *values)


def cut_kernel(quarter, value, _, *rest):
    outs, sems = rest[:-1], rest[-1]
    depth = outs[0].shape[0]
    copies = []
    for d, out in enumerate(outs):
        at = pl.ds(pl.multiple_of((quarter[0] ^ DIFFERS[d]) * depth, depth), depth)
        copies.append(pltpu.make_async_copy(value.at[at], out, sems.at[d]))
    for copy in copies:
        copy.start()
    for copy in copies:
        copy.wait()


def cut_after(quarter, value, earlier):
    shape = jax.ShapeDtypeStruct((value.shape[0] // 4, value.shape[1]), value.dtype)
    return call(
        cut_kernel, quarter, (value, earlier), [ANYWHERE] * 2, [shape] * 4, [ANYWHERE] * 4,
        [pltpu.SemaphoreType.DMA((4,))],
    )


def split_kernel(_, *refs):
    pieces, (high, low) = refs[:4], refs[4:]
    columns = pieces[0].shape[1]
    for d, piece in enumerate(pieces):
        at = slice(d * columns, (d + 1) * columns)
        high[:, at], low[:, at] = halves(piece[...])


def split(scalars, pieces):
    depth, columns = pieces[0].shape
    shape = pltpu.VMEM((depth, 4 * columns), jnp.bfloat16)
    found = call(split_kernel, scalars, pieces, [whole(piece) for piece in pieces], [shape] * 2, [VMEM] * 2)
    return [pltpu.with_memory_space_constraint(value, pltpu.VMEM) for value in found]


def multiplied(blocks, left_high, left_low, high, low, store):
    depth = left_high.shape[1]
    at = 0
    for block in blocks:
        value = block[...].reshape(block.shape[0] * block.shape[1], depth)
        span = slice(at, at + value.shape[0])
        left_high[span], left_low[span] = halves(value)
        at += value.shape[0]
    columns = high.shape[1] // 4
    for d in range(4):
        span = slice(d * columns, (d + 1) * columns)
        total = jnp.dot(left_high[...], high[:, span], preferred_element_type=jnp.float32)
        total += jnp.dot(left_high[...], low[:, span], preferred_element_type=jnp.float32)
        total += jnp.dot(left_low[...], high[:, span], preferred_element_type=jnp.float32)
        store(d, total.reshape(-1, 4, blocks[0].shape[1], columns))


def places(d):
    return [(block, block ^ (0, 2, 1, 3)[d]) for block in range(4)]


def early_products(swap, part, planes, rights, before=()):
    arrays = [array for plane in planes for array in plane]
    rows, depth = arrays[0].shape[1:]
    columns = rights[0].shape[1] // 4

    def kernel(swap, *refs):
        blocks, rest = refs[: len(arrays)], refs[len(arrays) + len(before):]
        high, low, keep, third, *gives, left_high, left_low = rest
        swapped = swap[0] == 1

        def store(d, total):
            for block, into in places(d):
                zero, one = total[0, block], total[1, block]
                keep[d, 0, into] = jnp.where(swapped, one, zero)
                gives[d][0, into] = jnp.where(swapped, zero, one)
                third[d, 0, into] = total[2, block]

        multiplied(blocks, left_high, left_low, high, low, store)

    kept = jax.ShapeDtypeStruct((4, 2, 4, rows, columns), jnp.float32)
    given = jax.ShapeDtypeStruct((2, 4, rows, columns), jnp.float32)
    once = pl.Buffered(1)
    kept_out = pl.BlockSpec((4, 1, 4, rows, columns), lambda *_: (0, part, 0, 0, 0), pipeline_mode=once)
    given_out = pl.BlockSpec((1, 4, rows, columns), lambda *_: (part, 0, 0, 0), pipeline_mode=once)
    scratch = pltpu.VMEM((12 * rows, depth), jnp.bfloat16)
    first = 1 + len(arrays)
    return call(
        kernel, swap, (*arrays, *before, *rights),
        [whole(array) for array in arrays] + [ANYWHERE] * len(before) + [VMEM] * 2,
        [kept] * 2 + [given] * 4, [kept_out] * 2 + [given_out] * 4, [scratch] * 2,
        {first + at: at for at in range(len(before))},
    )


def added_kernel(_, keep, *refs):
    gots, outs = refs[:len(refs) // 2], refs[len(refs) // 2:]
    for at, (got, out) in enumerate(zip(gots, outs)):
        out[...] = keep[at + 1] + got[...]


def added(scalars, keep, gots):
    shape = jax.ShapeDtypeStruct(gots[0].shape, jnp.float32)
    return call(
        added_kernel, scalars, (keep, *gots), [whole(value) for value in (keep, *gots)], [shape] * 3, [whole(shape)] * 3
    )


def late_products(flags, parts, third, rights, after):
    arrays = [array for part in parts for array in part]
    rows, depth = arrays[0].shape[1:]
    columns = rights[0].shape[1] // 4

    def kernel(swap, at_core, *refs):
        blocks, rest = refs[: len(arrays)], refs[len(arrays) + len(after):]
        high, low, ahead, keep, give, both, left_high, left_low = rest
        swapped, core = swap[0] == 1, at_core[0]

        def store(d, total):
            for part in range(2):
                for block, into in places(d):
                    zero, one = ahead[d, part, into], total[part, block]
                    kept, given = jnp.where(swapped, one, zero), jnp.where(swapped, zero, one)
                    if d == 0:
                        keep[0, part, into], give[part, into] = kept, given
                    else:
                        both[core, d - 1, part, into], both[1 - core, d - 1, part, into] = kept, given

        multiplied(blocks, left_high, left_low, high, low, store)

    piece = (2, 4, rows, columns)
    shapes = [jax.ShapeDtypeStruct(shape, jnp.float32) for shape in ((1, *piece), piece, (2, 3, *piece))]
    scratch = pltpu.VMEM((8 * rows, depth), jnp.bfloat16)
    return call(
        kernel, flags, (*arrays, *after, *rights, third),
        [whole(array) for array in arrays] + [ANYWHERE] * len(after) + [VMEM] * 2 + [whole(third)],
        shapes, [whole(shape) for shape in shapes], [scratch] * 2,
    )


def added_by_core_kernel(_, both, *outs):
    for d, out in enumerate(outs):
        out[...] = both[0, d] + both[1, d]


def added_by_core(scalars, both):
    shape = jax.ShapeDtypeStruct(both.shape[2:], jnp.float32)
    return call(added_by_core_kernel, scalars, (both,), [whole(both)], [shape] * 3, [whole(shape)] * 3)


def sum_kernel(side, keep, got, *refs):
    terms, (mine, theirs) = refs[:-2], refs[-2:]
    for out, part in ((mine, side[0]), (theirs, 1 - side[0])):
        across = terms[0][1 - part]
        out[...] = (keep[0, part] + got[part]) + (across + (terms[1][part] + terms[2][part]))


def summed(side, keep, got, terms):
    shape = jax.ShapeDtypeStruct(got.shape[1:], jnp.float32)
    own = pl.BlockSpec((1, *keep.shape[1:]), lambda *_: (0,) * keep.ndim, pipeline_mode=pl.Buffered(1))
    return call(
        sum_kernel, side, (keep, got, *terms), [own] + [whole(value) for value in (got, *terms)],
        [shape] * 2, [whole(shape)] * 2,
    )


def join_kernel(plane, first, one, other_one, two, other_two, out):
    for block in range(4):
        line = first[0] ^ block
        out[plane[0], line] = one[block] + other_one[block]
        out[1 - plane[0], line] = two[block] + other_two[block]


def join(place, values):
    shape = jax.ShapeDtypeStruct((2, *values[0].shape), jnp.float32)
    return call(join_kernel, place, values, [whole(value) for value in values], shape, whole(shape))


def per_device(left, right):
    rows, depth = left.shape[0], left.shape[1] // 4
    columns = right.shape[1]
    rep, grid = lax.axis_index("rep"), lax.axis_index("grid")
    core, x_hi = rep & 1, rep >> 1
    x_lo, z, y = grid >> 4, (grid >> 2) & 3, grid & 3
    quarter = 2 * (x_lo ^ (y >> 1)) + (x_lo ^ (y >> 1) ^ (y & 1))
    swap = (core ^ (z >> 1)).reshape(1)
    side = (x_hi ^ x_lo).reshape(1)

    def block(d):
        return lax.dynamic_slice(left, (0, (quarter ^ d) * depth), (rows, depth))

    mine = jnp.stack([block(0), send(block(1), dy=1), send(block(3), dy=2), send(block(2), dy=3)])
    other = send(mine, dx=1, dy=2)
    own_one, own_three = send(mine, dz=1), send(mine, dz=3)
    far, *_ = lax.optimization_barrier((other, own_one, own_three))
    far_one, far_three = lax.optimization_barrier((send(far, dz=1), send(far, dz=3)))

    own_two, far_two = send(own_three, dz=1), send(far_one, dz=3)

    pieces = cut_after(quarter.reshape(1), right, other)
    pieces = [pieces[0]] + [send(pieces[d], **NEAR[d]) for d in range(1, 4)]
    rights = split(swap, pieces)

    before = early_products(swap, 0, ((mine,), (own_three,), (own_one,)), rights)
    early = early_products(swap, 1, ((far,), (far_three,), (far_one,)), rights, before)

    keep, third, *gives = early
    got = [send(give, core=1) for give in gives]
    sums = added(swap, keep, got[1:])
    late_keep, late_give, both = late_products(
        (swap, core.reshape(1)), ((own_two,), (far_two,)), third, rights, sums
    )
    both = lax.all_to_all(both, AXES, 0, 0, tiled=True, axis_index_groups=CORES)

    ends = []
    for kept, given, terms in ((keep, got[0], sums), (late_keep, send(late_give, core=1), added_by_core(swap, both))):
        here, there = summed(side, kept, given, [send(terms[d - 1], **NEAR[d]) for d in range(1, 4)])
        ends += [here, send(there, dhi=1)]

    total = join((((z & 1) ^ swap[0]).reshape(1), (y ^ (2 * side[0])).reshape(1)), ends)
    return total.reshape(8 * rows, columns)


def solution(mesh):
    return jax.shard_map(
        per_device,
        mesh=mesh,
        in_specs=(P("grid", "rep"), P("rep", "grid")),
        out_specs=P("rep", "grid"),
        check_vma=False,
    )
```

```python
import jax
import jax.numpy as jnp
from jax import lax
from jax.experimental import pallas as pl
from jax.experimental.pallas import tpu as pltpu
from jax.sharding import PartitionSpec as P

AXES = ("rep", "grid")
PARAMS = pltpu.CompilerParams(vmem_limit_bytes=20 * 1024 * 1024)
SHORT = pl.CostEstimate(flops=1, bytes_accessed=1, transcendentals=0)
NEAR = (dict(), dict(dx=1), dict(dy=1), dict(dy=3))
DIFFERS = (0, 3, 1, 2)


def number(x_hi, core, x_lo, z, y):
    return (2 * x_hi + core) * 32 + 16 * x_lo + 4 * z + y


def send(value, dhi=0, core=0, dx=0, dz=0, dy=0):
    pairs = [
        (number(h, c, x, z, y), number(h ^ dhi, c ^ core, x ^ dx, z ^ dz, y ^ dy))
        for h in range(2) for c in range(2) for x in range(2) for z in range(4) for y in range(4)
    ]
    return lax.ppermute(value, AXES, pairs)


CORES = [
    [number(h, c, x, z, y) for c in range(2)]
    for h in range(2) for x in range(2) for z in range(4) for y in range(4)
]


def halves(value):
    high = value.astype(jnp.bfloat16)
    return high, (value - high.astype(jnp.float32)).astype(jnp.bfloat16)


def whole(value):
    return pl.BlockSpec(value.shape, lambda *_: (0,) * value.ndim, pipeline_mode=pl.Buffered(1))


ANYWHERE = pl.BlockSpec(memory_space=pl.ANY)
VMEM = pl.BlockSpec(memory_space=pltpu.VMEM)


def call(kernel, scalars, values, in_specs, out_shape, out_specs, scratch=(), aliases=None):
    scalars = scalars if isinstance(scalars, tuple) else (scalars,)
    aliases = {at + len(scalars) - 1: out for at, out in (aliases or {}).items()}
    return pl.pallas_call(
        kernel,
        grid_spec=pltpu.PrefetchScalarGridSpec(
            num_scalar_prefetch=len(scalars), grid=(1,), in_specs=in_specs, out_specs=out_specs, scratch_shapes=scratch
        ),
        out_shape=out_shape,
        input_output_aliases=aliases,
        compiler_params=PARAMS,
        cost_estimate=SHORT,
    )(*scalars, *values)


def cut_kernel(quarter, value, _, *rest):
    outs, sems = rest[:-1], rest[-1]
    depth = outs[0].shape[0]
    copies = []
    for d, out in enumerate(outs):
        at = pl.ds(pl.multiple_of((quarter[0] ^ DIFFERS[d]) * depth, depth), depth)
        copies.append(pltpu.make_async_copy(value.at[at], out, sems.at[d]))
    for copy in copies:
        copy.start()
    for copy in copies:
        copy.wait()


def cut_after(quarter, value, earlier):
    shape = jax.ShapeDtypeStruct((value.shape[0] // 4, value.shape[1]), value.dtype)
    return call(
        cut_kernel, quarter, (value, earlier), [ANYWHERE] * 2, [shape] * 4, [ANYWHERE] * 4,
        [pltpu.SemaphoreType.DMA((4,))],
    )


def split_kernel(_, *refs):
    *pieces, high, low = refs
    columns = pieces[0].shape[1]
    for d, piece in enumerate(pieces):
        at = slice(d * columns, (d + 1) * columns)
        high[:, at], low[:, at] = halves(piece[...])


def split(scalars, pieces):
    depth, columns = pieces[0].shape
    shape = pltpu.VMEM((depth, len(pieces) * columns), jnp.bfloat16)
    found = call(split_kernel, scalars, pieces, [whole(piece) for piece in pieces], [shape] * 2, [VMEM] * 2)
    return [pltpu.with_memory_space_constraint(value, pltpu.VMEM) for value in found]


def multiplied(blocks, left_high, left_low, rights, store):
    depth = left_high.shape[1]
    at = 0
    for block in blocks:
        value = block[...].reshape(block.shape[0] * block.shape[1], depth)
        span = slice(at, at + value.shape[0])
        left_high[span], left_low[span] = halves(value)
        at += value.shape[0]
    columns = rights[0].shape[1]
    for d in range(4):
        high, low = rights[2 * d][...], rights[2 * d + 1][...]
        total = jnp.dot(left_high[...], high, preferred_element_type=jnp.float32)
        total += jnp.dot(left_high[...], low, preferred_element_type=jnp.float32)
        total += jnp.dot(left_low[...], high, preferred_element_type=jnp.float32)
        store(d, total.reshape(-1, 4, blocks[0].shape[1], columns))


def places(d):
    return [(block, block ^ (0, 2, 1, 3)[d]) for block in range(4)]


def early_products(swap, part, planes, rights, before=()):
    arrays = [array for plane in planes for array in plane]
    rows, depth = arrays[0].shape[1:]
    columns = rights[0].shape[1]

    def kernel(swap, *refs):
        blocks, rest = refs[: len(arrays)], refs[len(arrays) + len(before):]
        *rights, keep, third, one_give, two_give, three_give, four_give, left_high, left_low = rest
        gives = one_give, two_give, three_give, four_give
        swapped = swap[0] == 1

        def store(d, total):
            for block, into in places(d):
                zero, one = total[0, block], total[1, block]
                keep[d, 0, into] = jnp.where(swapped, one, zero)
                gives[d][0, into] = jnp.where(swapped, zero, one)
                third[d, 0, into] = total[2, block]

        multiplied(blocks, left_high, left_low, rights, store)

    kept = jax.ShapeDtypeStruct((4, 2, 4, rows, columns), jnp.float32)
    given = jax.ShapeDtypeStruct((2, 4, rows, columns), jnp.float32)
    once = pl.Buffered(1)
    kept_out = pl.BlockSpec((4, 1, 4, rows, columns), lambda *_: (0, part, 0, 0, 0), pipeline_mode=once)
    given_out = pl.BlockSpec((1, 4, rows, columns), lambda *_: (part, 0, 0, 0), pipeline_mode=once)
    scratch = pltpu.VMEM((12 * rows, depth), jnp.bfloat16)
    first = 1 + len(arrays)
    return call(
        kernel, swap, (*arrays, *before, *rights),
        [whole(array) for array in arrays] + [ANYWHERE] * len(before) + [VMEM] * 8,
        [kept] * 2 + [given] * 4, [kept_out] * 2 + [given_out] * 4, [scratch] * 2,
        {first + at: at for at in range(len(before))},
    )


def added_kernel(_, keep, *refs):
    gots, outs = refs[:len(refs) // 2], refs[len(refs) // 2:]
    for at, (got, out) in enumerate(zip(gots, outs)):
        out[...] = keep[at + 1] + got[...]


def added(scalars, keep, gots):
    shape = jax.ShapeDtypeStruct(gots[0].shape, jnp.float32)
    return call(
        added_kernel, scalars, (keep, *gots), [whole(value) for value in (keep, *gots)], [shape] * 3, [whole(shape)] * 3
    )


def late_products(flags, parts, third, rights, after):
    arrays = [array for part in parts for array in part]
    rows, depth = arrays[0].shape[1:]
    columns = rights[0].shape[1]

    def kernel(swap, at_core, *refs):
        blocks, rest = refs[: len(arrays)], refs[len(arrays) + len(after):]
        *rights, ahead, keep, give, both, left_high, left_low = rest
        swapped, core = swap[0] == 1, at_core[0]

        def store(d, total):
            for part in range(2):
                for block, into in places(d):
                    zero, one = ahead[d, part, into], total[part, block]
                    kept, given = jnp.where(swapped, one, zero), jnp.where(swapped, zero, one)
                    if d == 0:
                        keep[0, part, into], give[part, into] = kept, given
                    else:
                        both[core, d - 1, part, into], both[1 - core, d - 1, part, into] = kept, given

        multiplied(blocks, left_high, left_low, rights, store)

    piece = (2, 4, rows, columns)
    shapes = [jax.ShapeDtypeStruct(shape, jnp.float32) for shape in ((1, *piece), piece, (2, 3, *piece))]
    scratch = pltpu.VMEM((8 * rows, depth), jnp.bfloat16)
    return call(
        kernel, flags, (*arrays, *after, *rights, third),
        [whole(array) for array in arrays] + [ANYWHERE] * len(after) + [VMEM] * 8 + [whole(third)],
        shapes, [whole(shape) for shape in shapes], [scratch] * 2,
    )


def added_by_core_kernel(_, both, *outs):
    for d, out in enumerate(outs):
        out[...] = both[0, d] + both[1, d]


def added_by_core(scalars, both):
    shape = jax.ShapeDtypeStruct(both.shape[2:], jnp.float32)
    return call(added_by_core_kernel, scalars, (both,), [whole(both)], [shape] * 3, [whole(shape)] * 3)


def sum_kernel(side, keep, got, *refs):
    terms, (mine, theirs) = refs[:-2], refs[-2:]
    for out, part in ((mine, side[0]), (theirs, 1 - side[0])):
        across = terms[0][1 - part]
        out[...] = (keep[0, part] + got[part]) + (across + (terms[1][part] + terms[2][part]))


def summed(side, keep, got, terms):
    shape = jax.ShapeDtypeStruct(got.shape[1:], jnp.float32)
    own = pl.BlockSpec((1, *keep.shape[1:]), lambda *_: (0,) * keep.ndim, pipeline_mode=pl.Buffered(1))
    return call(
        sum_kernel, side, (keep, got, *terms), [own] + [whole(value) for value in (got, *terms)],
        [shape] * 2, [whole(shape)] * 2,
    )


def join_kernel(plane, first, one, other_one, two, other_two, out):
    for block in range(4):
        line = first[0] ^ block
        out[plane[0], line] = one[block] + other_one[block]
        out[1 - plane[0], line] = two[block] + other_two[block]


def join(place, values):
    shape = jax.ShapeDtypeStruct((2, *values[0].shape), jnp.float32)
    return call(join_kernel, place, values, [whole(value) for value in values], shape, whole(shape))


def per_device(left, right):
    rows, depth = left.shape[0], left.shape[1] // 4
    columns = right.shape[1]
    rep, grid = lax.axis_index("rep"), lax.axis_index("grid")
    core, x_hi = rep & 1, rep >> 1
    x_lo, z, y = grid >> 4, (grid >> 2) & 3, grid & 3
    quarter = 2 * (x_lo ^ (y >> 1)) + (x_lo ^ (y >> 1) ^ (y & 1))
    swap = (core ^ (z >> 1)).reshape(1)
    side = (x_hi ^ x_lo).reshape(1)

    def block(d):
        return lax.dynamic_slice(left, (0, (quarter ^ d) * depth), (rows, depth))

    mine = jnp.stack([block(0), send(block(1), dy=1), send(block(3), dy=2), send(block(2), dy=3)])
    other = send(mine, dx=1, dy=2)
    own_one, own_three = send(mine, dz=1), send(mine, dz=3)
    far, *_ = lax.optimization_barrier((other, own_one, own_three))
    far_one, far_three = lax.optimization_barrier((send(far, dz=1), send(far, dz=3)))

    own_two, far_two = send(own_three, dz=1), send(far_one, dz=3)

    pieces = cut_after(quarter.reshape(1), right, other)
    pieces = [pieces[0]] + [send(pieces[d], **NEAR[d]) for d in range(1, 4)]
    rights = [half for piece in pieces for half in split(swap, [piece])]

    before = early_products(swap, 0, ((mine,), (own_three,), (own_one,)), rights)
    early = early_products(swap, 1, ((far,), (far_three,), (far_one,)), rights, before)

    keep, third, *gives = early
    got = [send(give, core=1) for give in gives]
    sums = added(swap, keep, got[1:])
    late_keep, late_give, both = late_products(
        (swap, core.reshape(1)), ((own_two,), (far_two,)), third, rights, sums
    )
    both = lax.all_to_all(both, AXES, 0, 0, tiled=True, axis_index_groups=CORES)

    ends = []
    for kept, given, terms in ((keep, got[0], sums), (late_keep, send(late_give, core=1), added_by_core(swap, both))):
        here, there = summed(side, kept, given, [send(terms[d - 1], **NEAR[d]) for d in range(1, 4)])
        ends += [here, send(there, dhi=1)]

    total = join((((z & 1) ^ swap[0]).reshape(1), (y ^ (2 * side[0])).reshape(1)), ends)
    return total.reshape(8 * rows, columns)


def solution(mesh):
    return jax.shard_map(
        per_device,
        mesh=mesh,
        in_specs=(P("grid", "rep"), P("rep", "grid")),
        out_specs=P("rep", "grid"),
        check_vma=False,
    )
```

```python
import jax
import jax.numpy as jnp
from jax import lax
from jax.experimental import pallas as pl
from jax.experimental.pallas import tpu as pltpu
from jax.sharding import PartitionSpec as P

AXES = ("rep", "grid")
PARAMS = pltpu.CompilerParams(vmem_limit_bytes=20 * 1024 * 1024)
SHORT = pl.CostEstimate(flops=1, bytes_accessed=1, transcendentals=0)
NEAR = (dict(), dict(dx=1), dict(dy=1), dict(dy=3))
DIFFERS = (0, 3, 1, 2)


def number(x_hi, core, x_lo, z, y):
    return (2 * x_hi + core) * 32 + 16 * x_lo + 4 * z + y


def send(value, dhi=0, core=0, dx=0, dz=0, dy=0):
    pairs = [
        (number(h, c, x, z, y), number(h ^ dhi, c ^ core, x ^ dx, z ^ dz, y ^ dy))
        for h in range(2) for c in range(2) for x in range(2) for z in range(4) for y in range(4)
    ]
    return lax.ppermute(value, AXES, pairs)


CORES = [
    [number(h, c, x, z, y) for c in range(2)]
    for h in range(2) for x in range(2) for z in range(4) for y in range(4)
]


def halves(value):
    high = value.astype(jnp.bfloat16)
    return high, (value - high.astype(jnp.float32)).astype(jnp.bfloat16)


def whole(value):
    return pl.BlockSpec(value.shape, lambda *_: (0,) * value.ndim, pipeline_mode=pl.Buffered(1))


ANYWHERE = pl.BlockSpec(memory_space=pl.ANY)
VMEM = pl.BlockSpec(memory_space=pltpu.VMEM)


def call(kernel, scalars, values, in_specs, out_shape, out_specs, scratch=(), aliases=None):
    scalars = scalars if isinstance(scalars, tuple) else (scalars,)
    aliases = {at + len(scalars) - 1: out for at, out in (aliases or {}).items()}
    return pl.pallas_call(
        kernel,
        grid_spec=pltpu.PrefetchScalarGridSpec(
            num_scalar_prefetch=len(scalars), grid=(1,), in_specs=in_specs, out_specs=out_specs, scratch_shapes=scratch
        ),
        out_shape=out_shape,
        input_output_aliases=aliases,
        compiler_params=PARAMS,
        cost_estimate=SHORT,
    )(*scalars, *values)


def cut_kernel(quarter, value, _, *rest):
    outs, sems = rest[:-1], rest[-1]
    depth = outs[0].shape[0]
    copies = []
    for d, out in enumerate(outs):
        at = pl.ds(pl.multiple_of((quarter[0] ^ DIFFERS[d]) * depth, depth), depth)
        copies.append(pltpu.make_async_copy(value.at[at], out, sems.at[d]))
    for copy in copies:
        copy.start()
    for copy in copies:
        copy.wait()


def cut_after(quarter, value, earlier):
    shape = jax.ShapeDtypeStruct((value.shape[0] // 4, value.shape[1]), value.dtype)
    return call(
        cut_kernel, quarter, (value, earlier), [ANYWHERE] * 2, [shape] * 4, [ANYWHERE] * 4,
        [pltpu.SemaphoreType.DMA((4,))],
    )


def split_kernel(_, *refs):
    *pieces, high, low = refs
    columns = pieces[0].shape[1]
    for d, piece in enumerate(pieces):
        at = slice(d * columns, (d + 1) * columns)
        high[:, at], low[:, at] = halves(piece[...])


def split(scalars, pieces):
    depth, columns = pieces[0].shape
    shape = pltpu.VMEM((depth, len(pieces) * columns), jnp.bfloat16)
    found = call(split_kernel, scalars, pieces, [whole(piece) for piece in pieces], [shape] * 2, [VMEM] * 2)
    return [pltpu.with_memory_space_constraint(value, pltpu.VMEM) for value in found]


def multiplied(blocks, left_high, left_low, rights, store):
    depth = left_high.shape[1]
    at = 0
    for block in blocks:
        value = block[...].reshape(block.shape[0] * block.shape[1], depth)
        span = slice(at, at + value.shape[0])
        left_high[span], left_low[span] = halves(value)
        at += value.shape[0]
    columns = rights[0].shape[1]
    for d in range(4):
        high, low = rights[2 * d][...], rights[2 * d + 1][...]
        total = jnp.dot(left_high[...], high, preferred_element_type=jnp.float32)
        total += jnp.dot(left_high[...], low, preferred_element_type=jnp.float32)
        total += jnp.dot(left_low[...], high, preferred_element_type=jnp.float32)
        store(d, total.reshape(-1, 4, blocks[0].shape[1], columns))


def places(d):
    return [(block, block ^ (0, 2, 1, 3)[d]) for block in range(4)]


def early_products(swap, part, planes, rights, before=()):
    arrays = [array for plane in planes for array in plane]
    rows, depth = arrays[0].shape[1:]
    columns = rights[0].shape[1]

    def kernel(swap, *refs):
        blocks, rest = refs[: len(arrays)], refs[len(arrays) + len(before):]
        *rights, keep, third, one_give, two_give, three_give, four_give, left_high, left_low = rest
        gives = one_give, two_give, three_give, four_give
        swapped = swap[0] == 1

        def store(d, total):
            for block, into in places(d):
                zero, one = total[0, block], total[1, block]
                keep[d, 0, into] = jnp.where(swapped, one, zero)
                gives[d][0, into] = jnp.where(swapped, zero, one)
                third[d, 0, into] = total[2, block]

        multiplied(blocks, left_high, left_low, rights, store)

    kept = jax.ShapeDtypeStruct((4, 2, 4, rows, columns), jnp.float32)
    given = jax.ShapeDtypeStruct((2, 4, rows, columns), jnp.float32)
    once = pl.Buffered(1)
    kept_out = pl.BlockSpec((4, 1, 4, rows, columns), lambda *_: (0, part, 0, 0, 0), pipeline_mode=once)
    given_out = pl.BlockSpec((1, 4, rows, columns), lambda *_: (part, 0, 0, 0), pipeline_mode=once)
    scratch = pltpu.VMEM((12 * rows, depth), jnp.bfloat16)
    first = 1 + len(arrays)
    return call(
        kernel, swap, (*arrays, *before, *rights),
        [whole(array) for array in arrays] + [ANYWHERE] * len(before) + [VMEM] * 8,
        [kept] * 2 + [given] * 4, [kept_out] * 2 + [given_out] * 4, [scratch] * 2,
        {first + at: at for at in range(len(before))},
    )


def added_kernel(_, keep, *refs):
    gots, outs = refs[:len(refs) // 2], refs[len(refs) // 2:]
    for at, (got, out) in enumerate(zip(gots, outs)):
        out[...] = keep[at + 1] + got[...]


def added(scalars, keep, gots):
    shape = jax.ShapeDtypeStruct(gots[0].shape, jnp.float32)
    return call(
        added_kernel, scalars, (keep, *gots), [whole(value) for value in (keep, *gots)], [shape] * 3, [whole(shape)] * 3
    )


def late_products(flags, parts, third, rights, after):
    arrays = [array for part in parts for array in part]
    rows, depth = arrays[0].shape[1:]
    columns = rights[0].shape[1]

    def kernel(swap, at_core, *refs):
        blocks, rest = refs[: len(arrays)], refs[len(arrays) + len(after):]
        *rights, ahead, keep, give, both, left_high, left_low = rest
        swapped, core = swap[0] == 1, at_core[0]

        def store(d, total):
            for part in range(2):
                for block, into in places(d):
                    zero, one = ahead[d, part, into], total[part, block]
                    kept, given = jnp.where(swapped, one, zero), jnp.where(swapped, zero, one)
                    if d == 0:
                        keep[0, part, into], give[part, into] = kept, given
                    else:
                        both[core, d - 1, part, into], both[1 - core, d - 1, part, into] = kept, given

        multiplied(blocks, left_high, left_low, rights, store)

    piece = (2, 4, rows, columns)
    shapes = [jax.ShapeDtypeStruct(shape, jnp.float32) for shape in ((1, *piece), piece, (2, 3, *piece))]
    scratch = pltpu.VMEM((8 * rows, depth), jnp.bfloat16)
    return call(
        kernel, flags, (*arrays, *after, *rights, third),
        [whole(array) for array in arrays] + [ANYWHERE] * len(after) + [VMEM] * 8 + [whole(third)],
        shapes, [whole(shape) for shape in shapes], [scratch] * 2,
    )


def added_by_core_kernel(_, both, *outs):
    for d, out in enumerate(outs):
        out[...] = both[0, d] + both[1, d]


def added_by_core(scalars, both):
    shape = jax.ShapeDtypeStruct(both.shape[2:], jnp.float32)
    return call(added_by_core_kernel, scalars, (both,), [whole(both)], [shape] * 3, [whole(shape)] * 3)


def sum_kernel(side, keep, got, *refs):
    terms, (mine, theirs) = refs[:-2], refs[-2:]
    for out, part in ((mine, side[0]), (theirs, 1 - side[0])):
        across = terms[0][1 - part]
        out[...] = (keep[0, part] + got[part]) + (across + (terms[1][part] + terms[2][part]))


def summed(side, keep, got, terms):
    shape = jax.ShapeDtypeStruct(got.shape[1:], jnp.float32)
    own = pl.BlockSpec((1, *keep.shape[1:]), lambda *_: (0,) * keep.ndim, pipeline_mode=pl.Buffered(1))
    return call(
        sum_kernel, side, (keep, got, *terms), [own] + [whole(value) for value in (got, *terms)],
        [shape] * 2, [whole(shape)] * 2,
    )


def part_specs(keep, got, terms, which):
    once = pl.Buffered(1)

    def of(value, flip):
        return pl.BlockSpec((1, *value.shape[1:]), lambda i, *scalars: (which(*scalars) ^ flip, 0, 0, 0), pipeline_mode=once)

    first = pl.BlockSpec((1, 1, *keep.shape[2:]), lambda i, *scalars: (0, which(*scalars), 0, 0, 0), pipeline_mode=once)
    return [first, of(got, 0)] + [of(term, at == 0) for at, term in enumerate(terms)]


def onward_kernel(_, keep, got, across, two, three, out):
    out[...] = (keep[0, 0] + got[0]) + (across[0] + (two[0] + three[0]))


def onward(side, keep, got, terms):
    shape = jax.ShapeDtypeStruct(got.shape[1:], jnp.float32)
    specs = part_specs(keep, got, terms, lambda side: 1 - side[0])
    return call(onward_kernel, side, (keep, got, *terms), specs, shape, whole(shape))


def join_kernel(plane, first, _, one, other_one, keep, got, across, two, three, other_two, out):
    for block in range(4):
        line = first[0] ^ block
        out[plane[0], line] = one[block] + other_one[block]
        near = across[0, block] + (two[0, block] + three[0, block])
        out[1 - plane[0], line] = (keep[0, 0, block] + got[0, block]) + (near + other_two[block])


def join(scalars, early, keep, got, terms, other):
    shape = jax.ShapeDtypeStruct((2, *early[0].shape), jnp.float32)
    specs = part_specs(keep, got, terms, lambda plane, first, side: side[0])
    return call(
        join_kernel, scalars, (*early, keep, got, *terms, other),
        [whole(value) for value in early] + specs + [whole(other)], shape, whole(shape),
    )


def per_device(left, right):
    rows, depth = left.shape[0], left.shape[1] // 4
    columns = right.shape[1]
    rep, grid = lax.axis_index("rep"), lax.axis_index("grid")
    core, x_hi = rep & 1, rep >> 1
    x_lo, z, y = grid >> 4, (grid >> 2) & 3, grid & 3
    quarter = 2 * (x_lo ^ (y >> 1)) + (x_lo ^ (y >> 1) ^ (y & 1))
    swap = (core ^ (z >> 1)).reshape(1)
    side = (x_hi ^ x_lo).reshape(1)

    def block(d):
        return lax.dynamic_slice(left, (0, (quarter ^ d) * depth), (rows, depth))

    mine = jnp.stack([block(0), send(block(1), dy=1), send(block(3), dy=2), send(block(2), dy=3)])
    other = send(mine, dx=1, dy=2)
    own_one, own_three = send(mine, dz=1), send(mine, dz=3)
    pieces = cut_after(quarter.reshape(1), right, other)
    far, *_ = lax.optimization_barrier((other, own_one, own_three, *pieces))
    far_one, far_three = lax.optimization_barrier((send(far, dz=1), send(far, dz=3)))

    own_two, far_two = send(own_three, dz=1), send(far_one, dz=3)

    pieces = [pieces[0]] + [send(pieces[d], **NEAR[d]) for d in range(1, 4)]
    rights = [half for piece in pieces for half in split(swap, [piece])]

    before = early_products(swap, 0, ((mine,), (own_three,), (own_one,)), rights)
    early = early_products(swap, 1, ((far,), (far_three,), (far_one,)), rights, before)

    keep, third, *gives = early
    got = [send(give, core=1) for give in gives]
    sums = added(swap, keep, got[1:])
    late_keep, late_give, both = late_products(
        (swap, core.reshape(1)), ((own_two,), (far_two,)), third, rights, sums
    )
    both = lax.all_to_all(both, AXES, 0, 0, tiled=True, axis_index_groups=CORES)

    here, there = summed(side, keep, got[0], [send(sums[d - 1], **NEAR[d]) for d in range(1, 4)])
    early_ends = here, send(there, dhi=1)

    late_got, late_sums = send(late_give, core=1), added_by_core(swap, both)
    terms = [send(late_sums[d - 1], **NEAR[d]) for d in range(1, 4)]
    passed = send(onward(side, late_keep, late_got, terms), dhi=1)

    scalars = ((z & 1) ^ swap[0]).reshape(1), (y ^ (2 * side[0])).reshape(1), side
    total = join(scalars, early_ends, late_keep, late_got, terms, passed)
    return total.reshape(8 * rows, columns)


def solution(mesh):
    return jax.shard_map(
        per_device,
        mesh=mesh,
        in_specs=(P("grid", "rep"), P("rep", "grid")),
        out_specs=P("rep", "grid"),
        check_vma=False,
    )
```

```python
import jax
import jax.numpy as jnp
from jax import lax
from jax.experimental import pallas as pl
from jax.experimental.pallas import tpu as pltpu
from jax.sharding import PartitionSpec as P

AXES = ("rep", "grid")
PARAMS = pltpu.CompilerParams(vmem_limit_bytes=15 * 1024 * 1024)
SHORT = pl.CostEstimate(flops=1, bytes_accessed=1, transcendentals=0)
NEAR = (dict(), dict(dx=1), dict(dy=1), dict(dy=3))
DIFFERS = (0, 3, 1, 2)


def number(x_hi, core, x_lo, z, y):
    return (2 * x_hi + core) * 32 + 16 * x_lo + 4 * z + y


def send(value, dhi=0, core=0, dx=0, dz=0, dy=0):
    pairs = [
        (number(h, c, x, z, y), number(h ^ dhi, c ^ core, x ^ dx, z ^ dz, y ^ dy))
        for h in range(2) for c in range(2) for x in range(2) for z in range(4) for y in range(4)
    ]
    return lax.ppermute(value, AXES, pairs)


CORES = [
    [number(h, c, x, z, y) for c in range(2)]
    for h in range(2) for x in range(2) for z in range(4) for y in range(4)
]


def halves(value):
    high = value.astype(jnp.bfloat16)
    return high, (value - high.astype(jnp.float32)).astype(jnp.bfloat16)


def whole(value):
    return pl.BlockSpec(value.shape, lambda *_: (0,) * value.ndim, pipeline_mode=pl.Buffered(1))


ANYWHERE = pl.BlockSpec(memory_space=pl.ANY)
VMEM = pl.BlockSpec(memory_space=pltpu.VMEM)


def call(kernel, scalars, values, in_specs, out_shape, out_specs, scratch=(), aliases=None):
    scalars = scalars if isinstance(scalars, tuple) else (scalars,)
    aliases = {at + len(scalars) - 1: out for at, out in (aliases or {}).items()}
    return pl.pallas_call(
        kernel,
        grid_spec=pltpu.PrefetchScalarGridSpec(
            num_scalar_prefetch=len(scalars), grid=(1,), in_specs=in_specs, out_specs=out_specs, scratch_shapes=scratch
        ),
        out_shape=out_shape,
        input_output_aliases=aliases,
        compiler_params=PARAMS,
        cost_estimate=SHORT,
    )(*scalars, *values)


def cut_kernel(quarter, value, _, *rest):
    outs, sems = rest[:-1], rest[-1]
    depth = outs[0].shape[0]
    copies = []
    for d, out in enumerate(outs):
        at = pl.ds(pl.multiple_of((quarter[0] ^ DIFFERS[d]) * depth, depth), depth)
        copies.append(pltpu.make_async_copy(value.at[at], out, sems.at[d]))
    for copy in copies:
        copy.start()
    for copy in copies:
        copy.wait()


def cut_after(quarter, value, earlier):
    shape = jax.ShapeDtypeStruct((value.shape[0] // 4, value.shape[1]), value.dtype)
    return call(
        cut_kernel, quarter, (value, earlier), [ANYWHERE] * 2, [shape] * 4, [ANYWHERE] * 4,
        [pltpu.SemaphoreType.DMA((4,))],
    )


def split_kernel(_, *refs):
    *pieces, high, low = refs
    columns = pieces[0].shape[1]
    for d, piece in enumerate(pieces):
        at = slice(d * columns, (d + 1) * columns)
        high[:, at], low[:, at] = halves(piece[...])


def split(scalars, pieces):
    depth, columns = pieces[0].shape
    shape = pltpu.VMEM((depth, len(pieces) * columns), jnp.bfloat16)
    found = call(split_kernel, scalars, pieces, [whole(piece) for piece in pieces], [shape] * 2, [VMEM] * 2)
    return [pltpu.with_memory_space_constraint(value, pltpu.VMEM) for value in found]


def multiplied(blocks, left_high, left_low, rights, store):
    depth = left_high.shape[1]
    at = 0
    for block in blocks:
        value = block[...].reshape(block.shape[0] * block.shape[1], depth)
        span = slice(at, at + value.shape[0])
        left_high[span], left_low[span] = halves(value)
        at += value.shape[0]
    columns = rights[0].shape[1]
    for d in range(4):
        high, low = rights[2 * d][...], rights[2 * d + 1][...]
        total = jnp.dot(left_high[...], high, preferred_element_type=jnp.float32)
        total += jnp.dot(left_high[...], low, preferred_element_type=jnp.float32)
        total += jnp.dot(left_low[...], high, preferred_element_type=jnp.float32)
        store(d, total.reshape(-1, 4, blocks[0].shape[1], columns))


def places(d):
    return [(block, block ^ (0, 2, 1, 3)[d]) for block in range(4)]


def early_products(swap, part, planes, rights, before=()):
    arrays = [array for plane in planes for array in plane]
    rows, depth = arrays[0].shape[1:]
    columns = rights[0].shape[1]

    def kernel(swap, *refs):
        blocks, rest = refs[: len(arrays)], refs[len(arrays) + len(before):]
        *rights, keep, third, one_give, two_give, three_give, four_give, left_high, left_low = rest
        gives = one_give, two_give, three_give, four_give
        swapped = swap[0] == 1

        def store(d, total):
            for block, into in places(d):
                zero, one = total[0, block], total[1, block]
                keep[d, 0, into] = jnp.where(swapped, one, zero)
                gives[d][0, into] = jnp.where(swapped, zero, one)
                third[d, 0, into] = total[2, block]

        multiplied(blocks, left_high, left_low, rights, store)

    kept = jax.ShapeDtypeStruct((4, 2, 4, rows, columns), jnp.float32)
    given = jax.ShapeDtypeStruct((2, 4, rows, columns), jnp.float32)
    once = pl.Buffered(1)
    kept_out = pl.BlockSpec((4, 1, 4, rows, columns), lambda *_: (0, part, 0, 0, 0), pipeline_mode=once)
    given_out = pl.BlockSpec((1, 4, rows, columns), lambda *_: (part, 0, 0, 0), pipeline_mode=once)
    scratch = pltpu.VMEM((12 * rows, depth), jnp.bfloat16)
    first = 1 + len(arrays)
    return call(
        kernel, swap, (*arrays, *before, *rights),
        [whole(array) for array in arrays] + [ANYWHERE] * len(before) + [VMEM] * 8,
        [kept] * 2 + [given] * 4, [kept_out] * 2 + [given_out] * 4, [scratch] * 2,
        {first + at: at for at in range(len(before))},
    )


def added_kernel(_, keep, *refs):
    gots, outs = refs[:len(refs) // 2], refs[len(refs) // 2:]
    for at, (got, out) in enumerate(zip(gots, outs)):
        out[...] = keep[at + 1] + got[...]


def added(scalars, keep, gots):
    shape = jax.ShapeDtypeStruct(gots[0].shape, jnp.float32)
    return call(
        added_kernel, scalars, (keep, *gots), [whole(value) for value in (keep, *gots)], [shape] * 3, [whole(shape)] * 3
    )


def late_products(flags, parts, third, rights, after):
    arrays = [array for part in parts for array in part]
    rows, depth = arrays[0].shape[1:]
    columns = rights[0].shape[1]

    def kernel(swap, at_core, *refs):
        blocks, rest = refs[: len(arrays)], refs[len(arrays) + len(after):]
        *rights, ahead, keep, give, both, left_high, left_low = rest
        swapped, core = swap[0] == 1, at_core[0]

        def store(d, total):
            for part in range(2):
                for block, into in places(d):
                    zero, one = ahead[d, part, into], total[part, block]
                    kept, given = jnp.where(swapped, one, zero), jnp.where(swapped, zero, one)
                    if d == 0:
                        keep[0, part, into], give[part, into] = kept, given
                    else:
                        both[core, d - 1, part, into], both[1 - core, d - 1, part, into] = kept, given

        multiplied(blocks, left_high, left_low, rights, store)

    piece = (2, 4, rows, columns)
    shapes = [jax.ShapeDtypeStruct(shape, jnp.float32) for shape in ((1, *piece), piece, (2, 3, *piece))]
    scratch = pltpu.VMEM((8 * rows, depth), jnp.bfloat16)
    return call(
        kernel, flags, (*arrays, *after, *rights, third),
        [whole(array) for array in arrays] + [ANYWHERE] * len(after) + [VMEM] * 8 + [whole(third)],
        shapes, [whole(shape) for shape in shapes], [scratch] * 2,
    )


def added_by_core_kernel(_, both, *outs):
    for d, out in enumerate(outs):
        out[...] = both[0, d] + both[1, d]


def added_by_core(scalars, both):
    shape = jax.ShapeDtypeStruct(both.shape[2:], jnp.float32)
    return call(added_by_core_kernel, scalars, (both,), [whole(both)], [shape] * 3, [whole(shape)] * 3)


def sum_kernel(side, keep, got, *refs):
    terms, (mine, theirs) = refs[:-2], refs[-2:]
    for out, part in ((mine, side[0]), (theirs, 1 - side[0])):
        across = terms[0][1 - part]
        out[...] = (keep[0, part] + got[part]) + (across + (terms[1][part] + terms[2][part]))


def summed(side, keep, got, terms):
    shape = jax.ShapeDtypeStruct(got.shape[1:], jnp.float32)
    own = pl.BlockSpec((1, *keep.shape[1:]), lambda *_: (0,) * keep.ndim, pipeline_mode=pl.Buffered(1))
    return call(
        sum_kernel, side, (keep, got, *terms), [own] + [whole(value) for value in (got, *terms)],
        [shape] * 2, [whole(shape)] * 2,
    )


def join_kernel(plane, first, one, other_one, two, other_two, out):
    for block in range(4):
        line = first[0] ^ block
        out[plane[0], line] = one[block] + other_one[block]
        out[1 - plane[0], line] = two[block] + other_two[block]


def join(place, values):
    shape = jax.ShapeDtypeStruct((2, *values[0].shape), jnp.float32)
    return call(join_kernel, place, values, [whole(value) for value in values], shape, whole(shape))


def per_device(left, right):
    rows, depth = left.shape[0], left.shape[1] // 4
    columns = right.shape[1]
    rep, grid = lax.axis_index("rep"), lax.axis_index("grid")
    core, x_hi = rep & 1, rep >> 1
    x_lo, z, y = grid >> 4, (grid >> 2) & 3, grid & 3
    quarter = 2 * (x_lo ^ (y >> 1)) + (x_lo ^ (y >> 1) ^ (y & 1))
    swap = (core ^ (z >> 1)).reshape(1)
    side = (x_hi ^ x_lo).reshape(1)

    def block(d):
        return lax.dynamic_slice(left, (0, (quarter ^ d) * depth), (rows, depth))

    mine = jnp.stack([block(0), send(block(1), dy=1), send(block(3), dy=2), send(block(2), dy=3)])
    other = send(mine, dx=1, dy=2)
    own_one, own_three = send(mine, dz=1), send(mine, dz=3)
    far, *_ = lax.optimization_barrier((other, own_one, own_three))
    far_one, far_three = lax.optimization_barrier((send(far, dz=1), send(far, dz=3)))

    own_two, far_two = send(own_three, dz=1), send(far_one, dz=3)

    pieces = cut_after(quarter.reshape(1), right, other)
    pieces = [pieces[0]] + [send(pieces[d], **NEAR[d]) for d in range(1, 4)]
    rights = [half for piece in pieces for half in split(swap, [piece])]

    before = early_products(swap, 0, ((mine,), (own_three,), (own_one,)), rights)
    early = early_products(swap, 1, ((far,), (far_three,), (far_one,)), rights, before)

    keep, third, *gives = early
    got = [send(give, core=1) for give in gives]
    sums = added(swap, keep, got[1:])
    late_keep, late_give, both = late_products(
        (swap, core.reshape(1)), ((own_two,), (far_two,)), third, rights, sums
    )
    both = lax.all_to_all(both, AXES, 0, 0, tiled=True, axis_index_groups=CORES)

    ends = []
    for kept, given, terms in ((keep, got[0], sums), (late_keep, send(late_give, core=1), added_by_core(swap, both))):
        here, there = summed(side, kept, given, [send(terms[d - 1], **NEAR[d]) for d in range(1, 4)])
        ends += [here, send(there, dhi=1)]

    total = join((((z & 1) ^ swap[0]).reshape(1), (y ^ (2 * side[0])).reshape(1)), ends)
    return total.reshape(8 * rows, columns)


def solution(mesh):
    return jax.shard_map(
        per_device,
        mesh=mesh,
        in_specs=(P("grid", "rep"), P("rep", "grid")),
        out_specs=P("rep", "grid"),
        check_vma=False,
    )
```

```python
import jax
import jax.numpy as jnp
from jax import lax
from jax.experimental import pallas as pl
from jax.experimental.pallas import tpu as pltpu
from jax.sharding import PartitionSpec as P

AXES = ("rep", "grid")
PARAMS = pltpu.CompilerParams(vmem_limit_bytes=20 * 1024 * 1024)
SHORT = pl.CostEstimate(flops=1, bytes_accessed=1, transcendentals=0)
NEAR = (dict(), dict(dx=1), dict(dy=1), dict(dy=3))
DIFFERS = (0, 3, 1, 2)


def number(x_hi, core, x_lo, z, y):
    return (2 * x_hi + core) * 32 + 16 * x_lo + 4 * z + y


def send(value, dhi=0, core=0, dx=0, dz=0, dy=0):
    pairs = [
        (number(h, c, x, z, y), number(h ^ dhi, c ^ core, x ^ dx, z ^ dz, y ^ dy))
        for h in range(2) for c in range(2) for x in range(2) for z in range(4) for y in range(4)
    ]
    return lax.ppermute(value, AXES, pairs)


CORES = [
    [number(h, c, x, z, y) for c in range(2)]
    for h in range(2) for x in range(2) for z in range(4) for y in range(4)
]


def halves(value):
    high = value.astype(jnp.bfloat16)
    return high, (value - high.astype(jnp.float32)).astype(jnp.bfloat16)


def whole(value):
    return pl.BlockSpec(value.shape, lambda *_: (0,) * value.ndim, pipeline_mode=pl.Buffered(1))


ANYWHERE = pl.BlockSpec(memory_space=pl.ANY)
VMEM = pl.BlockSpec(memory_space=pltpu.VMEM)


def call(kernel, scalars, values, in_specs, out_shape, out_specs, scratch=(), aliases=None):
    scalars = scalars if isinstance(scalars, tuple) else (scalars,)
    aliases = {at + len(scalars) - 1: out for at, out in (aliases or {}).items()}
    return pl.pallas_call(
        kernel,
        grid_spec=pltpu.PrefetchScalarGridSpec(
            num_scalar_prefetch=len(scalars), grid=(1,), in_specs=in_specs, out_specs=out_specs, scratch_shapes=scratch
        ),
        out_shape=out_shape,
        input_output_aliases=aliases,
        compiler_params=PARAMS,
        cost_estimate=SHORT,
    )(*scalars, *values)


def cut_kernel(quarter, value, _, *rest):
    outs, sems = rest[:-1], rest[-1]
    depth = outs[0].shape[0]
    copies = []
    for d, out in enumerate(outs):
        at = pl.ds(pl.multiple_of((quarter[0] ^ DIFFERS[d]) * depth, depth), depth)
        copies.append(pltpu.make_async_copy(value.at[at], out, sems.at[d]))
    for copy in copies:
        copy.start()
    for copy in copies:
        copy.wait()


def cut_after(quarter, value, earlier):
    shape = jax.ShapeDtypeStruct((value.shape[0] // 4, value.shape[1]), value.dtype)
    return call(
        cut_kernel, quarter, (value, earlier), [ANYWHERE] * 2, [shape] * 4, [ANYWHERE] * 4,
        [pltpu.SemaphoreType.DMA((4,))],
    )


def split_kernel(_, *refs):
    *pieces, high, low = refs
    columns = pieces[0].shape[1]
    for d, piece in enumerate(pieces):
        at = slice(d * columns, (d + 1) * columns)
        high[:, at], low[:, at] = halves(piece[...])


def split(scalars, pieces):
    depth, columns = pieces[0].shape
    shape = pltpu.VMEM((depth, len(pieces) * columns), jnp.bfloat16)
    found = call(split_kernel, scalars, pieces, [whole(piece) for piece in pieces], [shape] * 2, [VMEM] * 2)
    return [pltpu.with_memory_space_constraint(value, pltpu.VMEM) for value in found]


def multiplied(blocks, left_high, left_low, rights, store):
    depth = left_high.shape[1]
    at = 0
    for block in blocks:
        value = block[...].reshape(block.shape[0] * block.shape[1], depth)
        span = slice(at, at + value.shape[0])
        left_high[span], left_low[span] = halves(value)
        at += value.shape[0]
    columns = rights[0].shape[1]
    for d in range(4):
        high, low = rights[2 * d][...], rights[2 * d + 1][...]
        total = jnp.dot(left_high[...], high, preferred_element_type=jnp.float32)
        total += jnp.dot(left_high[...], low, preferred_element_type=jnp.float32)
        total += jnp.dot(left_low[...], high, preferred_element_type=jnp.float32)
        store(d, total.reshape(-1, 4, blocks[0].shape[1], columns))


def places(d):
    return [(block, block ^ (0, 2, 1, 3)[d]) for block in range(4)]


def early_products(swap, part, planes, rights, before=()):
    arrays = [array for plane in planes for array in plane]
    rows, depth = arrays[0].shape[1:]
    columns = rights[0].shape[1]

    def kernel(swap, *refs):
        blocks, rest = refs[: len(arrays)], refs[len(arrays) + len(before):]
        *rights, keep, one_give, two_give, three_give, four_give, left_high, left_low = rest
        gives = one_give, two_give, three_give, four_give
        swapped = swap[0] == 1

        def store(d, total):
            for block, into in places(d):
                zero, one = total[0, block], total[1, block]
                keep[d, 0, into] = jnp.where(swapped, one, zero)
                gives[d][0, into] = jnp.where(swapped, zero, one)

        multiplied(blocks, left_high, left_low, rights, store)

    kept = jax.ShapeDtypeStruct((4, 2, 4, rows, columns), jnp.float32)
    given = jax.ShapeDtypeStruct((2, 4, rows, columns), jnp.float32)
    once = pl.Buffered(1)
    kept_out = pl.BlockSpec((4, 1, 4, rows, columns), lambda *_: (0, part, 0, 0, 0), pipeline_mode=once)
    given_out = pl.BlockSpec((1, 4, rows, columns), lambda *_: (part, 0, 0, 0), pipeline_mode=once)
    scratch = pltpu.VMEM((8 * rows, depth), jnp.bfloat16)
    first = 1 + len(arrays)
    return call(
        kernel, swap, (*arrays, *before, *rights),
        [whole(array) for array in arrays] + [ANYWHERE] * len(before) + [VMEM] * 8,
        [kept] + [given] * 4, [kept_out] + [given_out] * 4, [scratch] * 2,
        {first + at: at for at in range(len(before))},
    )


def added_kernel(_, keep, *refs):
    gots, outs = refs[:len(refs) // 2], refs[len(refs) // 2:]
    for at, (got, out) in enumerate(zip(gots, outs)):
        out[...] = keep[at + 1] + got[...]


def added(scalars, keep, gots):
    shape = jax.ShapeDtypeStruct(gots[0].shape, jnp.float32)
    return call(
        added_kernel, scalars, (keep, *gots), [whole(value) for value in (keep, *gots)], [shape] * 3, [whole(shape)] * 3
    )


def ahead_products(scalars, arrays, rights):
    rows, depth = arrays[0].shape[1:]

    def kernel(_, *refs):
        blocks, (*rights, out, left_high, left_low) = refs[: len(arrays)], refs[len(arrays):]

        def store(d, total):
            for part in range(2):
                for block, into in places(d):
                    out[d, part, into] = total[part, block]

        multiplied(blocks, left_high, left_low, rights, store)

    shape = jax.ShapeDtypeStruct((4, 2, 4, rows, rights[0].shape[1]), jnp.float32)
    scratch = pltpu.VMEM((8 * rows, depth), jnp.bfloat16)
    return call(
        kernel, scalars, (*arrays, *rights), [whole(array) for array in arrays] + [VMEM] * 8,
        shape, whole(shape), [scratch] * 2,
    )


def late_products(flags, parts, third, rights, after):
    arrays = [array for part in parts for array in part]
    rows, depth = arrays[0].shape[1:]
    columns = rights[0].shape[1]

    def kernel(swap, at_core, *refs):
        blocks, rest = refs[: len(arrays)], refs[len(arrays) + len(after):]
        *rights, ahead, keep, give, both, left_high, left_low = rest
        swapped, core = swap[0] == 1, at_core[0]

        def store(d, total):
            for part in range(2):
                for block, into in places(d):
                    zero, one = ahead[d, part, into], total[part, block]
                    kept, given = jnp.where(swapped, one, zero), jnp.where(swapped, zero, one)
                    if d == 0:
                        keep[0, part, into], give[part, into] = kept, given
                    else:
                        both[core, d - 1, part, into], both[1 - core, d - 1, part, into] = kept, given

        multiplied(blocks, left_high, left_low, rights, store)

    piece = (2, 4, rows, columns)
    shapes = [jax.ShapeDtypeStruct(shape, jnp.float32) for shape in ((1, *piece), piece, (2, 3, *piece))]
    scratch = pltpu.VMEM((8 * rows, depth), jnp.bfloat16)
    return call(
        kernel, flags, (*arrays, *after, *rights, third),
        [whole(array) for array in arrays] + [ANYWHERE] * len(after) + [VMEM] * 8 + [whole(third)],
        shapes, [whole(shape) for shape in shapes], [scratch] * 2,
    )


def added_by_core_kernel(_, both, *outs):
    for d, out in enumerate(outs):
        out[...] = both[0, d] + both[1, d]


def added_by_core(scalars, both):
    shape = jax.ShapeDtypeStruct(both.shape[2:], jnp.float32)
    return call(added_by_core_kernel, scalars, (both,), [whole(both)], [shape] * 3, [whole(shape)] * 3)


def sum_kernel(side, keep, got, *refs):
    terms, (mine, theirs) = refs[:-2], refs[-2:]
    for out, part in ((mine, side[0]), (theirs, 1 - side[0])):
        across = terms[0][1 - part]
        out[...] = (keep[0, part] + got[part]) + (across + (terms[1][part] + terms[2][part]))


def summed(side, keep, got, terms):
    shape = jax.ShapeDtypeStruct(got.shape[1:], jnp.float32)
    own = pl.BlockSpec((1, *keep.shape[1:]), lambda *_: (0,) * keep.ndim, pipeline_mode=pl.Buffered(1))
    return call(
        sum_kernel, side, (keep, got, *terms), [own] + [whole(value) for value in (got, *terms)],
        [shape] * 2, [whole(shape)] * 2,
    )


def join_kernel(plane, first, one, other_one, two, other_two, out):
    for block in range(4):
        line = first[0] ^ block
        out[plane[0], line] = one[block] + other_one[block]
        out[1 - plane[0], line] = two[block] + other_two[block]


def join(place, values):
    shape = jax.ShapeDtypeStruct((2, *values[0].shape), jnp.float32)
    return call(join_kernel, place, values, [whole(value) for value in values], shape, whole(shape))


def per_device(left, right):
    rows, depth = left.shape[0], left.shape[1] // 4
    columns = right.shape[1]
    rep, grid = lax.axis_index("rep"), lax.axis_index("grid")
    core, x_hi = rep & 1, rep >> 1
    x_lo, z, y = grid >> 4, (grid >> 2) & 3, grid & 3
    quarter = 2 * (x_lo ^ (y >> 1)) + (x_lo ^ (y >> 1) ^ (y & 1))
    swap = (core ^ (z >> 1)).reshape(1)
    side = (x_hi ^ x_lo).reshape(1)

    def block(d):
        return lax.dynamic_slice(left, (0, (quarter ^ d) * depth), (rows, depth))

    mine = jnp.stack([block(0), send(block(1), dy=1), send(block(3), dy=2), send(block(2), dy=3)])
    other = send(mine, dx=1, dy=2)
    own_one, own_three = send(mine, dz=1), send(mine, dz=3)
    far, *_ = lax.optimization_barrier((other, own_one, own_three))
    far_one, far_three = lax.optimization_barrier((send(far, dz=1), send(far, dz=3)))

    own_two, far_two = send(own_three, dz=1), send(far_one, dz=3)

    pieces = cut_after(quarter.reshape(1), right, other)
    pieces = [pieces[0]] + [send(pieces[d], **NEAR[d]) for d in range(1, 4)]
    rights = [half for piece in pieces for half in split(swap, [piece])]

    before = early_products(swap, 0, ((mine,), (own_three,)), rights)
    early = early_products(swap, 1, ((far,), (far_three,)), rights, before)

    keep, *gives = early
    third = ahead_products(swap, (own_one, far_one), rights)
    got = [send(give, core=1) for give in gives]
    sums = added(swap, keep, got[1:])
    late_keep, late_give, both = late_products(
        (swap, core.reshape(1)), ((own_two,), (far_two,)), third, rights, sums
    )
    both = lax.all_to_all(both, AXES, 0, 0, tiled=True, axis_index_groups=CORES)

    ends = []
    for kept, given, terms in ((keep, got[0], sums), (late_keep, send(late_give, core=1), added_by_core(swap, both))):
        here, there = summed(side, kept, given, [send(terms[d - 1], **NEAR[d]) for d in range(1, 4)])
        ends += [here, send(there, dhi=1)]

    total = join((((z & 1) ^ swap[0]).reshape(1), (y ^ (2 * side[0])).reshape(1)), ends)
    return total.reshape(8 * rows, columns)


def solution(mesh):
    return jax.shard_map(
        per_device,
        mesh=mesh,
        in_specs=(P("grid", "rep"), P("rep", "grid")),
        out_specs=P("rep", "grid"),
        check_vma=False,
    )
```
